128 devices in a mesh: wide: 16 (over x_hi, z, core), narrow: 8 (over y, x_lo).
Axes of the slice: x: 4 (x_hi: 2, x_lo: 2; x = x_hi * 2 + x_lo), y: 4, z: 4, core: 2. Of those that a mesh axis runs over, the one named last changes fastest.
Arguments:
- velocity: float32 [3, 128, 128, 512], P(None, 'wide', 'narrow'), may hold values from -4 to 4
- bfield: float32 [128, 128, 512], P('wide', 'narrow'), may hold values from 1 to 3
Outputs:
- force: float32 [3, 128, 128, 512], P(None, 'wide', 'narrow')
- pressure: float32 [128, 128, 512], P('wide', 'narrow')
The draws below stay inside these ranges and needn't reach their ends.
All inputs are finite; a program needn't handle non-finite values.
Results may differ from the reference program's by a relative error of at most 0.00023.
Values sent between devices are 32-bit elements; how exact they have to be, the bound alone decides.
No kernel may reach another device: no remote copies, remote signals or barrier semaphores. Data moves between devices by JAX's collectives and lax.ppermute only.
A program may use at most 128 MiB of HBM per device.

```python
import math
import jax
import jax.numpy as jnp
import numpy as np
from jax import lax

NZ = 128
NX = 128
NY = 512


def levels(own_key, extent, split, least, largest):
    gain, own = 1.0, jax.random.fold_in(own_key, 6)
    for dim, parts in split:
        heights = jnp.exp(jax.random.uniform(jax.random.fold_in(own, dim), (parts,), jnp.float32, least / len(split), largest / len(split)))
        gain = gain * jnp.repeat(heights, extent[dim] // parts).reshape([-1 if axis == dim else 1 for axis in range(len(extent))])
    return gain


def scatter_about(rng, extent, deviation, bound, split=(), held_as=jnp.bfloat16):
    drawn = jax.random.normal(rng, extent, jnp.float32) * deviation
    if len(split) > 0:
        drawn = levels(rng, extent, split, -0.22, 0.18) * drawn
    return jnp.clip(drawn, min=-bound, max=bound).astype(held_as)


def setup_inputs(seed: int = 0) -> dict:
    splits = jax.random.split(jax.random.key(seed), 3)
    velocity = scatter_about(splits[0], (3, NZ, NX, NY), 1.0, 4.0, ((1, 16), (2, 8)), jnp.float32)
    bfield = jnp.clip(1.0 + 2.0 * jax.random.uniform(splits[1], (NZ, NX, NY), jnp.float32) ** levels(splits[1], (NZ, NX, NY), ((0, 16), (1, 8)), -0.2, 0.2), 1.0, 3.0)
    return dict(velocity=velocity, bfield=bfield)


HIGHEST = lax.Precision.HIGHEST

def legendre_pair(degree, points):
    below = np.ones(points.shape)
    current = points * 1.0
    for step_index in range(2, degree + 1):
        below, current = (current, ((2 * step_index - 1) * points * current - (step_index - 1) * below) / step_index)
    return (current, below)

def jacobi_eigen(matrix):
    order = matrix.shape[0]
    current = matrix * 1.0
    vectors = np.eye(order)
    for sweep in range(12):
        for row in range(order - 1):
            for column in range(row + 1, order):
                angle = 0.5 * math.atan2(2.0 * float(current[row, column]), float(current[row, row]) - float(current[column, column]))
                cosine = math.cos(angle)
                sine = math.sin(angle)
                rotation = np.eye(order)
                rotation[row, row] = cosine
                rotation[column, column] = cosine
                rotation[row, column] = -sine
                rotation[column, row] = sine
                current = rotation.T @ current @ rotation
                vectors = vectors @ rotation
    positions = np.arange(order)
    return (current[positions, positions] * 1.0, vectors)

def node_tables():
    poly_order = 7
    node_total = 8
    points = np.cos(np.pi * np.arange(node_total) / poly_order)
    for attempt in range(60):
        value_top, value_below = legendre_pair(poly_order, points)
        points = points - (points * value_top - value_below) / (node_total * value_top)
    points = np.sort(points)
    value_top, value_below = legendre_pair(poly_order, points)
    gll_weights = 2.0 / (poly_order * node_total * value_top ** 2)
    spacing = points[:, None] - points[None, :] + np.eye(node_total)
    derivative = value_top[:, None] / (value_top[None, :] * spacing) * (1.0 - np.eye(node_total))
    derivative[0, 0] = -poly_order * node_total / 4.0
    derivative[-1, -1] = poly_order * node_total / 4.0
    gauss = np.cos(np.pi * (np.arange(12) + 0.75) / 12.5)
    for attempt in range(60):
        value_top, value_below = legendre_pair(12, gauss)
        slope_now = 12 * (gauss * value_top - value_below) / (gauss ** 2 - 1.0)
        gauss = gauss - value_top / slope_now
    value_top, value_below = legendre_pair(12, gauss)
    slope_now = 12 * (gauss * value_top - value_below) / (gauss ** 2 - 1.0)
    gauss_weights = 2.0 / ((1.0 - gauss ** 2) * slope_now ** 2)
    interp = np.ones((12, 8))
    for column in range(8):
        for other_node in range(8):
            if other_node != column:
                interp[:, column] = interp[:, column] * (gauss - points[other_node]) / (points[column] - points[other_node])
    slopes = interp @ derivative
    stiffness = derivative.T @ (gll_weights[:, None] * derivative)
    wide_stiff = np.zeros((22, 22))
    wide_mass = np.zeros(22)
    for element in range(3):
        first_row = 7 * element
        wide_stiff[first_row:first_row + 8, first_row:first_row + 8] += stiffness
        wide_mass[first_row:first_row + 8] += gll_weights
    box_stiff = wide_stiff[6:16, 6:16]
    scaling = 1.0 / np.sqrt(wide_mass[6:16])
    eigvals, eigvecs = jacobi_eigen(scaling[:, None] * box_stiff * scaling[None, :])
    eigvecs = scaling[:, None] * eigvecs
    inverse_sum = 1.0 / (eigvals[:, None, None] + eigvals[None, :, None] + eigvals[None, None, :])
    qweights = gauss_weights[:, None, None] * gauss_weights[None, :, None] * gauss_weights[None, None, :]
    node_cube = gll_weights[:, None, None] * gll_weights[None, :, None] * gll_weights[None, None, :]
    tables = (interp, slopes, derivative, stiffness, gll_weights, eigvecs, inverse_sum, qweights, node_cube)
    return tuple((jnp.asarray(table, dtype=jnp.float32) for table in tables))

def along_first(matrix, values):
    return jnp.einsum('qa,...abcn->...qbcn', matrix, values, precision=HIGHEST)

def along_second(matrix, values):
    return jnp.einsum('qb,...abcn->...aqcn', matrix, values, precision=HIGHEST)

def along_third(matrix, values):
    return jnp.einsum('qc,...abcn->...abqn', matrix, values, precision=HIGHEST)

def to_elems(field):
    components, z_nodes, x_nodes, y_nodes = field.shape
    blocks = field.reshape(components, z_nodes // 8, 8, x_nodes // 8, 8, y_nodes // 8, 8)
    blocks = blocks.transpose(1, 0, 2, 4, 6, 3, 5)
    return blocks.reshape(z_nodes // 8, components, 8, 8, 8, x_nodes // 8 * (y_nodes // 8))

def from_elems(cells, x_count, y_count):
    z_count, components = (cells.shape[0], cells.shape[1])
    blocks = cells.reshape(z_count, components, 8, 8, 8, x_count, y_count)
    blocks = blocks.transpose(1, 0, 2, 5, 3, 6, 4)
    return blocks.reshape(components, z_count * 8, x_count * 8, y_count * 8)

def element_force(velo_cells, field_cells, interp, slopes, qweights):
    first_value = along_first(interp, velo_cells)
    first_slope = along_first(slopes, velo_cells)
    mid_value = along_second(interp, first_value)
    mid_thick = along_second(slopes, first_value)
    mid_cast = along_second(interp, first_slope)
    values = along_third(interp, mid_value)
    grad_width = along_third(slopes, mid_value)
    grad_thick = along_third(interp, mid_thick)
    grad_cast = along_third(interp, mid_cast)
    convect = values[0] * grad_cast + values[1] * grad_thick + values[2] * grad_width
    field_quad = along_third(interp, along_second(interp, along_first(interp, field_cells)))
    braking = jnp.asarray([1.0, 0.0, 1.0], dtype=jnp.float32)[:, None, None, None, None]
    quad_force = (-convect - field_quad * field_quad * values * braking) * qweights[..., None]
    transposed = interp.T
    return along_first(transposed, along_second(transposed, along_third(transposed, quad_force)))

def local_force(velocity, bfield, interp, slopes, qweights):
    x_nodes, y_nodes = (bfield.shape[1], bfield.shape[2])
    velo_cells = to_elems(velocity)
    field_cells = to_elems(bfield[None])

    def per_slab(operands):
        return element_force(operands[0], operands[1][0], interp, slopes, qweights)
    slabs = lax.map(per_slab, (velo_cells, field_cells))
    return from_elems(slabs, x_nodes // 8, y_nodes // 8)

def weak_divergence(force, derivative, node_cube):
    cells = to_elems(force)
    spread = along_first(derivative, cells[:, 0]) + along_second(derivative, cells[:, 1]) + along_third(derivative, cells[:, 2])
    return from_elems((spread * node_cube[..., None])[:, None], force.shape[2] // 8, force.shape[3] // 8)

def apply_stiffness(field, stiffness, gll_weights):
    cells = to_elems(field)[:, 0]
    weight_cast = gll_weights[:, None, None, None]
    weight_thick = gll_weights[None, :, None, None]
    weight_width = gll_weights[None, None, :, None]
    total = along_first(stiffness, cells) * weight_thick * weight_width
    total = total + along_second(stiffness, cells) * weight_cast * weight_width
    total = total + along_third(stiffness, cells) * weight_cast * weight_thick
    return from_elems(total[:, None], field.shape[2] // 8, field.shape[3] // 8)

def inverse_multiplicity(z_nodes, x_nodes, y_nodes, z_offset, x_offset, z_total, x_total):

    def per_axis(length, offset, grid_total):
        position = jnp.arange(length, dtype=jnp.int32)
        global_pos = position + offset
        on_edge = (position % 8 == 0) | (position % 8 == 7)
        on_border = (global_pos == 0) | (global_pos == grid_total - 1)
        return jnp.where(on_edge & jnp.logical_not(on_border), 0.5, 1.0).astype(jnp.float32)
    return per_axis(z_nodes, z_offset, z_total)[:, None, None] * per_axis(x_nodes, x_offset, x_total)[None, :, None] * per_axis(y_nodes, 0, y_nodes)[None, None, :]

def fold_pairs(values, dimension, below_rim, above_rim):
    dims_now = values.shape
    number = dims_now[dimension] // 8
    split_up = values.reshape(dims_now[:dimension] + (number, 8) + dims_now[dimension + 1:])
    leading = (slice(None),) * dimension
    node_last = split_up[leading + (slice(None), 7)]
    node_first = split_up[leading + (slice(None), 0)]
    shared = lax.slice_in_dim(node_last, 0, number - 1, axis=dimension) + lax.slice_in_dim(node_first, 1, number, axis=dimension)
    end_last = lax.slice_in_dim(node_last, number - 1, number, axis=dimension)
    end_first = lax.slice_in_dim(node_first, 0, 1, axis=dimension)
    if above_rim is not None:
        end_last = end_last + above_rim
    if below_rim is not None:
        end_first = end_first + below_rim
    new_last = jnp.concatenate([shared, end_last], axis=dimension)
    new_first = jnp.concatenate([end_first, shared], axis=dimension)
    split_up = split_up.at[leading + (slice(None), 7)].set(new_last)
    split_up = split_up.at[leading + (slice(None), 0)].set(new_first)
    return split_up.reshape(dims_now)

def assemble(values):
    return fold_pairs(fold_pairs(fold_pairs(values, 1, None, None), 2, None, None), 3, None, None)

def box_axis(widened, dimension, number):
    left_side = lax.slice_in_dim(widened, 0, 8 * number, 8, dimension)
    right_side = lax.slice_in_dim(widened, 11, 8 * number + 4, 8, dimension)
    middle = lax.slice_in_dim(widened, 2, 8 * number + 2, 1, dimension)
    dims_now = widened.shape
    split_shape = dims_now[:dimension] + (number, 8) + dims_now[dimension + 1:]
    edge_shape = dims_now[:dimension] + (number, 1) + dims_now[dimension + 1:]
    return jnp.concatenate([left_side.reshape(edge_shape), middle.reshape(split_shape), right_side.reshape(edge_shape)], axis=dimension + 1)

def solve_boxes(widened, eigvecs, inverse_sum, weight):
    z_count = (widened.shape[1] - 4) // 8
    x_count = (widened.shape[2] - 4) // 8
    y_count = (widened.shape[3] - 4) // 8
    boxes = box_axis(box_axis(box_axis(widened[0], 2, y_count), 1, x_count), 0, z_count)
    boxes = boxes.transpose(0, 1, 3, 5, 2, 4).reshape(z_count, 10, 10, 10, x_count * y_count)
    transposed = eigvecs.T
    spectral = along_third(transposed, along_second(transposed, along_first(transposed, boxes))) * inverse_sum[..., None]
    solved = along_third(eigvecs, along_second(eigvecs, along_first(eigvecs, spectral)))
    interior = solved[:, 1:9, 1:9, 1:9]
    return from_elems(interior[:, None], x_count, y_count) * weight

def pad_all(values):
    return jnp.pad(values, ((0, 0), (2, 2), (2, 2), (2, 2)))

def reference(velocity, bfield):
    interp, slopes, derivative, stiffness, gll_weights, eigvecs, inverse_sum, qweights, node_cube = node_tables()
    z_nodes, x_nodes, y_nodes = bfield.shape
    force = assemble(local_force(velocity, bfield, interp, slopes, qweights))
    weight = inverse_multiplicity(z_nodes, x_nodes, y_nodes, 0, 0, z_nodes, x_nodes)
    source = assemble(weak_divergence(force, derivative, node_cube))
    first_pass = assemble(solve_boxes(pad_all(source), eigvecs, inverse_sum, weight))
    residue = source - assemble(apply_stiffness(first_pass, stiffness, gll_weights))
    pressure = first_pass + assemble(solve_boxes(pad_all(residue), eigvecs, inverse_sum, weight))
    return (force, pressure[0])
```

```python
import ml_dtypes
import jax
import jax.numpy as jnp
import numpy as np
from jax import lax
from jax.experimental import pallas as pl
from jax.experimental.pallas import tpu as pltpu
from jax.sharding import PartitionSpec as P

F32 = jnp.float32
BF16 = jnp.bfloat16
MIB = 2**20


def legendre_pair(degree, points):
    below, current = np.ones(points.shape), points * 1.0
    for step in range(2, degree + 1):
        below, current = current, ((2 * step - 1) * points * current - (step - 1) * below) / step
    return current, below


def tables_1d():
    points = np.cos(np.pi * np.arange(8) / 7)
    for _ in range(60):
        top, below = legendre_pair(7, points)
        points = points - (points * top - below) / (8 * top)
    points = np.sort(points)
    top, below = legendre_pair(7, points)
    w = 2.0 / (56 * top**2)
    spacing = points[:, None] - points[None, :] + np.eye(8)
    deriv = top[:, None] / (top[None, :] * spacing) * (1.0 - np.eye(8))
    deriv[0, 0], deriv[-1, -1] = -14.0, 14.0
    gauss = np.cos(np.pi * (np.arange(12) + 0.75) / 12.5)
    for _ in range(60):
        top, below = legendre_pair(12, gauss)
        gauss = gauss - top / (12 * (gauss * top - below) / (gauss**2 - 1.0))
    top, below = legendre_pair(12, gauss)
    slope = 12 * (gauss * top - below) / (gauss**2 - 1.0)
    v = 2.0 / ((1.0 - gauss**2) * slope**2)
    interp = np.ones((12, 8))
    for col in range(8):
        for other in range(8):
            if other != col:
                interp[:, col] *= (gauss - points[other]) / (points[col] - points[other])
    stiff = deriv.T @ (w[:, None] * deriv)
    wide_stiff, wide_mass = np.zeros((22, 22)), np.zeros(22)
    for el in range(3):
        r = 7 * el
        wide_stiff[r : r + 8, r : r + 8] += stiff
        wide_mass[r : r + 8] += w
    scale = 1.0 / np.sqrt(wide_mass[6:16])
    lam, vec = np.linalg.eigh(scale[:, None] * wide_stiff[6:16, 6:16] * scale[None, :])
    return interp, interp @ deriv, deriv, stiff, w, scale[:, None] * vec, lam, v


def hi_lo(m):
    hi = m.astype(ml_dtypes.bfloat16)
    return hi, (m - hi.astype(np.float64)).astype(ml_dtypes.bfloat16)


def left_const(m):
    hi, lo = hi_lo(m)
    return np.concatenate([hi, hi, lo], axis=1)


def right_const(m):
    hi, lo = hi_lo(m)
    return np.concatenate([hi, hi, lo], axis=0)


def block_diag(m, count):
    return np.kron(np.eye(count), m)


def own(z, x):
    return 16 * z + x


def local_rows(terms, xs):
    out = np.zeros((8 * len(xs), 128))
    for k, x in enumerate(xs):
        el, j = divmod(x, 8)
        for z in range(8):
            for zm, xm in terms:
                for z2 in range(8):
                    for j2 in range(8):
                        out[8 * k + z, own(z2, 8 * el + j2)] += zm[z, z2] * xm[j, j2]
    return out


def extended_rows(terms):
    local = local_rows(terms, range(16)).reshape(16, 8, 128)
    out = np.zeros((144, 144))
    for x in range(16):
        for z in range(8):
            out[own(z, x), :128] = local[x, z]
            if x in (7, 8):
                out[own(z, x), :128] += local[15 - x, z]
    for z in range(8):
        for zm, xm in terms:
            for z2 in range(8):
                out[own(z, 0), 128 + z2] += zm[z, z2] * xm[7, 7]
                out[128 + z, 128 + z2] += zm[z, z2] * xm[6, 7]
                out[own(z, 15), 136 + z2] += zm[z, z2] * xm[0, 0]
                out[136 + z, 136 + z2] += zm[z, z2] * xm[1, 0]
    return out


def box_rows(vec):
    nodes = np.zeros((10, 2, 10, 240))

    def put(zk, el, xk, z, place):
        if xk == 0 and el == 0:
            x = "l"
        elif xk == 9 and el == 1:
            x = "r"
        else:
            x = 8 * el + (-2 if xk == 0 else 9 if xk == 9 else xk - 1)
        side = {"l": 0, "r": 8}.get(x)
        if place == "own":
            row = own(z, x) if side is None else 128 + side + z
        elif place == "below":
            row = 144 + ((z - 6) * 16 + x if side is None else 32 + side + z)
        else:
            row = 192 + (z * 16 + x if side is None else 32 + side + z)
        nodes[zk, el, xk, row] += 1.0

    for el in range(2):
        for xk in range(10):
            put(0, el, xk, 6, "below")
            put(1, el, xk, 7, "below")
            put(8, el, xk, 0, "above")
            put(9, el, xk, 1, "above")
            for z in range(8):
                put(z + 1, el, xk, z, "own")
    into = np.einsum("zi,xj,zexr->iejr", vec, vec, nodes).reshape(200, 240)
    back = np.zeros((8, 16, 10, 2, 10))
    inner = vec[1:9]
    for z in range(8):
        for x in range(16):
            el, j = divmod(x, 8)
            block = inner[z][:, None] * inner[j][None, :]
            if x in (7, 8):
                back[z, x, :, el] += 0.5 * block
                back[z, x, :, 1 - el] += 0.5 * inner[z][:, None] * inner[7 - j][None, :]
            else:
                back[z, x, :, el] += block
    back = back.reshape(128, 200)
    return np.pad(into, ((0, 8), (0, 0))), np.pad(back, ((0, 0), (0, 8)))


def box_lanes(vec, count):
    into = np.zeros((8 * count, 10 * count))
    back = np.zeros((10 * count, 8 * count))
    for e in range(count):
        spots = [8 * e - 2] + list(range(8 * e, 8 * e + 8)) + [8 * e + 9]
        for k, y in enumerate(spots):
            if 0 <= y < 8 * count:
                into[y, 10 * e : 10 * e + 10] += vec[k]
        for j in range(8):
            col = vec[j + 1]
            y = 8 * e + j
            if j == 0 and e > 0:
                back[10 * e : 10 * e + 10, [y - 1, y]] += 0.5 * col[:, None]
            elif j == 7 and e < count - 1:
                back[10 * e : 10 * e + 10, [y, y + 1]] += 0.5 * col[:, None]
            else:
                back[10 * e : 10 * e + 10, y] += col
    return into, back


def constants():
    interp, slopes, deriv, stiff, w, vec, lam, v = tables_1d()
    eye2 = np.eye(2)
    zx = lambda a, b: np.kron(a, np.kron(eye2, b))
    c = {}
    c["y_in"] = right_const(
        np.concatenate([block_diag(interp.T, 32), block_diag(slopes.T, 32)], axis=1)
    )
    c["zx_in"] = left_const(
        np.concatenate([zx(interp, interp), zx(slopes, interp), zx(interp, slopes)], axis=0)
    )
    test = v[:, None] * interp
    back = zx(test.T, test.T).reshape(8, 16, 288)
    pair = back[:, 7] + back[:, 8]
    back[:, 7], back[:, 8] = pair, pair
    c["zx_out"] = left_const(back.reshape(128, 288))
    c["y_out"] = right_const(block_diag(test, 32))
    wm, wd = np.diag(w), w[:, None] * deriv
    parts = ([(wd, wm)], [(wm, wd)], [(wm, wm)])
    sides = (14, 15, 1, 0)
    c["div_msg01"] = left_const(np.concatenate([local_rows(t, sides) for t in parts[:2]], 1))
    c["div_msg2"] = left_const(local_rows(parts[2], sides))
    c["div01"] = left_const(np.concatenate([extended_rows(t) for t in parts[:2]], 1))
    c["div2"] = left_const(extended_rows(parts[2]))
    kterms = [(stiff, wm), (wm, stiff)]
    c["st_msg"] = left_const(
        np.concatenate([local_rows(kterms, sides), local_rows(parts[2], sides)], 0)
    )
    c["st"] = left_const(np.concatenate([extended_rows(kterms), extended_rows(parts[2])], 0))
    c["wd_y"] = right_const(block_diag(wd.T, 32))
    c["k_y"] = right_const(block_diag(stiff.T, 32))
    c["w_y"] = np.tile(w, 64)[None].astype(np.float32)
    into, back = box_rows(vec)
    c["box_in"], c["box_out"] = left_const(into), left_const(back)
    into, back = box_lanes(vec, 64)
    c["ybox_in"], c["ybox_out"] = right_const(into), right_const(back)
    inv = 1.0 / (lam[:, None, None, None] + lam[None, None, :, None] + lam)
    inv = np.broadcast_to(inv[:, :, :, None, :], (10, 1, 10, 64, 10))
    inv = np.broadcast_to(inv, (10, 2, 10, 64, 10)).reshape(200, 640)
    c["inv"] = np.pad(inv, ((0, 8), (0, 0))).astype(np.float32)
    return c


def split(x):
    hi = x.astype(BF16)
    return hi, (x - hi.astype(F32)).astype(BF16)


def rmul(x, const):
    hi, lo = split(x)
    return jnp.dot(jnp.concatenate([hi, lo, hi], axis=1), const, preferred_element_type=F32)


def lmul(const, x):
    hi, lo = split(x)
    return jnp.dot(const, jnp.concatenate([hi, lo, hi], axis=0), preferred_element_type=F32)


def rmul_halves(x, const):
    return jnp.concatenate([rmul(x[:, :256], const), rmul(x[:, 256:], const)], axis=1)


def dss_lanes(x):
    lane = lax.broadcasted_iota(jnp.int32, x.shape, 1)
    n = x.shape[1]
    up = jnp.where((lane % 8 == 7) & (lane < n - 1), pltpu.roll(x, n - 1, 1), 0.0)
    down = jnp.where((lane % 8 == 0) & (lane > 0), pltpu.roll(x, 1, 1), 0.0)
    return x + up + down


def flags():
    z, x = lax.axis_index("wide"), lax.axis_index("narrow")
    nz, nx = lax.axis_size("wide"), lax.axis_size("narrow")
    as_flag = lambda t: t.astype(F32)
    return as_flag(z > 0), as_flag(z < nz - 1), as_flag(x > 0), as_flag(x < nx - 1)


def force_kernel(v_ref, b_ref, y_in, zx_in, zx_out, y_out, f_ref, up_ref, down_ref):
    v = v_ref[...].reshape(384, 512)
    b = b_ref[...].reshape(128, 512)
    halves = []
    for h in range(2):
        cut = slice(256 * h, 256 * h + 256)
        first = rmul(v[:, cut], y_in[...])
        bq = lmul(zx_in[:288, :], rmul(b[:, cut], y_in[:, :384]))
        u, gz, gx, gy = [], [], [], []
        for c in range(3):
            rows = slice(128 * c, 128 * c + 128)
            most = lmul(zx_in[...], first[rows, :384])
            u.append(most[:288])
            gz.append(most[288:576])
            gx.append(most[576:])
            gy.append(lmul(zx_in[:288, :], first[rows, 384:]))
        b2 = bq * bq
        back = []
        for c in range(3):
            conv = u[0] * gz[c] + u[1] * gx[c] + u[2] * gy[c]
            if c != 1:
                conv = conv + b2 * u[c]
            back.append(lmul(zx_out[...], -conv))
        halves.append(rmul(jnp.concatenate(back, axis=0), y_out[...]))
    f = dss_lanes(jnp.concatenate(halves, axis=1))
    f_ref[...] = f
    for c in range(3):
        up_ref[16 * c : 16 * c + 16] = f[128 * c + 112 : 128 * c + 128]
        down_ref[16 * c : 16 * c + 16] = f[128 * c : 128 * c + 16]


def edge(ref, base, x):
    return jnp.concatenate([ref[base + x + 16 * z : base + x + 16 * z + 1] for z in range(8)], axis=0)


def add_edge(ref, base, x, rows):
    for z in range(8):
        ref[base + x + 16 * z : base + x + 16 * z + 1] += rows[z : z + 1]


def div_msg_kernel(f_ref, fb_ref, fa_ref, m01, m2, wd_y, w_y, fz_ref, r_ref, l_ref):
    has_b, has_a, _, _ = flags()
    fz_ref[...] = f_ref[...]
    for c in range(3):
        piece = slice(16 * c, 16 * c + 16)
        fz_ref[128 * c : 128 * c + 16] += fb_ref[piece] * has_b
        fz_ref[128 * c + 112 : 128 * c + 128] += fa_ref[piece] * has_a
    f = fz_ref[...]
    s = lmul(m01[...], f[:256]) * w_y[...] + rmul_halves(lmul(m2[...], f[256:]), wd_y[...])
    r_ref[:16] = s[:16]
    l_ref[:16] = s[16:]
    for c in range(3):
        r_ref[16 + 8 * c : 24 + 8 * c] = edge(fz_ref, 128 * c, 15)
        l_ref[16 + 8 * c : 24 + 8 * c] = edge(fz_ref, 128 * c, 0)


def extend_into(s, from_l, from_r, out_ref, acc_ref):
    acc_ref[...] = s
    add_edge(acc_ref, 0, 0, from_l[8:16])
    add_edge(acc_ref, 0, 15, from_r[8:16])
    acc_ref[128:136] += from_l[:8]
    acc_ref[136:144] += from_r[:8]
    return dss_lanes(acc_ref[...])


def layers_out(s, up_ref, down_ref):
    up_ref[:32] = s[96:128]
    up_ref[32:] = s[128:]
    down_ref[:32] = s[:32]
    down_ref[32:] = s[128:]


def div_kernel(
    fz_ref, ml_ref, mr_ref, m01, m2, wd_y, w_y, f_ref, s_ref, up_ref, down_ref, acc_ref
):
    _, _, has_l, has_r = flags()
    ml, mr = ml_ref[...] * has_l, mr_ref[...] * has_r
    f_ref[...] = fz_ref[...]
    rows = []
    for c in range(3):
        base = 128 * c
        add_edge(f_ref, base, 0, ml[16 + 8 * c : 24 + 8 * c])
        add_edge(f_ref, base, 15, mr[16 + 8 * c : 24 + 8 * c])
        rows += [
            f_ref[base : base + 128],
            edge(fz_ref, base, 0) * has_l,
            edge(fz_ref, base, 15) * has_r,
        ]
    f01 = jnp.concatenate(rows[:6], axis=0)
    f2 = jnp.concatenate(rows[6:], axis=0)
    s = lmul(m01[...], f01) * w_y[...] + rmul_halves(lmul(m2[...], f2), wd_y[...])
    s = extend_into(s, ml, mr, s_ref, acc_ref)
    s_ref[...] = s
    layers_out(s, up_ref, down_ref)


def box_kernel(s_ref, sb_ref, sa_ref, box_in, ybox_in, inv, box_out, ybox_out, g_ref, up_ref, down_ref):
    has_b, has_a, has_l, has_r = flags()
    s = jnp.concatenate([s_ref[...], sb_ref[...] * has_b, sa_ref[...] * has_a], axis=0)
    t = rmul(lmul(box_in[...], s), ybox_in[...]) * inv[...]
    g = rmul(lmul(box_out[...], t), ybox_out[...])
    row = lax.broadcasted_iota(jnp.int32, (128, 1), 0)
    z, x = row // 16, row % 16
    weight = 1.0 - 0.5 * jnp.where(z == 0, has_b, jnp.where(z == 7, has_a, 0.0))
    weight = weight * (1.0 - 0.5 * jnp.where(x == 0, has_l, jnp.where(x == 15, has_r, 0.0)))
    g = g * weight
    g_ref[...] = g
    up_ref[...] = g[112:]
    down_ref[...] = g[:16]


def join_z(g_ref, gb_ref, ga_ref, out_ref):
    has_b, has_a, _, _ = flags()
    out_ref[...] = g_ref[...]
    out_ref[:16] += gb_ref[...] * has_b
    out_ref[112:] += ga_ref[...] * has_a


def stiff_msg_kernel(g_ref, gb_ref, ga_ref, st_msg, k_y, w_y, gz_ref, r_ref, l_ref):
    join_z(g_ref, gb_ref, ga_ref, gz_ref)
    both = lmul(st_msg[...], gz_ref[...])
    s = both[:32] * w_y[...] + rmul_halves(both[32:], k_y[...])
    r_ref[:16] = s[:16]
    l_ref[:16] = s[16:]
    r_ref[16:] = edge(gz_ref, 0, 15)
    l_ref[16:] = edge(gz_ref, 0, 0)


def stiff_kernel(
    gz_ref, ml_ref, mr_ref, s_ref, st, k_y, w_y, p_ref, res_ref, up_ref, down_ref, acc_ref
):
    _, _, has_l, has_r = flags()
    ml, mr = ml_ref[...] * has_l, mr_ref[...] * has_r
    p_ref[...] = gz_ref[...]
    add_edge(p_ref, 0, 0, ml[16:])
    add_edge(p_ref, 0, 15, mr[16:])
    rows = [p_ref[...], edge(gz_ref, 0, 0) * has_l, edge(gz_ref, 0, 15) * has_r]
    both = lmul(st[...], jnp.concatenate(rows, axis=0))
    s = both[:144] * w_y[...] + rmul_halves(both[144:], k_y[...])
    res = s_ref[...] - extend_into(s, ml, mr, res_ref, acc_ref)
    res_ref[...] = res
    layers_out(res, up_ref, down_ref)


def last_z_kernel(g_ref, gb_ref, ga_ref, p_ref, out_ref, r_ref, l_ref):
    join_z(g_ref, gb_ref, ga_ref, out_ref)
    r_ref[...] = edge(out_ref, 0, 15)
    l_ref[...] = edge(out_ref, 0, 0)
    out_ref[...] += p_ref[...]


def last_x_kernel(g_ref, ml_ref, mr_ref, out_ref):
    _, _, has_l, has_r = flags()
    out_ref[...] = g_ref[...]
    add_edge(out_ref, 0, 0, ml_ref[...] * has_l)
    add_edge(out_ref, 0, 15, mr_ref[...] * has_r)


def call(kernel, name, outs, *args, scratch=(), vmem=16):
    shape = lambda rows: jax.ShapeDtypeStruct(rows if isinstance(rows, tuple) else (rows, 512), F32)
    spec = pl.BlockSpec(memory_space=pltpu.VMEM)
    return pl.pallas_call(
        kernel,
        out_shape=[shape(o) for o in outs],
        in_specs=[spec] * len(args),
        out_specs=[spec] * len(outs),
        scratch_shapes=[pltpu.VMEM((rows, 512), F32) for rows in scratch],
        compiler_params=pltpu.CompilerParams(vmem_limit_bytes=vmem * MIB),
        name=name,
    )(*args)


def exchange(axis, forward, backward):
    n = lax.axis_size(axis)
    ahead = [(i, (i + 1) % n) for i in range(n)]
    behind = [(j, i) for i, j in ahead]
    return lax.ppermute(forward, axis, ahead), lax.ppermute(backward, axis, behind)


def shards(velocity, bfield):
    c = {name: jnp.asarray(value) for name, value in constants().items()}
    consts = lambda *names: [c[name] for name in names]
    f, up, down = call(
        force_kernel,
        "force",
        (384, 48, 48),
        velocity,
        bfield,
        *consts("y_in", "zx_in", "zx_out", "y_out"),
        vmem=40,
    )
    below, above = exchange("wide", up, down)
    fz, right, left = call(
        div_msg_kernel,
        "div_msg",
        (384, 40, 40),
        f,
        below,
        above,
        *consts("div_msg01", "div_msg2", "wd_y", "w_y"),
    )
    from_l, from_r = exchange("narrow", right, left)
    force, s, up, down = call(
        div_kernel,
        "div",
        (384, 144, 48, 48),
        fz,
        from_l,
        from_r,
        *consts("div01", "div2", "wd_y", "w_y"),
        scratch=(144,),
    )
    box = consts("box_in", "ybox_in", "inv", "box_out", "ybox_out")
    below, above = exchange("wide", up, down)
    g, up, down = call(box_kernel, "box_first", (128, 16, 16), s, below, above, *box)
    below, above = exchange("wide", up, down)
    gz, right, left = call(
        stiff_msg_kernel,
        "stiff_msg",
        (128, 24, 24),
        g,
        below,
        above,
        *consts("st_msg", "k_y", "w_y"),
    )
    from_l, from_r = exchange("narrow", right, left)
    first, res, up, down = call(
        stiff_kernel,
        "stiff",
        (128, 144, 48, 48),
        gz,
        from_l,
        from_r,
        s,
        *consts("st", "k_y", "w_y"),
        scratch=(144,),
    )
    below, above = exchange("wide", up, down)
    g, up, down = call(box_kernel, "box_second", (128, 16, 16), res, below, above, *box)
    below, above = exchange("wide", up, down)
    total, right, left = call(last_z_kernel, "last_z", (128, 8, 8), g, below, above, first)
    from_l, from_r = exchange("narrow", right, left)
    (pressure,) = call(last_x_kernel, "last_x", (128,), total, from_l, from_r)
    return force.reshape(3, 8, 16, 512), pressure.reshape(8, 16, 512)


def solution(mesh):
    placed = (P(None, "wide", "narrow", None), P("wide", "narrow", None))
    return jax.shard_map(
        shards, mesh=mesh, in_specs=placed, out_specs=placed, check_vma=False
    )
```

```python
import functools

import jax
import jax.numpy as jnp
import ml_dtypes
import numpy as np
from jax import lax
from jax.experimental import pallas as pl
from jax.experimental.pallas import tpu as pltpu
from jax.sharding import PartitionSpec as P

F32 = jnp.float32
BF16 = jnp.bfloat16
MIB = 2**20
FORCE_VMEM = 56


def legendre_pair(degree, points):
    below, current = np.ones(points.shape), points * 1.0
    for step in range(2, degree + 1):
        below, current = current, ((2 * step - 1) * points * current - (step - 1) * below) / step
    return current, below


def tables_1d():
    points = np.cos(np.pi * np.arange(8) / 7)
    for _ in range(60):
        top, below = legendre_pair(7, points)
        points = points - (points * top - below) / (8 * top)
    points = np.sort(points)
    top, below = legendre_pair(7, points)
    w = 2.0 / (56 * top**2)
    spacing = points[:, None] - points[None, :] + np.eye(8)
    deriv = top[:, None] / (top[None, :] * spacing) * (1.0 - np.eye(8))
    deriv[0, 0], deriv[-1, -1] = -14.0, 14.0
    gauss = np.cos(np.pi * (np.arange(12) + 0.75) / 12.5)
    for _ in range(60):
        top, below = legendre_pair(12, gauss)
        gauss = gauss - top / (12 * (gauss * top - below) / (gauss**2 - 1.0))
    top, below = legendre_pair(12, gauss)
    slope = 12 * (gauss * top - below) / (gauss**2 - 1.0)
    v = 2.0 / ((1.0 - gauss**2) * slope**2)
    interp = np.ones((12, 8))
    for col in range(8):
        for other in range(8):
            if other != col:
                interp[:, col] *= (gauss - points[other]) / (points[col] - points[other])
    stiff = deriv.T @ (w[:, None] * deriv)
    wide_stiff, wide_mass = np.zeros((22, 22)), np.zeros(22)
    for el in range(3):
        r = 7 * el
        wide_stiff[r : r + 8, r : r + 8] += stiff
        wide_mass[r : r + 8] += w
    scale = 1.0 / np.sqrt(wide_mass[6:16])
    lam, vec = np.linalg.eigh(scale[:, None] * wide_stiff[6:16, 6:16] * scale[None, :])
    return interp, interp @ deriv, deriv, stiff, w, scale[:, None] * vec, lam, v


def hi_lo(m):
    hi = m.astype(ml_dtypes.bfloat16)
    return hi, (m - hi.astype(np.float64)).astype(ml_dtypes.bfloat16)


def left_const(m):
    hi, lo = hi_lo(m)
    return np.concatenate([hi, hi, lo], axis=1)


def right_const(m):
    hi, lo = hi_lo(m)
    return np.concatenate([hi, hi, lo], axis=0)


def block_diag(m, count):
    return np.kron(np.eye(count), m)


def own(z, x):
    return 16 * z + x


def local_rows(terms, xs):
    out = np.zeros((8 * len(xs), 128))
    for k, x in enumerate(xs):
        el, j = divmod(x, 8)
        for z in range(8):
            for zm, xm in terms:
                for z2 in range(8):
                    for j2 in range(8):
                        out[8 * k + z, own(z2, 8 * el + j2)] += zm[z, z2] * xm[j, j2]
    return out


def extended_rows(terms):
    local = local_rows(terms, range(16)).reshape(16, 8, 128)
    out = np.zeros((144, 144))
    for x in range(16):
        for z in range(8):
            out[own(z, x), :128] = local[x, z]
            if x in (7, 8):
                out[own(z, x), :128] += local[15 - x, z]
    for z in range(8):
        for zm, xm in terms:
            for z2 in range(8):
                out[own(z, 0), 128 + z2] += zm[z, z2] * xm[7, 7]
                out[128 + z, 128 + z2] += zm[z, z2] * xm[6, 7]
                out[own(z, 15), 136 + z2] += zm[z, z2] * xm[0, 0]
                out[136 + z, 136 + z2] += zm[z, z2] * xm[1, 0]
    return out


def z_rows(mats):
    blocks = [np.zeros((144, 144)) for _ in mats]
    for out, m in zip(blocks, mats):
        out[:128, :128] = np.kron(m, np.eye(16))
        out[128:136, 128:136] = m
        out[136:, 136:] = m
    return np.concatenate(blocks, axis=1)


def join_rows(zm, w):
    out = np.zeros((192, 384))
    below, above, down, up, far_b, far_a = 144, 200, 256, 296, 336, 360
    for t in range(18):
        side = t - 16
        own_row = lambda z: own(z, t) if t < 16 else 128 + 8 * side + z
        layer = lambda base, k: base + 16 * k + t if t < 16 else base + 48 + 2 * side + k
        msg_face = lambda base: base + 32 + t if t < 16 else base + 52 + side
        face = lambda base, k: base + 16 * k + t if t < 16 else base + 36 + 2 * k + side
        far = lambda base: base + t if t < 16 else base + 20 + side
        b7, b6, a0, a1 = np.zeros((4, 384))
        b7[layer(below, 1)] = b6[layer(below, 0)] = 1.0
        b7[face(down, 0)], b7[face(down, 1)], b7[far(far_b)] = zm[7, 7], w[7], zm[7, 0]
        b6[face(down, 0)], b6[far(far_b)] = zm[6, 7], zm[6, 0]
        a0[layer(above, 0)] = a1[layer(above, 1)] = 1.0
        a0[face(up, 0)], a0[face(up, 1)], a0[far(far_a)] = zm[0, 0], w[0], zm[0, 7]
        a1[face(up, 0)], a1[far(far_a)] = zm[1, 0], zm[1, 7]
        for z in range(8):
            row = out[own_row(z)]
            row[own_row(z)] += 1.0
            row[msg_face(below)] += zm[z, 0]
            row[msg_face(above)] += zm[z, 7]
        out[own_row(0)] += b7
        out[own_row(7)] += a0
        out[144 + t], out[168 + t] = b6, a1
    return out


def box_rows(vec):
    nodes = np.zeros((10, 2, 10, 192))
    for zk in range(10):
        for el in range(2):
            for xk in range(10):
                x = 8 * el + (-2 if xk == 0 else 9 if xk == 9 else xk - 1)
                side = -1 if x < 0 else 1 if x > 15 else 0
                if 0 < zk < 9:
                    row = {0: own(zk - 1, x), -1: 128 + zk - 1, 1: 136 + zk - 1}[side]
                else:
                    row = (144 if zk == 0 else 168) + {0: x, -1: 16, 1: 17}[side]
                nodes[zk, el, xk, row] = 1.0
    into = np.einsum("zi,xj,zexr->iejr", vec, vec, nodes).reshape(200, 192)
    back = np.zeros((8, 16, 10, 2, 10))
    inner = vec[1:9]
    for z in range(8):
        for x in range(16):
            el, j = divmod(x, 8)
            block = inner[z][:, None] * inner[j][None, :]
            if x in (7, 8):
                back[z, x, :, el] += 0.5 * block
                back[z, x, :, 1 - el] += 0.5 * inner[z][:, None] * inner[7 - j][None, :]
            else:
                back[z, x, :, el] += block
    back = back.reshape(128, 200)
    return np.pad(into, ((0, 8), (0, 0))), np.pad(back, ((0, 0), (0, 8)))


def box_lanes(vec, count):
    into = np.zeros((8 * count, 10 * count))
    back = np.zeros((10 * count, 8 * count))
    for e in range(count):
        spots = [8 * e - 2] + list(range(8 * e, 8 * e + 8)) + [8 * e + 9]
        for k, y in enumerate(spots):
            if 0 <= y < 8 * count:
                into[y, 10 * e : 10 * e + 10] += vec[k]
        for j in range(8):
            col = vec[j + 1]
            y = 8 * e + j
            if j == 0 and e > 0:
                back[10 * e : 10 * e + 10, [y - 1, y]] += 0.5 * col[:, None]
            elif j == 7 and e < count - 1:
                back[10 * e : 10 * e + 10, [y, y + 1]] += 0.5 * col[:, None]
            else:
                back[10 * e : 10 * e + 10, y] += col
    return into, back


def face_coefs(zm):
    return np.array([[zm[0, 7], zm[1, 7]], [zm[6, 0], zm[7, 0]]])


def constants():
    interp, slopes, deriv, stiff, w, vec, lam, v = tables_1d()
    eye2 = np.eye(2)
    zx = lambda a, b: np.kron(a, np.kron(eye2, b))
    c = {}
    c["y_in"] = right_const(
        np.concatenate([block_diag(interp.T, 32), block_diag(slopes.T, 32)], axis=1)
    )
    c["zx_in"] = left_const(
        np.concatenate([zx(interp, interp), zx(slopes, interp), zx(interp, slopes)], axis=0)
    )
    test = v[:, None] * interp
    back = zx(test.T, test.T).reshape(8, 16, 288)
    pair = back[:, 7] + back[:, 8]
    back[:, 7], back[:, 8] = pair, pair
    c["zx_out"] = left_const(back.reshape(128, 288))
    c["y_out"] = right_const(block_diag(test, 32))
    one, wm, wd = np.eye(8), np.diag(w), w[:, None] * deriv
    sides = (14, 15, 1, 0)
    for name, xm in (("w", wm), ("wd", wd), ("k", stiff)):
        c["xm_" + name] = left_const(local_rows([(one, xm)], sides))
        c["xe_" + name] = left_const(extended_rows([(one, xm)]))
    c["z_div"], c["z_st"] = left_const(z_rows((wd, wm))), left_const(z_rows((stiff, wm)))
    c["join_div"], c["join_st"] = left_const(join_rows(wd, w)), left_const(join_rows(stiff, w))
    c["pick_div"], c["pick_st"] = face_coefs(wd), face_coefs(stiff)
    c["wd_y"] = right_const(block_diag(wd.T, 32))
    c["k_y"] = right_const(block_diag(stiff.T, 32))
    c["w_y"] = np.tile(w, 64)[None].astype(np.float32)
    into, back = box_rows(vec)
    c["box_in"], c["box_out"] = left_const(into), left_const(back)
    into, back = box_lanes(vec, 64)
    c["ybox_in"], c["ybox_out"] = right_const(into), right_const(back)
    inv = 1.0 / (lam[:, None, None, None] + lam[None, None, :, None] + lam)
    inv = np.broadcast_to(inv[:, :, :, None, :], (10, 1, 10, 64, 10))
    inv = np.broadcast_to(inv, (10, 2, 10, 64, 10)).reshape(200, 640)
    c["inv"] = np.pad(inv, ((0, 8), (0, 0))).astype(np.float32)
    return c


def split(x):
    hi = x.astype(BF16)
    return hi, (x - hi.astype(F32)).astype(BF16)


def rmul(x, const):
    hi, lo = split(x)
    return jnp.dot(jnp.concatenate([hi, lo, hi], axis=1), const, preferred_element_type=F32)


def lmul(const, x):
    hi, lo = split(x)
    return jnp.dot(const, jnp.concatenate([hi, lo, hi], axis=0), preferred_element_type=F32)


def rmul_halves(x, const):
    return jnp.concatenate([rmul(x[:, :256], const), rmul(x[:, 256:], const)], axis=1)


def dss_lanes(x):
    lane = lax.broadcasted_iota(jnp.int32, x.shape, 1)
    n = x.shape[1]
    up = jnp.where((lane % 8 == 7) & (lane < n - 1), pltpu.roll(x, n - 1, 1), 0.0)
    down = jnp.where((lane % 8 == 0) & (lane > 0), pltpu.roll(x, 1, 1), 0.0)
    return x + up + down


def flags():
    z, x = lax.axis_index("wide"), lax.axis_index("narrow")
    nz, nx = lax.axis_size("wide"), lax.axis_size("narrow")
    as_flag = lambda t: t.astype(F32)
    return as_flag(z > 0), as_flag(z < nz - 1), as_flag(x > 0), as_flag(x < nx - 1)


def force_kernel(*refs):
    sources, (f_ref, r_ref, l_ref), held, sem = refs[:10], refs[10:13], refs[13:23], refs[23]
    copies = [pltpu.make_async_copy(a, b, sem.at[k]) for k, (a, b) in enumerate(zip(sources, held))]
    for k in (0, 2, 1, 3, 4, 5, 6, 7, 8, 9):
        copies[k].start()
    v_ref, b_ref, y_in, zx_in, zx_out, y_out, xm_w, xm_wd, wd_y, w_y = held
    copies[0].wait()
    copies[2].wait()
    copies[1].wait()
    copies[3].wait()
    v = v_ref[...].reshape(384, 512)
    b = b_ref[...].reshape(128, 512)
    halves = []
    for h in range(2):
        cut = slice(256 * h, 256 * h + 256)
        first = rmul(v[:, cut], y_in[...])
        bq = lmul(zx_in[:288, :], rmul(b[:, cut], y_in[:, :384]))
        u, gz, gx, gy = [], [], [], []
        for c in range(3):
            rows = slice(128 * c, 128 * c + 128)
            most = lmul(zx_in[...], first[rows, :384])
            u.append(most[:288])
            gz.append(most[288:576])
            gx.append(most[576:])
            gy.append(lmul(zx_in[:288, :], first[rows, 384:]))
        b2 = bq * bq
        back = []
        if h == 0:
            for copy in copies[4:]:
                copy.wait()
        for c in range(3):
            conv = u[0] * gz[c] + u[1] * gx[c] + u[2] * gy[c]
            if c != 1:
                conv = conv + b2 * u[c]
            back.append(lmul(zx_out[...], -conv))
        halves.append(rmul(jnp.concatenate(back, axis=0), y_out[...]))
    f = dss_lanes(jnp.concatenate(halves, axis=1))
    f_ref[...] = f
    s = lmul(xm_wd[...], f[128:256]) * w_y[...]
    s = s + rmul_halves(lmul(xm_w[...], f[256:]), wd_y[...])
    r_ref[:16] = s[:16]
    l_ref[:16] = s[16:]
    for k, (c, step) in enumerate(((0, 0), (1, 0), (2, 0), (0, 1))):
        r_ref[16 + 8 * k : 24 + 8 * k] = edge(f_ref, 128 * c, 15 - step)
        l_ref[16 + 8 * k : 24 + 8 * k] = edge(f_ref, 128 * c, step)


def edge(ref, base, x):
    return jnp.concatenate([ref[base + x + 16 * z : base + x + 16 * z + 1] for z in range(8)], axis=0)


def add_edge(ref, base, x, rows):
    for z in range(8):
        ref[base + x + 16 * z : base + x + 16 * z + 1] += rows[z : z + 1]


def extend(s, from_l, from_r, acc_ref):
    acc_ref[...] = s
    add_edge(acc_ref, 0, 0, from_l[8:16])
    add_edge(acc_ref, 0, 15, from_r[8:16])
    acc_ref[128:136] += from_l[:8]
    acc_ref[136:144] += from_r[:8]
    acc_ref[...] = dss_lanes(acc_ref[...])


def with_edges(full, raw_ref, base, has_l, has_r):
    edges = [edge(raw_ref, base, 0) * has_l, edge(raw_ref, base, 15) * has_r]
    return jnp.concatenate([full, *edges], axis=0)


def scaled_edges(ghost, last, w_y, ends):
    return jnp.concatenate([ghost * ends[0], last * ends[1]], axis=0) * w_y[...]


def send_faces(w_end, u, h0_ref, h12_ref, up_ref, down_ref, up_face_ref, down_face_ref, in_ref):
    for ref, own_ref, a, b, z in (
        (up_ref, up_face_ref, 6, 7, 7),
        (down_ref, down_face_ref, 0, 1, 0),
    ):
        ref[:16] = u[16 * a : 16 * a + 16]
        ref[16:32] = u[16 * b : 16 * b + 16]
        ref[32:48] = own_ref[:16] = h0_ref[16 * z : 16 * z + 16]
        own_ref[16:32] = h12_ref[16 * z : 16 * z + 16]
        half = 16 if z == 7 else 0
        ref[half : half + 16] += w_end * own_ref[16:32]
        h12 = [w_end * h12_ref[128 + 8 * s + z : 129 + 8 * s + z] for s in (0, 1)]
        rows = [u[128 + 8 * s + k : 129 + 8 * s + k] for s in (0, 1) for k in (a, b)]
        rows[z // 7] = rows[z // 7] + h12[0]
        rows[2 + z // 7] = rows[2 + z // 7] + h12[1]
        faces = [h[128 + 8 * s + z : 129 + 8 * s + z] for h in (h0_ref, h12_ref) for s in (0, 1)]
        ref[48:56] = jnp.concatenate(rows + faces, axis=0)
        own_ref[32:] = ref[48:56]
    in_ref[...] = jnp.where(is_odd(), down_ref[...], up_ref[...])


def is_odd():
    return lax.axis_index("wide") % 2 == 1


def div_kernel(ends, f_ref, ml_ref, mr_ref, xe_w, xe_wd, z_div, wd_y, w_y, *refs):
    force_ref, f_up_ref, f_down_ref, u_ref, *faces = refs[:9]
    h0_ref, h12_ref, fx_ref, sem = refs[9:]
    _, _, has_l, has_r = flags()
    ml, mr = ml_ref[...] * has_l, mr_ref[...] * has_r
    fx_ref[...] = f_ref[...]
    full = []
    for c in range(3):
        base, piece = 128 * c, slice(16 + 8 * c, 24 + 8 * c)
        add_edge(fx_ref, base, 0, ml[piece])
        add_edge(fx_ref, base, 15, mr[piece])
        full.append(with_edges(fx_ref[base : base + 128], f_ref, base, has_l, has_r))
        f_up_ref[16 * c : 16 * c + 16] = fx_ref[base + 112 : base + 128]
        f_down_ref[16 * c : 16 * c + 16] = fx_ref[base : base + 16]
    copy = pltpu.make_async_copy(fx_ref, force_ref, sem.at[0])
    copy.start()
    from_l = scaled_edges(ml[40:48], ml[16:24], w_y, ends)
    from_r = scaled_edges(mr[40:48], mr[16:24], w_y, ends)
    extend(lmul(xe_w[...], full[0]) * w_y[...], from_l, from_r, h0_ref)
    h = lmul(xe_wd[...], full[1]) * w_y[...] + rmul_halves(lmul(xe_w[...], full[2]), wd_y[...])
    extend(h, ml[:16], mr[:16], h12_ref)
    u = lmul(z_div[...], jnp.concatenate([h0_ref[...], h12_ref[...]], axis=0))
    u_ref[...] = u
    send_faces(ends[1], u, h0_ref, h12_ref, *faces)
    copy.wait()


def outer_kernel(coefs, up_ref, down_ref, in_ref, out_ref):
    odd = is_odd()
    ca = jnp.where(odd, coefs[1][0], coefs[0][0])
    cb = jnp.where(odd, coefs[1][1], coefs[0][1])
    out_ref[...] = jnp.where(odd, up_ref[...], down_ref[...])
    face, far_l, far_r = in_ref[32:48], in_ref[52:53], in_ref[53:54]
    out_ref[:16] += ca * face
    out_ref[16:32] += cb * face
    out_ref[48:52] += jnp.concatenate([ca * far_l, cb * far_l, ca * far_r, cb * far_r], axis=0)


def far_kernel(out_msg_ref, far_ref):
    has_b, has_a, _, _ = flags()
    flag = jnp.where(is_odd(), has_a, has_b)
    far_ref[:16] = out_msg_ref[32:48] * flag
    far_ref[16:] = out_msg_ref[48:56] * flag


def join(u_ref, up_ref, down_ref, in_ref, out_ref, far_ref, const):
    has_b, has_a, _, _ = flags()
    odd = is_odd()
    inner = in_ref[...]
    outer = out_ref[...] * jnp.where(odd, has_a, has_b)
    far = far_ref[...]
    rows = [
        u_ref[...],
        jnp.where(odd, inner, outer),
        jnp.where(odd, outer, inner),
        down_ref[...] * has_b,
        up_ref[...] * has_a,
        jnp.where(odd, far, 0.0),
        jnp.where(odd, 0.0, far),
    ]
    return lmul(const[...], jnp.concatenate(rows, axis=0))


def box(s, box_in, ybox_in, inv, box_out, ybox_out):
    has_b, has_a, has_l, has_r = flags()
    t = rmul(lmul(box_in[...], s), ybox_in[...]) * inv[...]
    g = rmul(lmul(box_out[...], t), ybox_out[...])
    row = lax.broadcasted_iota(jnp.int32, (128, 1), 0)
    z, x = row // 16, row % 16
    weight = 1.0 - 0.5 * jnp.where(z == 0, has_b, jnp.where(z == 7, has_a, 0.0))
    weight = weight * (1.0 - 0.5 * jnp.where(x == 0, has_l, jnp.where(x == 15, has_r, 0.0)))
    return g * weight


def first_kernel(*refs):
    join_refs, box_refs, (xm_w, xm_k, k_y, w_y) = refs[:7], refs[7:12], refs[12:16]
    s_ref, g_ref, r_ref, l_ref = refs[16:]
    s = join(*join_refs)
    s_ref[...] = s
    g = box(s, *box_refs)
    g_ref[...] = g
    q = lmul(xm_k[...], g) * w_y[...] + rmul_halves(lmul(xm_w[...], g), k_y[...])
    r_ref[:16] = q[:16]
    l_ref[:16] = q[16:]
    r_ref[16:24] = edge(g_ref, 0, 15)
    l_ref[16:24] = edge(g_ref, 0, 0)
    r_ref[24:] = edge(g_ref, 0, 14)
    l_ref[24:] = edge(g_ref, 0, 1)


def stiff_kernel(ends, g_ref, ml_ref, mr_ref, xe_w, xe_k, z_st, k_y, w_y, *refs):
    gx_ref, u_ref, *faces = refs[:7]
    p_ref, q_ref = refs[7:]
    _, _, has_l, has_r = flags()
    ml, mr = ml_ref[...] * has_l, mr_ref[...] * has_r
    gx_ref[...] = g_ref[...]
    add_edge(gx_ref, 0, 0, ml[16:24])
    add_edge(gx_ref, 0, 15, mr[16:24])
    full = with_edges(gx_ref[...], g_ref, 0, has_l, has_r)
    from_l = scaled_edges(ml[24:], ml[16:24], w_y, ends)
    from_r = scaled_edges(mr[24:], mr[16:24], w_y, ends)
    plain = lmul(xe_w[...], full)
    extend(plain * w_y[...], from_l, from_r, p_ref)
    q = lmul(xe_k[...], full) * w_y[...] + rmul_halves(plain, k_y[...])
    extend(q, ml[:16], mr[:16], q_ref)
    u = lmul(z_st[...], jnp.concatenate([p_ref[...], q_ref[...]], axis=0))
    u_ref[...] = u
    send_faces(ends[1], u, p_ref, q_ref, *faces)


def second_kernel(s_ref, *refs):
    join_refs, box_refs, (g_ref, r_ref, l_ref) = refs[:7], refs[7:12], refs[12:]
    g_ref[...] = box(s_ref[...] - join(*join_refs), *box_refs)
    r_ref[...] = edge(g_ref, 0, 15)
    l_ref[...] = edge(g_ref, 0, 0)


def last_x_kernel(g_ref, gx_ref, ml_ref, mr_ref, f_up, f_down, out_ref, in_msg_ref, out_msg_ref):
    _, _, has_l, has_r = flags()
    out_ref[...] = g_ref[...] + gx_ref[...]
    add_edge(out_ref, 0, 0, ml_ref[...] * has_l)
    add_edge(out_ref, 0, 15, mr_ref[...] * has_r)
    odd = is_odd()
    for rows, up, down in (
        (slice(0, 16), out_ref[112:], out_ref[:16]),
        (slice(16, 64), f_up[...], f_down[...]),
    ):
        in_msg_ref[rows] = jnp.where(odd, down, up)
        out_msg_ref[rows] = jnp.where(odd, up, down)


def last_z_kernel(g_ref, f_up, f_down, in_ref, out_msg_ref, _, out_ref, force_ref, face_ref, sem):
    has_b, has_a, _, _ = flags()
    odd = is_odd()
    inner, outer = in_ref[...], out_msg_ref[...] * jnp.where(odd, has_a, has_b)
    below, above = jnp.where(odd, inner, outer), jnp.where(odd, outer, inner)
    face_ref[:48] = f_down[...] + below[16:]
    face_ref[48:] = f_up[...] + above[16:]
    copies = []
    for c in range(3):
        for k, row in enumerate((128 * c, 128 * c + 112)):
            src = face_ref.at[pl.ds(48 * k + 16 * c, 16)]
            dst = force_ref.at[pl.ds(row, 16)]
            copies.append(pltpu.make_async_copy(src, dst, sem.at[2 * c + k]))
            copies[-1].start()
    out_ref[...] = g_ref[...]
    out_ref[:16] += below[:16]
    out_ref[112:] += above[:16]
    for copy in copies:
        copy.wait()


def call(kernel, name, outs, *args, scratch=(), sems=0, vmem=16, hbm_in=(), hbm_out=(), alias=None):
    shape = lambda rows: jax.ShapeDtypeStruct((rows, 512), F32)
    spec = lambda k, far: pl.BlockSpec(memory_space=pltpu.HBM if k in far else pltpu.VMEM)
    scratch = [pltpu.VMEM((k, 512), F32) if isinstance(k, int) else k for k in scratch]
    return pl.pallas_call(
        kernel,
        out_shape=[shape(o) for o in outs],
        in_specs=[spec(k, hbm_in) for k in range(len(args))],
        out_specs=[spec(k, hbm_out) for k in range(len(outs))],
        scratch_shapes=scratch + ([pltpu.SemaphoreType.DMA((sems,))] if sems else []),
        input_output_aliases=alias or {},
        compiler_params=pltpu.CompilerParams(vmem_limit_bytes=vmem * MIB),
        name=name,
    )(*args)


def exchange_x(rightward, leftward):
    n = lax.axis_size("narrow")
    right = [(i, (i + 1) % n) for i in range(n)]
    left = [(j, i) for i, j in right]
    return lax.ppermute(rightward, "narrow", right), lax.ppermute(leftward, "narrow", left)


def other_core(x):
    n = lax.axis_size("wide")
    return lax.ppermute(x, "wide", [(i, i + 1 - 2 * (i % 2)) for i in range(n)])


def next_chip(x):
    nz, nx = lax.axis_size("wide"), lax.axis_size("narrow")
    pairs = []
    for z in range(nz):
        to = z - 1 + 2 * (z % 2)
        for k in range(nx):
            other = (to, k) if 0 <= to < nz else (z, k + 1 - 2 * (k % 2))
            pairs.append((z * nx + k, other[0] * nx + other[1]))
    return lax.ppermute(x, ("wide", "narrow"), pairs)


def meet(up, down, inner_msg, coefs, name):
    inner = other_core(inner_msg)
    coefs = [[float(t) for t in row] for row in coefs]
    (msg,) = call(functools.partial(outer_kernel, coefs), name, (56,), up, down, inner)
    outer = next_chip(msg)
    (far,) = call(far_kernel, name + "_far", (24,), outer)
    return inner, outer, other_core(far)


def shards(velocity, bfield):
    tables = constants()
    picks = tables.pop("pick_div"), tables.pop("pick_st")
    c = {name: jnp.asarray(value) for name, value in tables.items()}
    consts = lambda *names: [c[name] for name in names]
    weights = tables_1d()[4]
    ends = float(weights[1]), float(weights[0])
    force_args = (
        velocity,
        bfield,
        *consts("y_in", "zx_in", "zx_out", "y_out", "xm_w", "xm_wd", "wd_y", "w_y"),
    )
    f, right, left = call(
        force_kernel,
        "force",
        (384, 48, 48),
        *force_args,
        scratch=[pltpu.VMEM(a.shape, a.dtype) for a in force_args],
        sems=10,
        vmem=FORCE_VMEM,
        hbm_in=range(10),
    )
    from_l, from_r = exchange_x(right, left)
    force, f_up, f_down, u, up, down, up_face, down_face, inner = call(
        functools.partial(div_kernel, ends),
        "div",
        (384, 48, 48, 144, 56, 56, 40, 40, 56),
        f,
        from_l,
        from_r,
        *consts("xe_w", "xe_wd", "z_div", "wd_y", "w_y"),
        scratch=(144, 144, 384),
        sems=1,
        hbm_out=(0,),
    )
    inner, outer, far = meet(up, down, inner, picks[0], "div_out")
    box_consts = consts("box_in", "ybox_in", "inv", "box_out", "ybox_out")
    s, g, right, left = call(
        first_kernel,
        "first_pass",
        (192, 128, 32, 32),
        u,
        up_face,
        down_face,
        inner,
        outer,
        far,
        c["join_div"],
        *box_consts,
        *consts("xm_w", "xm_k", "k_y", "w_y"),
    )
    from_l, from_r = exchange_x(right, left)
    gx, u, up, down, up_face, down_face, inner = call(
        functools.partial(stiff_kernel, ends),
        "stiff",
        (128, 144, 56, 56, 40, 40, 56),
        g,
        from_l,
        from_r,
        *consts("xe_w", "xe_k", "z_st", "k_y", "w_y"),
        scratch=(144, 144),
    )
    inner, outer, far = meet(up, down, inner, picks[1], "stiff_out")
    g, right, left = call(
        second_kernel,
        "second_pass",
        (128, 8, 8),
        s,
        u,
        up_face,
        down_face,
        inner,
        outer,
        far,
        c["join_st"],
        *box_consts,
    )
    from_l, from_r = exchange_x(right, left)
    total, inner, outer = call(
        last_x_kernel, "last_x", (128, 64, 64), g, gx, from_l, from_r, f_up, f_down
    )
    outer, inner = next_chip(outer), other_core(inner)
    pressure, force = call(
        last_z_kernel,
        "last_z",
        (128, 384),
        total,
        f_up,
        f_down,
        inner,
        outer,
        force,
        scratch=(96,),
        sems=6,
        hbm_in=(5,),
        hbm_out=(1,),
        alias={5: 1},
    )
    return force.reshape(3, 8, 16, 512), pressure.reshape(8, 16, 512)


def solution(mesh):
    placed = (P(None, "wide", "narrow", None), P("wide", "narrow", None))
    return jax.shard_map(
        shards, mesh=mesh, in_specs=placed, out_specs=placed, check_vma=False
    )
```

```python
import functools

import jax
import jax.numpy as jnp
import ml_dtypes
import numpy as np
from jax import lax
from jax.experimental import pallas as pl
from jax.experimental.pallas import tpu as pltpu
from jax.sharding import PartitionSpec as P

F32 = jnp.float32
BF16 = jnp.bfloat16
MIB = 2**20


def legendre_pair(degree, points):
    below, current = np.ones(points.shape), points * 1.0
    for step in range(2, degree + 1):
        below, current = current, ((2 * step - 1) * points * current - (step - 1) * below) / step
    return current, below


def tables_1d():
    points = np.cos(np.pi * np.arange(8) / 7)
    for _ in range(60):
        top, below = legendre_pair(7, points)
        points = points - (points * top - below) / (8 * top)
    points = np.sort(points)
    top, below = legendre_pair(7, points)
    w = 2.0 / (56 * top**2)
    spacing = points[:, None] - points[None, :] + np.eye(8)
    deriv = top[:, None] / (top[None, :] * spacing) * (1.0 - np.eye(8))
    deriv[0, 0], deriv[-1, -1] = -14.0, 14.0
    gauss = np.cos(np.pi * (np.arange(12) + 0.75) / 12.5)
    for _ in range(60):
        top, below = legendre_pair(12, gauss)
        gauss = gauss - top / (12 * (gauss * top - below) / (gauss**2 - 1.0))
    top, below = legendre_pair(12, gauss)
    slope = 12 * (gauss * top - below) / (gauss**2 - 1.0)
    v = 2.0 / ((1.0 - gauss**2) * slope**2)
    interp = np.ones((12, 8))
    for col in range(8):
        for other in range(8):
            if other != col:
                interp[:, col] *= (gauss - points[other]) / (points[col] - points[other])
    stiff = deriv.T @ (w[:, None] * deriv)
    wide_stiff, wide_mass = np.zeros((22, 22)), np.zeros(22)
    for el in range(3):
        r = 7 * el
        wide_stiff[r : r + 8, r : r + 8] += stiff
        wide_mass[r : r + 8] += w
    scale = 1.0 / np.sqrt(wide_mass[6:16])
    lam, vec = np.linalg.eigh(scale[:, None] * wide_stiff[6:16, 6:16] * scale[None, :])
    return interp, interp @ deriv, deriv, stiff, w, scale[:, None] * vec, lam, v


def hi_lo(m):
    hi = m.astype(ml_dtypes.bfloat16)
    return hi, (m - hi.astype(np.float64)).astype(ml_dtypes.bfloat16)


def left_const(m):
    hi, lo = hi_lo(m)
    return np.concatenate([hi, hi, lo], axis=1)


def right_const(m):
    return np.concatenate(hi_lo(m), axis=0)


def block_diag(m, count):
    return np.kron(np.eye(count), m)


def own(z, x):
    return 16 * z + x


def local_rows(terms, xs):
    out = np.zeros((8 * len(xs), 128))
    for k, x in enumerate(xs):
        el, j = divmod(x, 8)
        for z in range(8):
            for zm, xm in terms:
                for z2 in range(8):
                    for j2 in range(8):
                        out[8 * k + z, own(z2, 8 * el + j2)] += zm[z, z2] * xm[j, j2]
    return out


def extended_rows(terms):
    local = local_rows(terms, range(16)).reshape(16, 8, 128)
    out = np.zeros((144, 144))
    for x in range(16):
        for z in range(8):
            out[own(z, x), :128] = local[x, z]
            if x in (7, 8):
                out[own(z, x), :128] += local[15 - x, z]
    for z in range(8):
        for zm, xm in terms:
            for z2 in range(8):
                out[own(z, 0), 128 + z2] += zm[z, z2] * xm[7, 7]
                out[128 + z, 128 + z2] += zm[z, z2] * xm[6, 7]
                out[own(z, 15), 136 + z2] += zm[z, z2] * xm[0, 0]
                out[136 + z, 136 + z2] += zm[z, z2] * xm[1, 0]
    return out


def z_rows(mats):
    blocks = [np.zeros((144, 144)) for _ in mats]
    for out, m in zip(blocks, mats):
        out[:128, :128] = np.kron(m, np.eye(16))
        out[128:136, 128:136] = m
        out[136:, 136:] = m
    return np.concatenate(blocks, axis=1)


def join_rows(zm, w):
    out = np.zeros((192, 384))
    below, above, down, up, far_b, far_a = 144, 200, 256, 296, 336, 360
    for t in range(18):
        side = t - 16
        own_row = lambda z: own(z, t) if t < 16 else 128 + 8 * side + z
        layer = lambda base, k: base + 16 * k + t if t < 16 else base + 48 + 2 * side + k
        msg_face = lambda base: base + 32 + t if t < 16 else base + 52 + side
        face = lambda base, k: base + 16 * k + t if t < 16 else base + 36 + 2 * k + side
        far = lambda base: base + t if t < 16 else base + 20 + side
        b7, b6, a0, a1 = np.zeros((4, 384))
        b7[layer(below, 1)] = b6[layer(below, 0)] = 1.0
        b7[face(down, 0)], b7[face(down, 1)], b7[far(far_b)] = zm[7, 7], w[7], zm[7, 0]
        b6[face(down, 0)], b6[far(far_b)] = zm[6, 7], zm[6, 0]
        a0[layer(above, 0)] = a1[layer(above, 1)] = 1.0
        a0[face(up, 0)], a0[face(up, 1)], a0[far(far_a)] = zm[0, 0], w[0], zm[0, 7]
        a1[face(up, 0)], a1[far(far_a)] = zm[1, 0], zm[1, 7]
        for z in range(8):
            row = out[own_row(z)]
            row[own_row(z)] += 1.0
            row[msg_face(below)] += zm[z, 0]
            row[msg_face(above)] += zm[z, 7]
        out[own_row(0)] += b7
        out[own_row(7)] += a0
        out[144 + t], out[168 + t] = b6, a1
    return out


def box_rows(vec):
    nodes = np.zeros((10, 2, 10, 192))
    for zk in range(10):
        for el in range(2):
            for xk in range(10):
                x = 8 * el + (-2 if xk == 0 else 9 if xk == 9 else xk - 1)
                side = -1 if x < 0 else 1 if x > 15 else 0
                if 0 < zk < 9:
                    row = {0: own(zk - 1, x), -1: 128 + zk - 1, 1: 136 + zk - 1}[side]
                else:
                    row = (144 if zk == 0 else 168) + {0: x, -1: 16, 1: 17}[side]
                nodes[zk, el, xk, row] = 1.0
    into = np.einsum("zi,xj,zexr->iejr", vec, vec, nodes).reshape(200, 192)
    back = np.zeros((8, 16, 10, 2, 10))
    inner = vec[1:9]
    for z in range(8):
        for x in range(16):
            el, j = divmod(x, 8)
            block = inner[z][:, None] * inner[j][None, :]
            if x in (7, 8):
                back[z, x, :, el] += 0.5 * block
                back[z, x, :, 1 - el] += 0.5 * inner[z][:, None] * inner[7 - j][None, :]
            else:
                back[z, x, :, el] += block
    back = back.reshape(128, 200)
    return np.pad(into, ((0, 8), (0, 0))), np.pad(back, ((0, 0), (0, 8)))


def box_lanes(vec, count):
    into = np.zeros((8 * count, 10 * count))
    back = np.zeros((10 * count, 8 * count))
    for e in range(count):
        spots = [8 * e - 2] + list(range(8 * e, 8 * e + 8)) + [8 * e + 9]
        for k, y in enumerate(spots):
            if 0 <= y < 8 * count:
                into[y, 10 * e : 10 * e + 10] += vec[k]
        for j in range(8):
            col = vec[j + 1]
            y = 8 * e + j
            if j == 0 and e > 0:
                back[10 * e : 10 * e + 10, [y - 1, y]] += 0.5 * col[:, None]
            elif j == 7 and e < count - 1:
                back[10 * e : 10 * e + 10, [y, y + 1]] += 0.5 * col[:, None]
            else:
                back[10 * e : 10 * e + 10, y] += col
    return into, back


def face_coefs(zm):
    return np.array([[zm[0, 7], zm[1, 7]], [zm[6, 0], zm[7, 0]]])


def constants():
    interp, slopes, deriv, stiff, w, vec, lam, v = tables_1d()
    eye2 = np.eye(2)
    zx = lambda a, b: np.kron(a, np.kron(eye2, b))
    c = {}
    c["y_in"] = right_const(
        np.concatenate([block_diag(interp.T, 32), block_diag(slopes.T, 32)], axis=1)
    )
    c["zx_in"] = np.concatenate(
        hi_lo(np.concatenate([zx(interp, interp), zx(slopes, interp), zx(interp, slopes)], axis=0)),
        axis=1,
    )
    test = v[:, None] * interp
    back = zx(test.T, test.T).reshape(8, 16, 288)
    pair = back[:, 7] + back[:, 8]
    back[:, 7], back[:, 8] = pair, pair
    c["zx_out"] = left_const(back.reshape(128, 288))
    c["y_out"] = right_const(block_diag(test, 32))
    one, wm, wd = np.eye(8), np.diag(w), w[:, None] * deriv
    sides = (14, 15, 1, 0)
    for name, xm in (("w", wm), ("wd", wd), ("k", stiff)):
        c["xm_" + name] = left_const(local_rows([(one, xm)], sides))
        c["xe_" + name] = left_const(extended_rows([(one, xm)]))
    c["z_div"], c["z_st"] = left_const(z_rows((wd, wm))), left_const(z_rows((stiff, wm)))
    c["join_div"], c["join_st"] = left_const(join_rows(wd, w)), left_const(join_rows(stiff, w))
    c["pick_div"], c["pick_st"] = face_coefs(wd), face_coefs(stiff)
    c["wd_y"] = right_const(block_diag(wd.T, 32))
    c["k_y"] = right_const(block_diag(stiff.T, 32))
    c["w_y"] = np.tile(w, 64)[None].astype(np.float32)
    into, back = box_rows(vec)
    c["box_in"], c["box_out"] = left_const(into), left_const(back)
    into, back = box_lanes(vec, 64)
    c["ybox_in"], c["ybox_out"] = right_const(into), right_const(back)
    inv = 1.0 / (lam[:, None, None, None] + lam[None, None, :, None] + lam)
    inv = np.broadcast_to(inv[:, :, :, None, :], (10, 1, 10, 64, 10))
    inv = np.broadcast_to(inv, (10, 2, 10, 64, 10)).reshape(200, 640)
    c["inv"] = np.pad(inv, ((0, 8), (0, 0))).astype(np.float32)
    return c


def split(x):
    hi = x.astype(BF16)
    return hi, (x - hi.astype(F32)).astype(BF16)


def rmul(x, const):
    hi, lo = split(x)
    depth = const.shape[0] // 2
    const = jnp.concatenate([const[:depth], const], axis=0)
    return jnp.dot(jnp.concatenate([hi, lo, hi], axis=1), const, preferred_element_type=F32)


def lmul(const, x):
    hi, lo = split(x)
    return jnp.dot(const, jnp.concatenate([hi, lo, hi], axis=0), preferred_element_type=F32)


def rmul_halves(x, const):
    return jnp.concatenate([rmul(x[:, :256], const), rmul(x[:, 256:], const)], axis=1)


def dss_lanes(x):
    lane = lax.broadcasted_iota(jnp.int32, x.shape, 1)
    n = x.shape[1]
    up = jnp.where((lane % 8 == 7) & (lane < n - 1), pltpu.roll(x, n - 1, 1), 0.0)
    down = jnp.where((lane % 8 == 0) & (lane > 0), pltpu.roll(x, 1, 1), 0.0)
    return x + up + down


def flags():
    z, x = lax.axis_index("wide"), lax.axis_index("narrow")
    nz, nx = lax.axis_size("wide"), lax.axis_size("narrow")
    as_flag = lambda t: t.astype(F32)
    return as_flag(z > 0), as_flag(z < nz - 1), as_flag(x > 0), as_flag(x < nx - 1)


def force_kernel(*refs):
    sources, (f_ref, r_ref, l_ref), held, sem = refs[:10], refs[10:13], refs[13:23], refs[23]
    v_ref, b_ref, y_in, zx_in, zx_out, y_out, xm_w, xm_wd, wd_y, w_y = held
    copies = [pltpu.make_async_copy(a, b, sem.at[k]) for k, (a, b) in enumerate(zip(sources, held))]
    for k in (2, 0, 1, 3, 4, 5, 6, 7, 8, 9):
        copies[k].start()
    copies[2].wait()
    copies[0].wait()
    v = v_ref[...].reshape(384, 512)
    parts = [rmul(v[:, cut], y_in[...]) for cut in (slice(0, 256), slice(256, 512))]
    value = jnp.concatenate([p[:, :384] for p in parts], axis=1)
    slope = jnp.concatenate([p[:, 384:] for p in parts], axis=1)
    for copy in (copies[1], *copies[3:]):
        copy.wait()
    low = zx_in[...]
    zx3 = jnp.concatenate([low[:, :128], low], axis=1)
    u, gz, gx, gy = [], [], [], []
    for c in range(3):
        rows = slice(128 * c, 128 * c + 128)
        most = lmul(zx3, value[rows])
        u.append(most[:288])
        gz.append(most[288:576])
        gx.append(most[576:])
        gy.append(lmul(zx3[:288], slope[rows]))
    b = b_ref[...].reshape(128, 512)
    parts = [rmul(b[:, cut], y_in[:, :384]) for cut in (slice(0, 256), slice(256, 512))]
    bq = lmul(zx3[:288], jnp.concatenate(parts, axis=1))
    b2 = bq * bq
    back = []
    for c in range(3):
        conv = u[0] * gz[c] + u[1] * gx[c] + u[2] * gy[c]
        if c != 1:
            conv = conv + b2 * u[c]
        back.append(lmul(zx_out[...], -conv))
    back = jnp.concatenate(back, axis=0)
    halves = [rmul(back[:, cut], y_out[...]) for cut in (slice(0, 384), slice(384, 768))]
    f = dss_lanes(jnp.concatenate(halves, axis=1))
    f_ref[...] = f
    s = lmul(xm_wd[...], f[128:256]) * w_y[...]
    s = s + rmul_halves(lmul(xm_w[...], f[256:]), wd_y[...])
    r_ref[:16] = s[:16]
    l_ref[:16] = s[16:]
    for k, (c, step) in enumerate(((0, 0), (1, 0), (2, 0), (0, 1))):
        r_ref[16 + 8 * k : 24 + 8 * k] = edge(f_ref, 128 * c, 15 - step)
        l_ref[16 + 8 * k : 24 + 8 * k] = edge(f_ref, 128 * c, step)


def edge(ref, base, x):
    return jnp.concatenate([ref[base + x + 16 * z : base + x + 16 * z + 1] for z in range(8)], axis=0)


def add_edge(ref, base, x, rows):
    for z in range(8):
        ref[base + x + 16 * z : base + x + 16 * z + 1] += rows[z : z + 1]


def extend(s, from_l, from_r, acc_ref):
    acc_ref[...] = s
    add_edge(acc_ref, 0, 0, from_l[8:16])
    add_edge(acc_ref, 0, 15, from_r[8:16])
    acc_ref[128:136] += from_l[:8]
    acc_ref[136:144] += from_r[:8]
    acc_ref[...] = dss_lanes(acc_ref[...])


def with_edges(full, raw_ref, base, has_l, has_r):
    edges = [edge(raw_ref, base, 0) * has_l, edge(raw_ref, base, 15) * has_r]
    return jnp.concatenate([full, *edges], axis=0)


def scaled_edges(ghost, last, w_y, ends):
    return jnp.concatenate([ghost * ends[0], last * ends[1]], axis=0) * w_y[...]


def send_faces(w_end, u, h0_ref, h12_ref, up_ref, down_ref, up_face_ref, down_face_ref, in_ref):
    for ref, own_ref, a, b, z in (
        (up_ref, up_face_ref, 6, 7, 7),
        (down_ref, down_face_ref, 0, 1, 0),
    ):
        ref[:16] = u[16 * a : 16 * a + 16]
        ref[16:32] = u[16 * b : 16 * b + 16]
        ref[32:48] = own_ref[:16] = h0_ref[16 * z : 16 * z + 16]
        own_ref[16:32] = h12_ref[16 * z : 16 * z + 16]
        half = 16 if z == 7 else 0
        ref[half : half + 16] += w_end * own_ref[16:32]
        h12 = [w_end * h12_ref[128 + 8 * s + z : 129 + 8 * s + z] for s in (0, 1)]
        rows = [u[128 + 8 * s + k : 129 + 8 * s + k] for s in (0, 1) for k in (a, b)]
        rows[z // 7] = rows[z // 7] + h12[0]
        rows[2 + z // 7] = rows[2 + z // 7] + h12[1]
        faces = [h[128 + 8 * s + z : 129 + 8 * s + z] for h in (h0_ref, h12_ref) for s in (0, 1)]
        ref[48:56] = jnp.concatenate(rows + faces, axis=0)
        own_ref[32:] = ref[48:56]
    in_ref[...] = jnp.where(is_odd(), down_ref[...], up_ref[...])


def is_odd():
    return lax.axis_index("wide") % 2 == 1


def div_kernel(ends, f_ref, ml_ref, mr_ref, xe_w, xe_wd, z_div, wd_y, w_y, *refs):
    force_ref, f_up_ref, f_down_ref, u_ref, *faces = refs[:9]
    h0_ref, h12_ref, fx_ref, sem = refs[9:]
    _, _, has_l, has_r = flags()
    ml, mr = ml_ref[...] * has_l, mr_ref[...] * has_r
    fx_ref[...] = f_ref[...]
    full = []
    for c in range(3):
        base, piece = 128 * c, slice(16 + 8 * c, 24 + 8 * c)
        add_edge(fx_ref, base, 0, ml[piece])
        add_edge(fx_ref, base, 15, mr[piece])
        full.append(with_edges(fx_ref[base : base + 128], f_ref, base, has_l, has_r))
        f_up_ref[16 * c : 16 * c + 16] = fx_ref[base + 112 : base + 128]
        f_down_ref[16 * c : 16 * c + 16] = fx_ref[base : base + 16]
    copy = pltpu.make_async_copy(fx_ref, force_ref, sem.at[0])
    copy.start()
    from_l = scaled_edges(ml[40:48], ml[16:24], w_y, ends)
    from_r = scaled_edges(mr[40:48], mr[16:24], w_y, ends)
    extend(lmul(xe_w[...], full[0]) * w_y[...], from_l, from_r, h0_ref)
    h = lmul(xe_wd[...], full[1]) * w_y[...] + rmul_halves(lmul(xe_w[...], full[2]), wd_y[...])
    extend(h, ml[:16], mr[:16], h12_ref)
    u = lmul(z_div[...], jnp.concatenate([h0_ref[...], h12_ref[...]], axis=0))
    u_ref[...] = u
    send_faces(ends[1], u, h0_ref, h12_ref, *faces)
    copy.wait()


def outer_kernel(coefs, up_ref, down_ref, in_ref, out_ref):
    odd = is_odd()
    ca = jnp.where(odd, coefs[1][0], coefs[0][0])
    cb = jnp.where(odd, coefs[1][1], coefs[0][1])
    out_ref[...] = jnp.where(odd, up_ref[...], down_ref[...])
    face, far_l, far_r = in_ref[32:48], in_ref[52:53], in_ref[53:54]
    out_ref[:16] += ca * face
    out_ref[16:32] += cb * face
    out_ref[48:52] += jnp.concatenate([ca * far_l, cb * far_l, ca * far_r, cb * far_r], axis=0)


def far_kernel(out_msg_ref, far_ref):
    has_b, has_a, _, _ = flags()
    flag = jnp.where(is_odd(), has_a, has_b)
    far_ref[:16] = out_msg_ref[32:48] * flag
    far_ref[16:] = out_msg_ref[48:56] * flag


def join(u_ref, up_ref, down_ref, in_ref, out_ref, far_ref, const):
    has_b, has_a, _, _ = flags()
    odd = is_odd()
    inner = in_ref[...]
    outer = out_ref[...] * jnp.where(odd, has_a, has_b)
    far = far_ref[...]
    rows = [
        u_ref[...],
        jnp.where(odd, inner, outer),
        jnp.where(odd, outer, inner),
        down_ref[...] * has_b,
        up_ref[...] * has_a,
        jnp.where(odd, far, 0.0),
        jnp.where(odd, 0.0, far),
    ]
    return lmul(const[...], jnp.concatenate(rows, axis=0))


def box(s, box_in, ybox_in, inv, box_out, ybox_out):
    has_b, has_a, has_l, has_r = flags()
    t = rmul(lmul(box_in[...], s), ybox_in[...]) * inv[...]
    g = rmul(lmul(box_out[...], t), ybox_out[...])
    row = lax.broadcasted_iota(jnp.int32, (128, 1), 0)
    z, x = row // 16, row % 16
    weight = 1.0 - 0.5 * jnp.where(z == 0, has_b, jnp.where(z == 7, has_a, 0.0))
    weight = weight * (1.0 - 0.5 * jnp.where(x == 0, has_l, jnp.where(x == 15, has_r, 0.0)))
    return g * weight


def first_kernel(*refs):
    join_refs, box_refs, (xm_w, xm_k, k_y, w_y) = refs[:7], refs[7:12], refs[12:16]
    s_ref, g_ref, r_ref, l_ref = refs[16:]
    s = join(*join_refs)
    s_ref[...] = s
    g = box(s, *box_refs)
    g_ref[...] = g
    q = lmul(xm_k[...], g) * w_y[...] + rmul_halves(lmul(xm_w[...], g), k_y[...])
    r_ref[:16] = q[:16]
    l_ref[:16] = q[16:]
    r_ref[16:24] = edge(g_ref, 0, 15)
    l_ref[16:24] = edge(g_ref, 0, 0)
    r_ref[24:] = edge(g_ref, 0, 14)
    l_ref[24:] = edge(g_ref, 0, 1)


def stiff_kernel(ends, g_ref, ml_ref, mr_ref, xe_w, xe_k, z_st, k_y, w_y, *refs):
    gx_ref, u_ref, *faces = refs[:7]
    p_ref, q_ref = refs[7:]
    _, _, has_l, has_r = flags()
    ml, mr = ml_ref[...] * has_l, mr_ref[...] * has_r
    gx_ref[...] = g_ref[...]
    add_edge(gx_ref, 0, 0, ml[16:24])
    add_edge(gx_ref, 0, 15, mr[16:24])
    full = with_edges(gx_ref[...], g_ref, 0, has_l, has_r)
    from_l = scaled_edges(ml[24:], ml[16:24], w_y, ends)
    from_r = scaled_edges(mr[24:], mr[16:24], w_y, ends)
    plain = lmul(xe_w[...], full)
    extend(plain * w_y[...], from_l, from_r, p_ref)
    q = lmul(xe_k[...], full) * w_y[...] + rmul_halves(plain, k_y[...])
    extend(q, ml[:16], mr[:16], q_ref)
    u = lmul(z_st[...], jnp.concatenate([p_ref[...], q_ref[...]], axis=0))
    u_ref[...] = u
    send_faces(ends[1], u, p_ref, q_ref, *faces)


def second_kernel(s_ref, *refs):
    join_refs, box_refs, (g_ref, r_ref, l_ref) = refs[:7], refs[7:12], refs[12:]
    g_ref[...] = box(s_ref[...] - join(*join_refs), *box_refs)
    r_ref[...] = edge(g_ref, 0, 15)
    l_ref[...] = edge(g_ref, 0, 0)


def last_x_kernel(g_ref, gx_ref, ml_ref, mr_ref, f_up, f_down, out_ref, in_msg_ref, out_msg_ref):
    _, _, has_l, has_r = flags()
    out_ref[...] = g_ref[...] + gx_ref[...]
    add_edge(out_ref, 0, 0, ml_ref[...] * has_l)
    add_edge(out_ref, 0, 15, mr_ref[...] * has_r)
    odd = is_odd()
    for rows, up, down in (
        (slice(0, 16), out_ref[112:], out_ref[:16]),
        (slice(16, 64), f_up[...], f_down[...]),
    ):
        in_msg_ref[rows] = jnp.where(odd, down, up)
        out_msg_ref[rows] = jnp.where(odd, up, down)


def last_z_kernel(g_ref, f_up, f_down, in_ref, out_msg_ref, _, out_ref, force_ref, face_ref, p_ref, sem):
    has_b, has_a, _, _ = flags()
    odd = is_odd()
    inner, outer = in_ref[...], out_msg_ref[...] * jnp.where(odd, has_a, has_b)
    below, above = jnp.where(odd, inner, outer), jnp.where(odd, outer, inner)
    p_ref[...] = g_ref[...]
    p_ref[:16] += below[:16]
    p_ref[112:] += above[:16]
    face_ref[:48] = f_down[...] + below[16:]
    face_ref[48:] = f_up[...] + above[16:]
    copies = [pltpu.make_async_copy(p_ref, out_ref, sem.at[6])]
    for c in range(3):
        for k, row in enumerate((128 * c, 128 * c + 112)):
            src = face_ref.at[pl.ds(48 * k + 16 * c, 16)]
            dst = force_ref.at[pl.ds(row, 16)]
            copies.append(pltpu.make_async_copy(src, dst, sem.at[2 * c + k]))
    for copy in copies:
        copy.start()
    for copy in copies:
        copy.wait()


def call(kernel, name, outs, *args, scratch=(), sems=0, vmem=16, hbm_in=(), hbm_out=(), alias=None):
    shape = lambda rows: jax.ShapeDtypeStruct((rows, 512), F32)
    spec = lambda k, far: pl.BlockSpec(memory_space=pltpu.HBM if k in far else pltpu.VMEM)
    scratch = [pltpu.VMEM((k, 512), F32) if isinstance(k, int) else k for k in scratch]
    return pl.pallas_call(
        kernel,
        out_shape=[shape(o) for o in outs],
        in_specs=[spec(k, hbm_in) for k in range(len(args))],
        out_specs=[spec(k, hbm_out) for k in range(len(outs))],
        scratch_shapes=scratch + ([pltpu.SemaphoreType.DMA((sems,))] if sems else []),
        input_output_aliases=alias or {},
        compiler_params=pltpu.CompilerParams(vmem_limit_bytes=vmem * MIB),
        name=name,
    )(*args)


def exchange_x(rightward, leftward):
    n = lax.axis_size("narrow")
    right = [(i, (i + 1) % n) for i in range(n)]
    left = [(j, i) for i, j in right]
    return lax.ppermute(rightward, "narrow", right), lax.ppermute(leftward, "narrow", left)


def other_core(x):
    n = lax.axis_size("wide")
    return lax.ppermute(x, "wide", [(i, i + 1 - 2 * (i % 2)) for i in range(n)])


def next_chip(x):
    nz, nx = lax.axis_size("wide"), lax.axis_size("narrow")
    pairs = []
    for z in range(nz):
        to = z - 1 + 2 * (z % 2)
        for k in range(nx):
            other = (to, k) if 0 <= to < nz else (z, k + 1 - 2 * (k % 2))
            pairs.append((z * nx + k, other[0] * nx + other[1]))
    return lax.ppermute(x, ("wide", "narrow"), pairs)


def meet(up, down, inner_msg, coefs, name):
    inner = other_core(inner_msg)
    coefs = [[float(t) for t in row] for row in coefs]
    (msg,) = call(functools.partial(outer_kernel, coefs), name, (56,), up, down, inner)
    outer = next_chip(msg)
    (far,) = call(far_kernel, name + "_far", (24,), outer)
    return inner, outer, other_core(far)


def shards(velocity, bfield):
    tables = constants()
    picks = tables.pop("pick_div"), tables.pop("pick_st")
    c = {name: jnp.asarray(value) for name, value in tables.items()}
    consts = lambda *names: [c[name] for name in names]
    weights = tables_1d()[4]
    ends = float(weights[1]), float(weights[0])
    force_args = (
        velocity,
        bfield,
        *consts("y_in", "zx_in", "zx_out", "y_out", "xm_w", "xm_wd", "wd_y", "w_y"),
    )
    force_args = [pltpu.with_memory_space_constraint(x, pltpu.HBM) for x in force_args]
    f, right, left = call(
        force_kernel,
        "force",
        (384, 48, 48),
        *force_args,
        scratch=[pltpu.VMEM(a.shape, a.dtype) for a in force_args],
        sems=10,
        vmem=32,
        hbm_in=range(10),
    )
    from_l, from_r = exchange_x(right, left)
    force, f_up, f_down, u, up, down, up_face, down_face, inner = call(
        functools.partial(div_kernel, ends),
        "div",
        (384, 48, 48, 144, 56, 56, 40, 40, 56),
        f,
        from_l,
        from_r,
        *consts("xe_w", "xe_wd", "z_div", "wd_y", "w_y"),
        scratch=(144, 144, 384),
        sems=1,
        hbm_out=(0,),
    )
    inner, outer, far = meet(up, down, inner, picks[0], "div_out")
    box_consts = consts("box_in", "ybox_in", "inv", "box_out", "ybox_out")
    s, g, right, left = call(
        first_kernel,
        "first_pass",
        (192, 128, 32, 32),
        u,
        up_face,
        down_face,
        inner,
        outer,
        far,
        c["join_div"],
        *box_consts,
        *consts("xm_w", "xm_k", "k_y", "w_y"),
    )
    from_l, from_r = exchange_x(right, left)
    gx, u, up, down, up_face, down_face, inner = call(
        functools.partial(stiff_kernel, ends),
        "stiff",
        (128, 144, 56, 56, 40, 40, 56),
        g,
        from_l,
        from_r,
        *consts("xe_w", "xe_k", "z_st", "k_y", "w_y"),
        scratch=(144, 144),
    )
    inner, outer, far = meet(up, down, inner, picks[1], "stiff_out")
    g, right, left = call(
        second_kernel,
        "second_pass",
        (128, 8, 8),
        s,
        u,
        up_face,
        down_face,
        inner,
        outer,
        far,
        c["join_st"],
        *box_consts,
    )
    from_l, from_r = exchange_x(right, left)
    total, inner, outer = call(
        last_x_kernel, "last_x", (128, 64, 64), g, gx, from_l, from_r, f_up, f_down
    )
    outer, inner = next_chip(outer), other_core(inner)
    pressure, force = call(
        last_z_kernel,
        "last_z",
        (128, 384),
        total,
        f_up,
        f_down,
        inner,
        outer,
        force,
        scratch=(96, 128),
        sems=7,
        hbm_in=(5,),
        hbm_out=(0, 1),
        alias={5: 1},
    )
    return force.reshape(3, 8, 16, 512), pressure.reshape(8, 16, 512)


def solution(mesh):
    placed = (P(None, "wide", "narrow", None), P("wide", "narrow", None))
    return jax.shard_map(
        shards, mesh=mesh, in_specs=placed, out_specs=placed, check_vma=False
    )
```

```python
import functools

import jax
import jax.numpy as jnp
import ml_dtypes
import numpy as np
from jax import lax
from jax.experimental import pallas as pl
from jax.experimental.pallas import tpu as pltpu
from jax.sharding import PartitionSpec as P

F32 = jnp.float32
BF16 = jnp.bfloat16
MIB = 2**20


def legendre_pair(degree, points):
    below, current = np.ones(points.shape), points * 1.0
    for step in range(2, degree + 1):
        below, current = current, ((2 * step - 1) * points * current - (step - 1) * below) / step
    return current, below


def tables_1d():
    points = np.cos(np.pi * np.arange(8) / 7)
    for _ in range(60):
        top, below = legendre_pair(7, points)
        points = points - (points * top - below) / (8 * top)
    points = np.sort(points)
    top, below = legendre_pair(7, points)
    w = 2.0 / (56 * top**2)
    spacing = points[:, None] - points[None, :] + np.eye(8)
    deriv = top[:, None] / (top[None, :] * spacing) * (1.0 - np.eye(8))
    deriv[0, 0], deriv[-1, -1] = -14.0, 14.0
    gauss = np.cos(np.pi * (np.arange(12) + 0.75) / 12.5)
    for _ in range(60):
        top, below = legendre_pair(12, gauss)
        gauss = gauss - top / (12 * (gauss * top - below) / (gauss**2 - 1.0))
    top, below = legendre_pair(12, gauss)
    slope = 12 * (gauss * top - below) / (gauss**2 - 1.0)
    v = 2.0 / ((1.0 - gauss**2) * slope**2)
    interp = np.ones((12, 8))
    for col in range(8):
        for other in range(8):
            if other != col:
                interp[:, col] *= (gauss - points[other]) / (points[col] - points[other])
    stiff = deriv.T @ (w[:, None] * deriv)
    wide_stiff, wide_mass = np.zeros((22, 22)), np.zeros(22)
    for el in range(3):
        r = 7 * el
        wide_stiff[r : r + 8, r : r + 8] += stiff
        wide_mass[r : r + 8] += w
    scale = 1.0 / np.sqrt(wide_mass[6:16])
    lam, vec = np.linalg.eigh(scale[:, None] * wide_stiff[6:16, 6:16] * scale[None, :])
    return interp, interp @ deriv, deriv, stiff, w, scale[:, None] * vec, lam, v


def hi_lo(m):
    hi = m.astype(ml_dtypes.bfloat16)
    return hi, (m - hi.astype(np.float64)).astype(ml_dtypes.bfloat16)


def left_const(m):
    hi, lo = hi_lo(m)
    return np.concatenate([hi, hi, lo], axis=1)


def right_const(m):
    return np.concatenate(hi_lo(m), axis=0)


def block_diag(m, count):
    return np.kron(np.eye(count), m)


def own(z, x):
    return 16 * z + x


def local_rows(terms, xs):
    out = np.zeros((8 * len(xs), 128))
    for k, x in enumerate(xs):
        el, j = divmod(x, 8)
        for z in range(8):
            for zm, xm in terms:
                for z2 in range(8):
                    for j2 in range(8):
                        out[8 * k + z, own(z2, 8 * el + j2)] += zm[z, z2] * xm[j, j2]
    return out


def extended_rows(terms):
    local = local_rows(terms, range(16)).reshape(16, 8, 128)
    out = np.zeros((144, 144))
    for x in range(16):
        for z in range(8):
            out[own(z, x), :128] = local[x, z]
            if x in (7, 8):
                out[own(z, x), :128] += local[15 - x, z]
    for z in range(8):
        for zm, xm in terms:
            for z2 in range(8):
                out[own(z, 0), 128 + z2] += zm[z, z2] * xm[7, 7]
                out[128 + z, 128 + z2] += zm[z, z2] * xm[6, 7]
                out[own(z, 15), 136 + z2] += zm[z, z2] * xm[0, 0]
                out[136 + z, 136 + z2] += zm[z, z2] * xm[1, 0]
    return out


def z_rows(mats):
    blocks = [np.zeros((144, 144)) for _ in mats]
    for out, m in zip(blocks, mats):
        out[:128, :128] = np.kron(m, np.eye(16))
        out[128:136, 128:136] = m
        out[136:, 136:] = m
    return np.concatenate(blocks, axis=1)


def join_rows(zm, w):
    out = np.zeros((192, 384))
    below, above, down, up, far_b, far_a = 144, 200, 256, 296, 336, 360
    for t in range(18):
        side = t - 16
        own_row = lambda z: own(z, t) if t < 16 else 128 + 8 * side + z
        layer = lambda base, k: base + 16 * k + t if t < 16 else base + 48 + 2 * side + k
        msg_face = lambda base: base + 32 + t if t < 16 else base + 52 + side
        face = lambda base, k: base + 16 * k + t if t < 16 else base + 36 + 2 * k + side
        far = lambda base: base + t if t < 16 else base + 20 + side
        b7, b6, a0, a1 = np.zeros((4, 384))
        b7[layer(below, 1)] = b6[layer(below, 0)] = 1.0
        b7[face(down, 0)], b7[face(down, 1)], b7[far(far_b)] = zm[7, 7], w[7], zm[7, 0]
        b6[face(down, 0)], b6[far(far_b)] = zm[6, 7], zm[6, 0]
        a0[layer(above, 0)] = a1[layer(above, 1)] = 1.0
        a0[face(up, 0)], a0[face(up, 1)], a0[far(far_a)] = zm[0, 0], w[0], zm[0, 7]
        a1[face(up, 0)], a1[far(far_a)] = zm[1, 0], zm[1, 7]
        for z in range(8):
            row = out[own_row(z)]
            row[own_row(z)] += 1.0
            row[msg_face(below)] += zm[z, 0]
            row[msg_face(above)] += zm[z, 7]
        out[own_row(0)] += b7
        out[own_row(7)] += a0
        out[144 + t], out[168 + t] = b6, a1
    return out


def box_rows(vec):
    nodes = np.zeros((10, 2, 10, 192))
    for zk in range(10):
        for el in range(2):
            for xk in range(10):
                x = 8 * el + (-2 if xk == 0 else 9 if xk == 9 else xk - 1)
                side = -1 if x < 0 else 1 if x > 15 else 0
                if 0 < zk < 9:
                    row = {0: own(zk - 1, x), -1: 128 + zk - 1, 1: 136 + zk - 1}[side]
                else:
                    row = (144 if zk == 0 else 168) + {0: x, -1: 16, 1: 17}[side]
                nodes[zk, el, xk, row] = 1.0
    into = np.einsum("zi,xj,zexr->iejr", vec, vec, nodes).reshape(200, 192)
    back = np.zeros((8, 16, 10, 2, 10))
    inner = vec[1:9]
    for z in range(8):
        for x in range(16):
            el, j = divmod(x, 8)
            block = inner[z][:, None] * inner[j][None, :]
            if x in (7, 8):
                back[z, x, :, el] += 0.5 * block
                back[z, x, :, 1 - el] += 0.5 * inner[z][:, None] * inner[7 - j][None, :]
            else:
                back[z, x, :, el] += block
    back = back.reshape(128, 200)
    return np.pad(into, ((0, 8), (0, 0))), np.pad(back, ((0, 0), (0, 8)))


def box_lanes(vec, count):
    into = np.zeros((8 * count, 10 * count))
    back = np.zeros((10 * count, 8 * count))
    for e in range(count):
        spots = [8 * e - 2] + list(range(8 * e, 8 * e + 8)) + [8 * e + 9]
        for k, y in enumerate(spots):
            if 0 <= y < 8 * count:
                into[y, 10 * e : 10 * e + 10] += vec[k]
        for j in range(8):
            col = vec[j + 1]
            y = 8 * e + j
            if j == 0 and e > 0:
                back[10 * e : 10 * e + 10, [y - 1, y]] += 0.5 * col[:, None]
            elif j == 7 and e < count - 1:
                back[10 * e : 10 * e + 10, [y, y + 1]] += 0.5 * col[:, None]
            else:
                back[10 * e : 10 * e + 10, y] += col
    return into, back


def face_coefs(zm):
    return np.array([[zm[0, 7], zm[1, 7]], [zm[6, 0], zm[7, 0]]])


def constants():
    interp, slopes, deriv, stiff, w, vec, lam, v = tables_1d()
    c = {}
    c["y_in"] = right_const(
        np.concatenate([block_diag(interp.T, 32), block_diag(slopes.T, 32)], axis=1)
    )
    c["zx_in"] = left_const(
        np.concatenate(
            [np.kron(interp, interp), np.kron(slopes, interp), np.kron(interp, slopes)], axis=0
        )
    )
    test = v[:, None] * interp
    c["zx_out"] = left_const(np.kron(test.T, test.T))
    c["y_out"] = right_const(block_diag(test, 32))
    one, wm, wd = np.eye(8), np.diag(w), w[:, None] * deriv
    sides = (14, 15, 1, 0)
    for name, xm in (("w", wm), ("wd", wd), ("k", stiff)):
        c["xm_" + name] = left_const(local_rows([(one, xm)], sides))
        c["xe_" + name] = left_const(extended_rows([(one, xm)]))
    c["z_div"], c["z_st"] = left_const(z_rows((wd, wm))), left_const(z_rows((stiff, wm)))
    c["pick_div"], c["pick_st"] = face_coefs(wd), face_coefs(stiff)
    c["wd_y"] = right_const(block_diag(wd.T, 32))
    c["k_y"] = right_const(block_diag(stiff.T, 32))
    c["w_y"] = np.tile(w, 64)[None].astype(np.float32)
    into, back = box_rows(vec)
    c["box_div"] = left_const(into @ join_rows(wd, w))
    c["box_st"] = left_const(into @ join_rows(stiff, w))
    c["box_out"] = left_const(back)
    into, back = box_lanes(vec, 64)
    c["ybox_in"], c["ybox_out"] = right_const(into), right_const(back)
    inv = 1.0 / (lam[:, None, None, None] + lam[None, None, :, None] + lam)
    inv = np.broadcast_to(inv[:, :, :, None, :], (10, 1, 10, 64, 10))
    inv = np.broadcast_to(inv, (10, 2, 10, 64, 10)).reshape(200, 640)
    c["inv"] = np.pad(inv, ((0, 8), (0, 0))).astype(np.float32)
    return c


def split(x):
    hi = x.astype(BF16)
    return hi, (x - hi.astype(F32)).astype(BF16)


def rmul(x, const):
    hi, lo = split(x)
    depth = const.shape[0] // 2
    const = jnp.concatenate([const[:depth], const], axis=0)
    return jnp.dot(jnp.concatenate([hi, lo, hi], axis=1), const, preferred_element_type=F32)


def lmul(const, x):
    hi, lo = split(x)
    return jnp.dot(const, jnp.concatenate([hi, lo, hi], axis=0), preferred_element_type=F32)


def rmul_halves(x, const):
    return jnp.concatenate([rmul(x[:, :256], const), rmul(x[:, 256:], const)], axis=1)


def dss_lanes(x):
    lane = lax.broadcasted_iota(jnp.int32, x.shape, 1)
    n = x.shape[1]
    up = jnp.where((lane % 8 == 7) & (lane < n - 1), pltpu.roll(x, n - 1, 1), 0.0)
    down = jnp.where((lane % 8 == 0) & (lane > 0), pltpu.roll(x, 1, 1), 0.0)
    return x + up + down


def flags():
    z, x = lax.axis_index("wide"), lax.axis_index("narrow")
    nz, nx = lax.axis_size("wide"), lax.axis_size("narrow")
    as_flag = lambda t: t.astype(F32)
    return as_flag(z > 0), as_flag(z < nz - 1), as_flag(x > 0), as_flag(x < nx - 1)


def force_kernel(*refs):
    sources, (f_ref, r_ref, l_ref), held, sem = refs[:10], refs[10:13], refs[13:23], refs[23]
    v_ref, b_ref, y_in, zx_in, zx_out, y_out, xm_w, xm_wd, wd_y, w_y = held
    copies = [pltpu.make_async_copy(a, b, sem.at[k]) for k, (a, b) in enumerate(zip(sources, held))]
    for k in (2, 0, 1, 3, 4, 5, 6, 7, 8, 9):
        copies[k].start()
    copies[2].wait()
    copies[0].wait()
    v = jnp.concatenate([v_ref[:, :, k : k + 8].reshape(192, 512) for k in (0, 8)], axis=0)
    parts = [rmul(v[:, cut], y_in[...]) for cut in (slice(0, 256), slice(256, 512))]
    value = jnp.concatenate([p[:, :384] for p in parts], axis=1)
    slope = jnp.concatenate([p[:, 384:] for p in parts], axis=1)
    for copy in (copies[1], *copies[3:]):
        copy.wait()
    b = jnp.concatenate([b_ref[:, k : k + 8].reshape(64, 512) for k in (0, 8)], axis=0)
    parts = [rmul(b[:, cut], y_in[:, :384]) for cut in (slice(0, 256), slice(256, 512))]
    field = jnp.concatenate(parts, axis=1)
    back = []
    for el in range(2):
        u, gz, gx, gy = [], [], [], []
        for c in range(3):
            rows = slice(192 * el + 64 * c, 192 * el + 64 * c + 64)
            most = lmul(zx_in[...], value[rows])
            u.append(most[:144])
            gz.append(most[144:288])
            gx.append(most[288:])
            gy.append(lmul(zx_in[:144], slope[rows]))
        bq = lmul(zx_in[:144], field[64 * el : 64 * el + 64])
        b2 = bq * bq
        for c in range(3):
            conv = u[0] * gz[c] + u[1] * gx[c] + u[2] * gy[c]
            if c != 1:
                conv = conv + b2 * u[c]
            back.append(lmul(zx_out[...], -conv))
    back = jnp.concatenate(back, axis=0)
    halves = [rmul(back[:, cut], y_out[...]) for cut in (slice(0, 384), slice(384, 768))]
    f = dss_lanes(jnp.concatenate(halves, axis=1))
    first, second = f[:192], f[192:]
    node = lax.broadcasted_iota(jnp.int32, (192, 512), 0) % 8
    both = (
        first + jnp.where(node == 7, pltpu.roll(second, 7, 0), 0.0),
        second + jnp.where(node == 0, pltpu.roll(first, 185, 0), 0.0),
    )
    for k in range(24):
        for el in range(2):
            f_ref[16 * k + 8 * el : 16 * k + 8 * el + 8] = both[el][8 * k : 8 * k + 8]
    f = f_ref[...]
    s = lmul(xm_wd[...], f[128:256]) * w_y[...]
    s = s + rmul_halves(lmul(xm_w[...], f[256:]), wd_y[...])
    r_ref[:16] = s[:16]
    l_ref[:16] = s[16:]
    for k, (c, step) in enumerate(((0, 0), (1, 0), (2, 0), (0, 1))):
        r_ref[16 + 8 * k : 24 + 8 * k] = edge(f_ref, 128 * c, 15 - step)
        l_ref[16 + 8 * k : 24 + 8 * k] = edge(f_ref, 128 * c, step)


def edge(ref, base, x):
    return jnp.concatenate([ref[base + x + 16 * z : base + x + 16 * z + 1] for z in range(8)], axis=0)


def add_edge(ref, base, x, rows):
    for z in range(8):
        ref[base + x + 16 * z : base + x + 16 * z + 1] += rows[z : z + 1]


def extend(s, from_l, from_r, acc_ref):
    acc_ref[...] = s
    add_edge(acc_ref, 0, 0, from_l[8:16])
    add_edge(acc_ref, 0, 15, from_r[8:16])
    acc_ref[128:136] += from_l[:8]
    acc_ref[136:144] += from_r[:8]
    acc_ref[...] = dss_lanes(acc_ref[...])


def with_edges(full, raw_ref, base, has_l, has_r):
    edges = [edge(raw_ref, base, 0) * has_l, edge(raw_ref, base, 15) * has_r]
    return jnp.concatenate([full, *edges], axis=0)


def scaled_edges(ghost, last, w_y, ends):
    return jnp.concatenate([ghost * ends[0], last * ends[1]], axis=0) * w_y[...]


def send_faces(w_end, u, h0_ref, h12_ref, up_ref, down_ref, up_face_ref, down_face_ref, in_ref):
    for ref, own_ref, a, b, z in (
        (up_ref, up_face_ref, 6, 7, 7),
        (down_ref, down_face_ref, 0, 1, 0),
    ):
        ref[:16] = u[16 * a : 16 * a + 16]
        ref[16:32] = u[16 * b : 16 * b + 16]
        ref[32:48] = own_ref[:16] = h0_ref[16 * z : 16 * z + 16]
        own_ref[16:32] = h12_ref[16 * z : 16 * z + 16]
        half = 16 if z == 7 else 0
        ref[half : half + 16] += w_end * own_ref[16:32]
        h12 = [w_end * h12_ref[128 + 8 * s + z : 129 + 8 * s + z] for s in (0, 1)]
        rows = [u[128 + 8 * s + k : 129 + 8 * s + k] for s in (0, 1) for k in (a, b)]
        rows[z // 7] = rows[z // 7] + h12[0]
        rows[2 + z // 7] = rows[2 + z // 7] + h12[1]
        faces = [h[128 + 8 * s + z : 129 + 8 * s + z] for h in (h0_ref, h12_ref) for s in (0, 1)]
        ref[48:56] = jnp.concatenate(rows + faces, axis=0)
        own_ref[32:] = ref[48:56]
    in_ref[...] = jnp.where(is_odd(), down_ref[...], up_ref[...])


def is_odd():
    return lax.axis_index("wide") % 2 == 1


def div_kernel(ends, f_ref, ml_ref, mr_ref, xe_w, xe_wd, z_div, wd_y, w_y, *refs):
    force_ref, f_up_ref, f_down_ref, u_ref, *faces = refs[:9]
    h0_ref, h12_ref, fx_ref, sem = refs[9:]
    _, _, has_l, has_r = flags()
    ml, mr = ml_ref[...] * has_l, mr_ref[...] * has_r
    fx_ref[...] = f_ref[...]
    full = []
    for c in range(3):
        base, piece = 128 * c, slice(16 + 8 * c, 24 + 8 * c)
        add_edge(fx_ref, base, 0, ml[piece])
        add_edge(fx_ref, base, 15, mr[piece])
        full.append(with_edges(fx_ref[base : base + 128], f_ref, base, has_l, has_r))
        f_up_ref[16 * c : 16 * c + 16] = fx_ref[base + 112 : base + 128]
        f_down_ref[16 * c : 16 * c + 16] = fx_ref[base : base + 16]
    copy = pltpu.make_async_copy(fx_ref, force_ref, sem.at[0])
    copy.start()
    from_l = scaled_edges(ml[40:48], ml[16:24], w_y, ends)
    from_r = scaled_edges(mr[40:48], mr[16:24], w_y, ends)
    extend(lmul(xe_w[...], full[0]) * w_y[...], from_l, from_r, h0_ref)
    h = lmul(xe_wd[...], full[1]) * w_y[...] + rmul_halves(lmul(xe_w[...], full[2]), wd_y[...])
    extend(h, ml[:16], mr[:16], h12_ref)
    u = lmul(z_div[...], jnp.concatenate([h0_ref[...], h12_ref[...]], axis=0))
    u_ref[...] = u
    send_faces(ends[1], u, h0_ref, h12_ref, *faces)
    copy.wait()


def outer_kernel(coefs, up_ref, down_ref, in_ref, out_ref):
    odd = is_odd()
    ca = jnp.where(odd, coefs[1][0], coefs[0][0])
    cb = jnp.where(odd, coefs[1][1], coefs[0][1])
    out_ref[...] = jnp.where(odd, up_ref[...], down_ref[...])
    face, far_l, far_r = in_ref[32:48], in_ref[52:53], in_ref[53:54]
    out_ref[:16] += ca * face
    out_ref[16:32] += cb * face
    out_ref[48:52] += jnp.concatenate([ca * far_l, cb * far_l, ca * far_r, cb * far_r], axis=0)


def far_kernel(out_msg_ref, far_ref):
    has_b, has_a, _, _ = flags()
    flag = jnp.where(is_odd(), has_a, has_b)
    far_ref[:16] = out_msg_ref[32:48] * flag
    far_ref[16:] = out_msg_ref[48:56] * flag


def join(u_ref, up_ref, down_ref, in_ref, out_ref, far_ref, const):
    has_b, has_a, _, _ = flags()
    odd = is_odd()
    inner = in_ref[...]
    outer = out_ref[...] * jnp.where(odd, has_a, has_b)
    far = far_ref[...]
    rows = [
        u_ref[...],
        jnp.where(odd, inner, outer),
        jnp.where(odd, outer, inner),
        down_ref[...] * has_b,
        up_ref[...] * has_a,
        jnp.where(odd, far, 0.0),
        jnp.where(odd, 0.0, far),
    ]
    return lmul(const[...], jnp.concatenate(rows, axis=0))


def box(t, ybox_in, inv, box_out, ybox_out):
    has_b, has_a, has_l, has_r = flags()
    t = rmul(t, ybox_in[...]) * inv[...]
    g = rmul(lmul(box_out[...], t), ybox_out[...])
    row = lax.broadcasted_iota(jnp.int32, (128, 1), 0)
    z, x = row // 16, row % 16
    weight = 1.0 - 0.5 * jnp.where(z == 0, has_b, jnp.where(z == 7, has_a, 0.0))
    weight = weight * (1.0 - 0.5 * jnp.where(x == 0, has_l, jnp.where(x == 15, has_r, 0.0)))
    return g * weight


def first_kernel(*refs):
    join_refs, box_refs, (xm_w, xm_k, k_y, w_y) = refs[:7], refs[7:11], refs[11:15]
    t_ref, g_ref, r_ref, l_ref = refs[15:]
    t = join(*join_refs)
    t_ref[...] = t
    g = box(t, *box_refs)
    g_ref[...] = g
    q = lmul(xm_k[...], g) * w_y[...] + rmul_halves(lmul(xm_w[...], g), k_y[...])
    r_ref[:16] = q[:16]
    l_ref[:16] = q[16:]
    r_ref[16:24] = edge(g_ref, 0, 15)
    l_ref[16:24] = edge(g_ref, 0, 0)
    r_ref[24:] = edge(g_ref, 0, 14)
    l_ref[24:] = edge(g_ref, 0, 1)


def stiff_kernel(ends, g_ref, ml_ref, mr_ref, xe_w, xe_k, z_st, k_y, w_y, *refs):
    gx_ref, u_ref, *faces = refs[:7]
    p_ref, q_ref = refs[7:]
    _, _, has_l, has_r = flags()
    ml, mr = ml_ref[...] * has_l, mr_ref[...] * has_r
    gx_ref[...] = g_ref[...]
    add_edge(gx_ref, 0, 0, ml[16:24])
    add_edge(gx_ref, 0, 15, mr[16:24])
    full = with_edges(gx_ref[...], g_ref, 0, has_l, has_r)
    from_l = scaled_edges(ml[24:], ml[16:24], w_y, ends)
    from_r = scaled_edges(mr[24:], mr[16:24], w_y, ends)
    plain = lmul(xe_w[...], full)
    extend(plain * w_y[...], from_l, from_r, p_ref)
    q = lmul(xe_k[...], full) * w_y[...] + rmul_halves(plain, k_y[...])
    extend(q, ml[:16], mr[:16], q_ref)
    u = lmul(z_st[...], jnp.concatenate([p_ref[...], q_ref[...]], axis=0))
    u_ref[...] = u
    send_faces(ends[1], u, p_ref, q_ref, *faces)


def second_kernel(t_ref, *refs):
    join_refs, box_refs, (g_ref, r_ref, l_ref) = refs[:7], refs[7:11], refs[11:]
    g_ref[...] = box(t_ref[...] - join(*join_refs), *box_refs)
    r_ref[...] = edge(g_ref, 0, 15)
    l_ref[...] = edge(g_ref, 0, 0)


def last_x_kernel(g_ref, gx_ref, ml_ref, mr_ref, f_up, f_down, out_ref, in_msg_ref, out_msg_ref):
    _, _, has_l, has_r = flags()
    out_ref[...] = g_ref[...] + gx_ref[...]
    add_edge(out_ref, 0, 0, ml_ref[...] * has_l)
    add_edge(out_ref, 0, 15, mr_ref[...] * has_r)
    odd = is_odd()
    for rows, up, down in (
        (slice(0, 16), out_ref[112:], out_ref[:16]),
        (slice(16, 64), f_up[...], f_down[...]),
    ):
        in_msg_ref[rows] = jnp.where(odd, down, up)
        out_msg_ref[rows] = jnp.where(odd, up, down)


def last_z_kernel(g_ref, f_up, f_down, in_ref, out_msg_ref, _, out_ref, force_ref, face_ref, p_ref, sem):
    has_b, has_a, _, _ = flags()
    odd = is_odd()
    inner, outer = in_ref[...], out_msg_ref[...] * jnp.where(odd, has_a, has_b)
    below, above = jnp.where(odd, inner, outer), jnp.where(odd, outer, inner)
    p_ref[...] = g_ref[...]
    p_ref[:16] += below[:16]
    p_ref[112:] += above[:16]
    face_ref[:48] = f_down[...] + below[16:]
    face_ref[48:] = f_up[...] + above[16:]
    copies = [pltpu.make_async_copy(p_ref, out_ref, sem.at[6])]
    for c in range(3):
        for k, row in enumerate((128 * c, 128 * c + 112)):
            src = face_ref.at[pl.ds(48 * k + 16 * c, 16)]
            dst = force_ref.at[pl.ds(row, 16)]
            copies.append(pltpu.make_async_copy(src, dst, sem.at[2 * c + k]))
    for copy in copies:
        copy.start()
    for copy in copies:
        copy.wait()


def call(kernel, name, outs, *args, scratch=(), sems=0, vmem=16, hbm_in=(), hbm_out=(), alias=None):
    shape = lambda rows: jax.ShapeDtypeStruct((rows, 512), F32)
    spec = lambda k, far: pl.BlockSpec(memory_space=pltpu.HBM if k in far else pltpu.VMEM)
    scratch = [pltpu.VMEM((k, 512), F32) if isinstance(k, int) else k for k in scratch]
    return pl.pallas_call(
        kernel,
        out_shape=[shape(o) for o in outs],
        in_specs=[spec(k, hbm_in) for k in range(len(args))],
        out_specs=[spec(k, hbm_out) for k in range(len(outs))],
        scratch_shapes=scratch + ([pltpu.SemaphoreType.DMA((sems,))] if sems else []),
        input_output_aliases=alias or {},
        compiler_params=pltpu.CompilerParams(vmem_limit_bytes=vmem * MIB),
        name=name,
    )(*args)


def exchange_x(rightward, leftward):
    n = lax.axis_size("narrow")
    right = [(i, (i + 1) % n) for i in range(n)]
    left = [(j, i) for i, j in right]
    return lax.ppermute(rightward, "narrow", right), lax.ppermute(leftward, "narrow", left)


def other_core(x):
    n = lax.axis_size("wide")
    return lax.ppermute(x, "wide", [(i, i + 1 - 2 * (i % 2)) for i in range(n)])


def next_chip(x):
    nz, nx = lax.axis_size("wide"), lax.axis_size("narrow")
    pairs = []
    for z in range(nz):
        to = z - 1 + 2 * (z % 2)
        for k in range(nx):
            other = (to, k) if 0 <= to < nz else (z, k + 1 - 2 * (k % 2))
            pairs.append((z * nx + k, other[0] * nx + other[1]))
    return lax.ppermute(x, ("wide", "narrow"), pairs)


def meet(up, down, inner_msg, coefs, name):
    inner = other_core(inner_msg)
    coefs = [[float(t) for t in row] for row in coefs]
    (msg,) = call(functools.partial(outer_kernel, coefs), name, (56,), up, down, inner)
    outer = next_chip(msg)
    (far,) = call(far_kernel, name + "_far", (24,), outer)
    return inner, outer, other_core(far)


def shards(velocity, bfield):
    tables = constants()
    picks = tables.pop("pick_div"), tables.pop("pick_st")
    c = {name: jnp.asarray(value) for name, value in tables.items()}
    consts = lambda *names: [c[name] for name in names]
    weights = tables_1d()[4]
    ends = float(weights[1]), float(weights[0])
    force_args = (
        velocity,
        bfield,
        *consts("y_in", "zx_in", "zx_out", "y_out", "xm_w", "xm_wd", "wd_y", "w_y"),
    )
    force_args = [pltpu.with_memory_space_constraint(x, pltpu.HBM) for x in force_args]
    f, right, left = call(
        force_kernel,
        "force",
        (384, 48, 48),
        *force_args,
        scratch=[pltpu.VMEM(a.shape, a.dtype) for a in force_args],
        sems=10,
        vmem=32,
        hbm_in=range(10),
    )
    from_l, from_r = exchange_x(right, left)
    force, f_up, f_down, u, up, down, up_face, down_face, inner = call(
        functools.partial(div_kernel, ends),
        "div",
        (384, 48, 48, 144, 56, 56, 40, 40, 56),
        f,
        from_l,
        from_r,
        *consts("xe_w", "xe_wd", "z_div", "wd_y", "w_y"),
        scratch=(144, 144, 384),
        sems=1,
        hbm_out=(0,),
    )
    inner, outer, far = meet(up, down, inner, picks[0], "div_out")
    box_consts = consts("ybox_in", "inv", "box_out", "ybox_out")
    spectral, g, right, left = call(
        first_kernel,
        "first_pass",
        (208, 128, 32, 32),
        u,
        up_face,
        down_face,
        inner,
        outer,
        far,
        c["box_div"],
        *box_consts,
        *consts("xm_w", "xm_k", "k_y", "w_y"),
    )
    from_l, from_r = exchange_x(right, left)
    gx, u, up, down, up_face, down_face, inner = call(
        functools.partial(stiff_kernel, ends),
        "stiff",
        (128, 144, 56, 56, 40, 40, 56),
        g,
        from_l,
        from_r,
        *consts("xe_w", "xe_k", "z_st", "k_y", "w_y"),
        scratch=(144, 144),
    )
    inner, outer, far = meet(up, down, inner, picks[1], "stiff_out")
    g, right, left = call(
        second_kernel,
        "second_pass",
        (128, 8, 8),
        spectral,
        u,
        up_face,
        down_face,
        inner,
        outer,
        far,
        c["box_st"],
        *box_consts,
    )
    from_l, from_r = exchange_x(right, left)
    total, inner, outer = call(
        last_x_kernel, "last_x", (128, 64, 64), g, gx, from_l, from_r, f_up, f_down
    )
    outer, inner = next_chip(outer), other_core(inner)
    pressure, force = call(
        last_z_kernel,
        "last_z",
        (128, 384),
        total,
        f_up,
        f_down,
        inner,
        outer,
        force,
        scratch=(96, 128),
        sems=7,
        hbm_in=(5,),
        hbm_out=(0, 1),
        alias={5: 1},
    )
    return force.reshape(3, 8, 16, 512), pressure.reshape(8, 16, 512)


def solution(mesh):
    placed = (P(None, "wide", "narrow", None), P("wide", "narrow", None))
    return jax.shard_map(
        shards, mesh=mesh, in_specs=placed, out_specs=placed, check_vma=False
    )
```

```python
import functools

import jax
import jax.numpy as jnp
import ml_dtypes
import numpy as np
from jax import lax
from jax.experimental import pallas as pl
from jax.experimental.pallas import tpu as pltpu
from jax.sharding import PartitionSpec as P

F32 = jnp.float32
BF16 = jnp.bfloat16
MIB = 2**20


def legendre_pair(degree, points):
    below, current = np.ones(points.shape), points * 1.0
    for step in range(2, degree + 1):
        below, current = current, ((2 * step - 1) * points * current - (step - 1) * below) / step
    return current, below


def tables_1d():
    points = np.cos(np.pi * np.arange(8) / 7)
    for _ in range(60):
        top, below = legendre_pair(7, points)
        points = points - (points * top - below) / (8 * top)
    points = np.sort(points)
    top, below = legendre_pair(7, points)
    w = 2.0 / (56 * top**2)
    spacing = points[:, None] - points[None, :] + np.eye(8)
    deriv = top[:, None] / (top[None, :] * spacing) * (1.0 - np.eye(8))
    deriv[0, 0], deriv[-1, -1] = -14.0, 14.0
    gauss = np.cos(np.pi * (np.arange(12) + 0.75) / 12.5)
    for _ in range(60):
        top, below = legendre_pair(12, gauss)
        gauss = gauss - top / (12 * (gauss * top - below) / (gauss**2 - 1.0))
    top, below = legendre_pair(12, gauss)
    slope = 12 * (gauss * top - below) / (gauss**2 - 1.0)
    v = 2.0 / ((1.0 - gauss**2) * slope**2)
    interp = np.ones((12, 8))
    for col in range(8):
        for other in range(8):
            if other != col:
                interp[:, col] *= (gauss - points[other]) / (points[col] - points[other])
    stiff = deriv.T @ (w[:, None] * deriv)
    wide_stiff, wide_mass = np.zeros((22, 22)), np.zeros(22)
    for el in range(3):
        r = 7 * el
        wide_stiff[r : r + 8, r : r + 8] += stiff
        wide_mass[r : r + 8] += w
    scale = 1.0 / np.sqrt(wide_mass[6:16])
    lam, vec = np.linalg.eigh(scale[:, None] * wide_stiff[6:16, 6:16] * scale[None, :])
    return interp, interp @ deriv, deriv, stiff, w, scale[:, None] * vec, lam, v


def hi_lo(m):
    hi = m.astype(ml_dtypes.bfloat16)
    return hi, (m - hi.astype(np.float64)).astype(ml_dtypes.bfloat16)


def left_const(m):
    hi, lo = hi_lo(m)
    return np.concatenate([hi, hi, lo], axis=1)


def right_const(m):
    return np.concatenate(hi_lo(m), axis=0)


def block_diag(m, count):
    return np.kron(np.eye(count), m)


def own(z, x):
    return 16 * z + x


def local_rows(terms, xs):
    out = np.zeros((8 * len(xs), 128))
    for k, x in enumerate(xs):
        el, j = divmod(x, 8)
        for z in range(8):
            for zm, xm in terms:
                for z2 in range(8):
                    for j2 in range(8):
                        out[8 * k + z, own(z2, 8 * el + j2)] += zm[z, z2] * xm[j, j2]
    return out


def extended_rows(terms):
    local = local_rows(terms, range(16)).reshape(16, 8, 128)
    out = np.zeros((144, 144))
    for x in range(16):
        for z in range(8):
            out[own(z, x), :128] = local[x, z]
            if x in (7, 8):
                out[own(z, x), :128] += local[15 - x, z]
    for z in range(8):
        for zm, xm in terms:
            for z2 in range(8):
                out[own(z, 0), 128 + z2] += zm[z, z2] * xm[7, 7]
                out[128 + z, 128 + z2] += zm[z, z2] * xm[6, 7]
                out[own(z, 15), 136 + z2] += zm[z, z2] * xm[0, 0]
                out[136 + z, 136 + z2] += zm[z, z2] * xm[1, 0]
    return out


def z_rows(mats):
    blocks = [np.zeros((144, 144)) for _ in mats]
    for out, m in zip(blocks, mats):
        out[:128, :128] = np.kron(m, np.eye(16))
        out[128:136, 128:136] = m
        out[136:, 136:] = m
    return np.concatenate(blocks, axis=1)


def join_rows(zm, w):
    out = np.zeros((192, 384))
    below, above, down, up, far_b, far_a = 144, 200, 256, 296, 336, 360
    for t in range(18):
        side = t - 16
        own_row = lambda z: own(z, t) if t < 16 else 128 + 8 * side + z
        layer = lambda base, k: base + 16 * k + t if t < 16 else base + 48 + 2 * side + k
        msg_face = lambda base: base + 32 + t if t < 16 else base + 52 + side
        face = lambda base, k: base + 16 * k + t if t < 16 else base + 36 + 2 * k + side
        far = lambda base: base + t if t < 16 else base + 20 + side
        b7, b6, a0, a1 = np.zeros((4, 384))
        b7[layer(below, 1)] = b6[layer(below, 0)] = 1.0
        b7[face(down, 0)], b7[face(down, 1)], b7[far(far_b)] = zm[7, 7], w[7], zm[7, 0]
        b6[face(down, 0)], b6[far(far_b)] = zm[6, 7], zm[6, 0]
        a0[layer(above, 0)] = a1[layer(above, 1)] = 1.0
        a0[face(up, 0)], a0[face(up, 1)], a0[far(far_a)] = zm[0, 0], w[0], zm[0, 7]
        a1[face(up, 0)], a1[far(far_a)] = zm[1, 0], zm[1, 7]
        for z in range(8):
            row = out[own_row(z)]
            row[own_row(z)] += 1.0
            row[msg_face(below)] += zm[z, 0]
            row[msg_face(above)] += zm[z, 7]
        out[own_row(0)] += b7
        out[own_row(7)] += a0
        out[144 + t], out[168 + t] = b6, a1
    return out


def box_rows(vec):
    nodes = np.zeros((10, 2, 10, 192))
    for zk in range(10):
        for el in range(2):
            for xk in range(10):
                x = 8 * el + (-2 if xk == 0 else 9 if xk == 9 else xk - 1)
                side = -1 if x < 0 else 1 if x > 15 else 0
                if 0 < zk < 9:
                    row = {0: own(zk - 1, x), -1: 128 + zk - 1, 1: 136 + zk - 1}[side]
                else:
                    row = (144 if zk == 0 else 168) + {0: x, -1: 16, 1: 17}[side]
                nodes[zk, el, xk, row] = 1.0
    into = np.einsum("zi,xj,zexr->iejr", vec, vec, nodes).reshape(200, 192)
    back = np.zeros((8, 16, 10, 2, 10))
    inner = vec[1:9]
    for z in range(8):
        for x in range(16):
            el, j = divmod(x, 8)
            block = inner[z][:, None] * inner[j][None, :]
            if x in (7, 8):
                back[z, x, :, el] += 0.5 * block
                back[z, x, :, 1 - el] += 0.5 * inner[z][:, None] * inner[7 - j][None, :]
            else:
                back[z, x, :, el] += block
    back = back.reshape(128, 200)
    return np.pad(into, ((0, 8), (0, 0))), np.pad(back, ((0, 0), (0, 8)))


def box_lanes(vec, count):
    into = np.zeros((8 * count, 10 * count))
    back = np.zeros((10 * count, 8 * count))
    for e in range(count):
        spots = [8 * e - 2] + list(range(8 * e, 8 * e + 8)) + [8 * e + 9]
        for k, y in enumerate(spots):
            if 0 <= y < 8 * count:
                into[y, 10 * e : 10 * e + 10] += vec[k]
        for j in range(8):
            col = vec[j + 1]
            y = 8 * e + j
            if j == 0 and e > 0:
                back[10 * e : 10 * e + 10, [y - 1, y]] += 0.5 * col[:, None]
            elif j == 7 and e < count - 1:
                back[10 * e : 10 * e + 10, [y, y + 1]] += 0.5 * col[:, None]
            else:
                back[10 * e : 10 * e + 10, y] += col
    return into, back


def face_coefs(zm):
    return np.array([[zm[0, 7], zm[1, 7]], [zm[6, 0], zm[7, 0]]])


def constants():
    interp, slopes, deriv, stiff, w, vec, lam, v = tables_1d()
    c = {}
    c["y_in"] = right_const(
        np.concatenate([block_diag(interp.T, 32), block_diag(slopes.T, 32)], axis=1)
    )
    c["zx_in"] = left_const(
        np.concatenate(
            [np.kron(interp, interp), np.kron(slopes, interp), np.kron(interp, slopes)], axis=0
        )
    )
    test = v[:, None] * interp
    c["zx_out"] = left_const(np.kron(test.T, test.T))
    c["y_out"] = right_const(block_diag(test, 32))
    one, wm, wd = np.eye(8), np.diag(w), w[:, None] * deriv
    sides = (14, 15, 1, 0)
    for name, xm in (("w", wm), ("wd", wd), ("k", stiff)):
        c["xm_" + name] = left_const(local_rows([(one, xm)], sides))
        c["xe_" + name] = left_const(extended_rows([(one, xm)]))
    c["z_div"], c["z_st"] = left_const(z_rows((wd, wm))), left_const(z_rows((stiff, wm)))
    c["pick_div"], c["pick_st"] = face_coefs(wd), face_coefs(stiff)
    c["wd_y"] = right_const(block_diag(wd.T, 32))
    c["k_y"] = right_const(block_diag(stiff.T, 32))
    c["w_y"] = np.tile(w, 64)[None].astype(np.float32)
    into, back = box_rows(vec)
    c["box_div"] = left_const(into @ join_rows(wd, w))
    c["box_st"] = left_const(into @ join_rows(stiff, w))
    c["box_out"] = left_const(back)
    into, back = box_lanes(vec, 64)
    c["ybox_in"], c["ybox_out"] = right_const(into), right_const(back)
    inv = 1.0 / (lam[:, None, None, None] + lam[None, None, :, None] + lam)
    inv = np.broadcast_to(inv[:, :, :, None, :], (10, 1, 10, 64, 10))
    inv = np.broadcast_to(inv, (10, 2, 10, 64, 10)).reshape(200, 640)
    c["inv"] = np.pad(inv, ((0, 8), (0, 0))).astype(np.float32)
    return c


def split(x):
    hi = x.astype(BF16)
    return hi, (x - hi.astype(F32)).astype(BF16)


def rmul(x, const):
    hi, lo = split(x)
    depth = const.shape[0] // 2
    const = jnp.concatenate([const[:depth], const], axis=0)
    return jnp.dot(jnp.concatenate([hi, lo, hi], axis=1), const, preferred_element_type=F32)


def lmul(const, x):
    hi, lo = split(x)
    return jnp.dot(const, jnp.concatenate([hi, lo, hi], axis=0), preferred_element_type=F32)


def rmul_halves(x, const):
    return jnp.concatenate([rmul(x[:, :256], const), rmul(x[:, 256:], const)], axis=1)


def dss_lanes(x):
    lane = lax.broadcasted_iota(jnp.int32, x.shape, 1)
    n = x.shape[1]
    up = jnp.where((lane % 8 == 7) & (lane < n - 1), pltpu.roll(x, n - 1, 1), 0.0)
    down = jnp.where((lane % 8 == 0) & (lane > 0), pltpu.roll(x, 1, 1), 0.0)
    return x + up + down


def flags():
    z, x = lax.axis_index("wide"), lax.axis_index("narrow")
    nz, nx = lax.axis_size("wide"), lax.axis_size("narrow")
    as_flag = lambda t: t.astype(F32)
    return as_flag(z > 0), as_flag(z < nz - 1), as_flag(x > 0), as_flag(x < nx - 1)


def force_kernel(*refs):
    sources, (f_ref, r_ref, l_ref), held, sem = refs[:10], refs[10:13], refs[13:23], refs[23]
    v_ref, b_ref, y_in, zx_in, zx_out, y_out, xm_w, xm_wd, wd_y, w_y = held
    copies = [pltpu.make_async_copy(a, b, sem.at[k]) for k, (a, b) in enumerate(zip(sources, held))]
    for k in (2, 0, 1, 3, 4, 5, 6, 7, 8, 9):
        copies[k].start()
    copies[2].wait()
    copies[0].wait()
    v = jnp.concatenate([v_ref[:, :, k : k + 8].reshape(192, 512) for k in (0, 8)], axis=0)
    parts = [rmul(v[:, cut], y_in[...]) for cut in (slice(0, 256), slice(256, 512))]
    value = jnp.concatenate([p[:, :384] for p in parts], axis=1)
    slope = jnp.concatenate([p[:, 384:] for p in parts], axis=1)
    for copy in (copies[1], *copies[3:]):
        copy.wait()
    b = jnp.concatenate([b_ref[:, k : k + 8].reshape(64, 512) for k in (0, 8)], axis=0)
    parts = [rmul(b[:, cut], y_in[:, :384]) for cut in (slice(0, 256), slice(256, 512))]
    field = jnp.concatenate(parts, axis=1)
    back = []
    for el in range(2):
        u, gz, gx, gy = [], [], [], []
        for c in range(3):
            rows = slice(192 * el + 64 * c, 192 * el + 64 * c + 64)
            most = lmul(zx_in[...], value[rows])
            u.append(most[:144])
            gz.append(most[144:288])
            gx.append(most[288:])
            gy.append(lmul(zx_in[:144], slope[rows]))
        bq = lmul(zx_in[:144], field[64 * el : 64 * el + 64])
        b2 = bq * bq
        for c in range(3):
            conv = u[0] * gz[c] + u[1] * gx[c] + u[2] * gy[c]
            if c != 1:
                conv = conv + b2 * u[c]
            back.append(lmul(zx_out[...], -conv))
    back = jnp.concatenate(back, axis=0)
    halves = [rmul(back[:, cut], y_out[...]) for cut in (slice(0, 384), slice(384, 768))]
    f = dss_lanes(jnp.concatenate(halves, axis=1))
    first, second = f[:192], f[192:]
    node = lax.broadcasted_iota(jnp.int32, (192, 512), 0) % 8
    both = (
        first + jnp.where(node == 7, pltpu.roll(second, 7, 0), 0.0),
        second + jnp.where(node == 0, pltpu.roll(first, 185, 0), 0.0),
    )
    for k in range(24):
        for el in range(2):
            f_ref[16 * k + 8 * el : 16 * k + 8 * el + 8] = both[el][8 * k : 8 * k + 8]
    f = f_ref[...]
    s = lmul(xm_wd[...], f[128:256]) * w_y[...]
    s = s + rmul_halves(lmul(xm_w[...], f[256:]), wd_y[...])
    r_ref[:16] = s[:16]
    l_ref[:16] = s[16:]
    for k, (c, step) in enumerate(((0, 0), (1, 0), (2, 0), (0, 1))):
        r_ref[16 + 8 * k : 24 + 8 * k] = edge(f_ref, 128 * c, 15 - step)
        l_ref[16 + 8 * k : 24 + 8 * k] = edge(f_ref, 128 * c, step)


def edge(ref, base, x):
    return jnp.concatenate([ref[base + x + 16 * z : base + x + 16 * z + 1] for z in range(8)], axis=0)


def add_edge(ref, base, x, rows):
    for z in range(8):
        ref[base + x + 16 * z : base + x + 16 * z + 1] += rows[z : z + 1]


def extend(s, from_l, from_r, acc_ref):
    acc_ref[...] = s
    add_edge(acc_ref, 0, 0, from_l[8:16])
    add_edge(acc_ref, 0, 15, from_r[8:16])
    acc_ref[128:136] += from_l[:8]
    acc_ref[136:144] += from_r[:8]
    acc_ref[...] = dss_lanes(acc_ref[...])


def with_edges(full, raw_ref, base, has_l, has_r):
    edges = [edge(raw_ref, base, 0) * has_l, edge(raw_ref, base, 15) * has_r]
    return jnp.concatenate([full, *edges], axis=0)


def scaled_edges(ghost, last, w_y, ends):
    return jnp.concatenate([ghost * ends[0], last * ends[1]], axis=0) * w_y[...]


def send_faces(w_end, u, h0_ref, h12_ref, up_ref, down_ref, up_face_ref, down_face_ref, in_ref):
    for ref, own_ref, a, b, z in (
        (up_ref, up_face_ref, 6, 7, 7),
        (down_ref, down_face_ref, 0, 1, 0),
    ):
        ref[:16] = u[16 * a : 16 * a + 16]
        ref[16:32] = u[16 * b : 16 * b + 16]
        ref[32:48] = own_ref[:16] = h0_ref[16 * z : 16 * z + 16]
        own_ref[16:32] = h12_ref[16 * z : 16 * z + 16]
        half = 16 if z == 7 else 0
        ref[half : half + 16] += w_end * own_ref[16:32]
        h12 = [w_end * h12_ref[128 + 8 * s + z : 129 + 8 * s + z] for s in (0, 1)]
        rows = [u[128 + 8 * s + k : 129 + 8 * s + k] for s in (0, 1) for k in (a, b)]
        rows[z // 7] = rows[z // 7] + h12[0]
        rows[2 + z // 7] = rows[2 + z // 7] + h12[1]
        faces = [h[128 + 8 * s + z : 129 + 8 * s + z] for h in (h0_ref, h12_ref) for s in (0, 1)]
        ref[48:56] = jnp.concatenate(rows + faces, axis=0)
        own_ref[32:] = ref[48:56]
    in_ref[...] = jnp.where(is_odd(), down_ref[...], up_ref[...])


def is_odd():
    return lax.axis_index("wide") % 2 == 1


def div_kernel(ends, f_ref, ml_ref, mr_ref, xe_w, xe_wd, z_div, wd_y, w_y, *refs):
    force_ref, f_up_ref, f_down_ref, u_ref, *faces = refs[:9]
    h0_ref, h12_ref, fx_ref, sem = refs[9:]
    _, _, has_l, has_r = flags()
    ml, mr = ml_ref[...] * has_l, mr_ref[...] * has_r
    fx_ref[...] = f_ref[...]
    full = []
    for c in range(3):
        base, piece = 128 * c, slice(16 + 8 * c, 24 + 8 * c)
        add_edge(fx_ref, base, 0, ml[piece])
        add_edge(fx_ref, base, 15, mr[piece])
        full.append(with_edges(fx_ref[base : base + 128], f_ref, base, has_l, has_r))
        f_up_ref[16 * c : 16 * c + 16] = fx_ref[base + 112 : base + 128]
        f_down_ref[16 * c : 16 * c + 16] = fx_ref[base : base + 16]
    copy = pltpu.make_async_copy(fx_ref, force_ref, sem.at[0])
    copy.start()
    from_l = scaled_edges(ml[40:48], ml[16:24], w_y, ends)
    from_r = scaled_edges(mr[40:48], mr[16:24], w_y, ends)
    extend(lmul(xe_w[...], full[0]) * w_y[...], from_l, from_r, h0_ref)
    h = lmul(xe_wd[...], full[1]) * w_y[...] + rmul_halves(lmul(xe_w[...], full[2]), wd_y[...])
    extend(h, ml[:16], mr[:16], h12_ref)
    u = lmul(z_div[...], jnp.concatenate([h0_ref[...], h12_ref[...]], axis=0))
    u_ref[...] = u
    send_faces(ends[1], u, h0_ref, h12_ref, *faces)
    copy.wait()


def outer_kernel(coefs, up_ref, down_ref, in_ref, out_ref):
    odd = is_odd()
    ca = jnp.where(odd, coefs[1][0], coefs[0][0])
    cb = jnp.where(odd, coefs[1][1], coefs[0][1])
    out_ref[...] = jnp.where(odd, up_ref[...], down_ref[...])
    face, far_l, far_r = in_ref[32:48], in_ref[52:53], in_ref[53:54]
    out_ref[:16] += ca * face
    out_ref[16:32] += cb * face
    out_ref[48:52] += jnp.concatenate([ca * far_l, cb * far_l, ca * far_r, cb * far_r], axis=0)


def outer_force_kernel(coefs, f_up, f_down, up_ref, down_ref, in_ref, out_ref, f_out_ref):
    outer_kernel(coefs, up_ref, down_ref, in_ref, out_ref)
    f_out_ref[...] = jnp.where(is_odd(), f_up[...], f_down[...])


def far_kernel(out_msg_ref, far_ref):
    has_b, has_a, _, _ = flags()
    flag = jnp.where(is_odd(), has_a, has_b)
    far_ref[:16] = out_msg_ref[32:48] * flag
    far_ref[16:] = out_msg_ref[48:56] * flag


def join(u_ref, up_ref, down_ref, in_ref, out_ref, far_ref, const):
    has_b, has_a, _, _ = flags()
    odd = is_odd()
    inner = in_ref[...]
    outer = out_ref[...] * jnp.where(odd, has_a, has_b)
    far = far_ref[...]
    rows = [
        u_ref[...],
        jnp.where(odd, inner, outer),
        jnp.where(odd, outer, inner),
        down_ref[...] * has_b,
        up_ref[...] * has_a,
        jnp.where(odd, far, 0.0),
        jnp.where(odd, 0.0, far),
    ]
    return lmul(const[...], jnp.concatenate(rows, axis=0))


def box(t, ybox_in, inv, box_out, ybox_out):
    has_b, has_a, has_l, has_r = flags()
    t = rmul(t, ybox_in[...]) * inv[...]
    g = rmul(lmul(box_out[...], t), ybox_out[...])
    row = lax.broadcasted_iota(jnp.int32, (128, 1), 0)
    z, x = row // 16, row % 16
    weight = 1.0 - 0.5 * jnp.where(z == 0, has_b, jnp.where(z == 7, has_a, 0.0))
    weight = weight * (1.0 - 0.5 * jnp.where(x == 0, has_l, jnp.where(x == 15, has_r, 0.0)))
    return g * weight


def first_kernel(*refs):
    t_ref, g_ref = refs[11:]
    t = join(*refs[:7])
    t_ref[...] = t
    g_ref[...] = box(t, *refs[7:11])


def stiff_msg_kernel(g_ref, xm_w, xm_k, k_y, w_y, *refs):
    r_ref, l_ref = refs[-2:]
    g = g_ref[...]
    q = lmul(xm_k[...], g) * w_y[...] + rmul_halves(lmul(xm_w[...], g), k_y[...])
    r_ref[:16] = q[:16]
    l_ref[:16] = q[16:]
    r_ref[16:24] = edge(g_ref, 0, 15)
    l_ref[16:24] = edge(g_ref, 0, 0)
    r_ref[24:] = edge(g_ref, 0, 14)
    l_ref[24:] = edge(g_ref, 0, 1)


def stiff_kernel(ends, g_ref, ml_ref, mr_ref, xe_w, xe_k, z_st, k_y, w_y, *refs):
    gx_ref, u_ref, *faces = refs[:7]
    p_ref, q_ref = refs[7:]
    _, _, has_l, has_r = flags()
    ml, mr = ml_ref[...] * has_l, mr_ref[...] * has_r
    gx_ref[...] = g_ref[...]
    add_edge(gx_ref, 0, 0, ml[16:24])
    add_edge(gx_ref, 0, 15, mr[16:24])
    full = with_edges(gx_ref[...], g_ref, 0, has_l, has_r)
    from_l = scaled_edges(ml[24:], ml[16:24], w_y, ends)
    from_r = scaled_edges(mr[24:], mr[16:24], w_y, ends)
    plain = lmul(xe_w[...], full)
    extend(plain * w_y[...], from_l, from_r, p_ref)
    q = lmul(xe_k[...], full) * w_y[...] + rmul_halves(plain, k_y[...])
    extend(q, ml[:16], mr[:16], q_ref)
    u = lmul(z_st[...], jnp.concatenate([p_ref[...], q_ref[...]], axis=0))
    u_ref[...] = u
    send_faces(ends[1], u, p_ref, q_ref, *faces)


def second_kernel(t_ref, *refs):
    join_refs, box_refs, (g_ref, r_ref, l_ref) = refs[:7], refs[7:11], refs[11:]
    g_ref[...] = box(t_ref[...] - join(*join_refs), *box_refs)
    r_ref[...] = edge(g_ref, 0, 15)
    l_ref[...] = edge(g_ref, 0, 0)


def last_x_kernel(g_ref, gx_ref, ml_ref, mr_ref, f_up, f_down, out_ref, in_msg_ref, out_msg_ref):
    _, _, has_l, has_r = flags()
    out_ref[...] = g_ref[...] + gx_ref[...]
    add_edge(out_ref, 0, 0, ml_ref[...] * has_l)
    add_edge(out_ref, 0, 15, mr_ref[...] * has_r)
    odd = is_odd()
    up, down = out_ref[112:], out_ref[:16]
    out_msg_ref[...] = jnp.where(odd, up, down)
    in_msg_ref[:16] = jnp.where(odd, down, up)
    in_msg_ref[16:] = jnp.where(odd, f_down[...], f_up[...])


def last_z_kernel(
    out_msg_ref, in_ref, f_out_ref, g_ref, f_up, f_down, _, out_ref, force_ref, face_ref, p_ref, sem
):
    has_b, has_a, _, _ = flags()
    odd = is_odd()
    inner, flag = in_ref[...], jnp.where(odd, has_a, has_b)
    outer = jnp.concatenate([out_msg_ref[...], f_out_ref[...]], axis=0) * flag
    below, above = jnp.where(odd, inner, outer), jnp.where(odd, outer, inner)
    p_ref[...] = g_ref[...]
    p_ref[:16] += below[:16]
    p_ref[112:] += above[:16]
    face_ref[:48] = f_down[...] + below[16:]
    face_ref[48:] = f_up[...] + above[16:]
    copies = [pltpu.make_async_copy(p_ref, out_ref, sem.at[6])]
    for c in range(3):
        for k, row in enumerate((128 * c, 128 * c + 112)):
            src = face_ref.at[pl.ds(48 * k + 16 * c, 16)]
            dst = force_ref.at[pl.ds(row, 16)]
            copies.append(pltpu.make_async_copy(src, dst, sem.at[2 * c + k]))
    for copy in copies:
        copy.start()
    for copy in copies:
        copy.wait()


def call(kernel, name, outs, *args, scratch=(), sems=0, vmem=16, hbm_in=(), hbm_out=(), alias=None):
    shape = lambda rows: jax.ShapeDtypeStruct((rows, 512), F32)
    spec = lambda k, far: pl.BlockSpec(memory_space=pltpu.HBM if k in far else pltpu.VMEM)
    scratch = [pltpu.VMEM((k, 512), F32) if isinstance(k, int) else k for k in scratch]
    return pl.pallas_call(
        kernel,
        out_shape=[shape(o) for o in outs],
        in_specs=[spec(k, hbm_in) for k in range(len(args))],
        out_specs=[spec(k, hbm_out) for k in range(len(outs))],
        scratch_shapes=scratch + ([pltpu.SemaphoreType.DMA((sems,))] if sems else []),
        input_output_aliases=alias or {},
        compiler_params=pltpu.CompilerParams(vmem_limit_bytes=vmem * MIB),
        name=name,
    )(*args)


def exchange_x(rightward, leftward):
    n = lax.axis_size("narrow")
    right = [(i, (i + 1) % n) for i in range(n)]
    left = [(j, i) for i, j in right]
    return lax.ppermute(rightward, "narrow", right), lax.ppermute(leftward, "narrow", left)


def other_core(x):
    n = lax.axis_size("wide")
    return lax.ppermute(x, "wide", [(i, i + 1 - 2 * (i % 2)) for i in range(n)])


def next_chip(x):
    nz, nx = lax.axis_size("wide"), lax.axis_size("narrow")
    pairs = []
    for z in range(nz):
        to = z - 1 + 2 * (z % 2)
        for k in range(nx):
            other = (to, k) if 0 <= to < nz else (z, k + 1 - 2 * (k % 2))
            pairs.append((z * nx + k, other[0] * nx + other[1]))
    return lax.ppermute(x, ("wide", "narrow"), pairs)


def meet(up, down, inner_msg, coefs, name, force_faces=()):
    inner = other_core(inner_msg)
    coefs = [[float(t) for t in row] for row in coefs]
    kernel, outs = (outer_force_kernel, (56, 48)) if force_faces else (outer_kernel, (56,))
    msgs = call(functools.partial(kernel, coefs), name, outs, *force_faces, up, down, inner)
    outer = next_chip(msgs[0])
    (far,) = call(far_kernel, name + "_far", (24,), outer)
    return inner, outer, other_core(far), *map(next_chip, msgs[1:])


def shards(velocity, bfield):
    tables = constants()
    picks = tables.pop("pick_div"), tables.pop("pick_st")
    c = {name: jnp.asarray(value) for name, value in tables.items()}
    consts = lambda *names: [c[name] for name in names]
    weights = tables_1d()[4]
    ends = float(weights[1]), float(weights[0])
    force_args = (
        velocity,
        bfield,
        *consts("y_in", "zx_in", "zx_out", "y_out", "xm_w", "xm_wd", "wd_y", "w_y"),
    )
    force_args = [pltpu.with_memory_space_constraint(x, pltpu.HBM) for x in force_args]
    f, right, left = call(
        force_kernel,
        "force",
        (384, 48, 48),
        *force_args,
        scratch=[pltpu.VMEM(a.shape, a.dtype) for a in force_args],
        sems=10,
        vmem=32,
        hbm_in=range(10),
    )
    from_l, from_r = exchange_x(right, left)
    force, f_up, f_down, u, up, down, up_face, down_face, inner = call(
        functools.partial(div_kernel, ends),
        "div",
        (384, 48, 48, 144, 56, 56, 40, 40, 56),
        f,
        from_l,
        from_r,
        *consts("xe_w", "xe_wd", "z_div", "wd_y", "w_y"),
        scratch=(144, 144, 384),
        sems=1,
        hbm_out=(0,),
    )
    inner, outer, far, f_out = meet(up, down, inner, picks[0], "div_out", (f_up, f_down))
    box_consts = consts("ybox_in", "inv", "box_out", "ybox_out")
    spectral, g = call(
        first_kernel,
        "first_pass",
        (208, 128),
        u,
        up_face,
        down_face,
        inner,
        outer,
        far,
        c["box_div"],
        *box_consts,
    )
    msg_consts = consts("xm_w", "xm_k", "k_y", "w_y")
    right, left = call(stiff_msg_kernel, "stiff_msg", (32, 32), g, *msg_consts, f_out)
    from_l, from_r = exchange_x(right, left)
    gx, u, up, down, up_face, down_face, inner = call(
        functools.partial(stiff_kernel, ends),
        "stiff",
        (128, 144, 56, 56, 40, 40, 56),
        g,
        from_l,
        from_r,
        *consts("xe_w", "xe_k", "z_st", "k_y", "w_y"),
        scratch=(144, 144),
    )
    inner, outer, far = meet(up, down, inner, picks[1], "stiff_out")
    g, right, left = call(
        second_kernel,
        "second_pass",
        (128, 8, 8),
        spectral,
        u,
        up_face,
        down_face,
        inner,
        outer,
        far,
        c["box_st"],
        *box_consts,
    )
    from_l, from_r = exchange_x(right, left)
    total, inner, outer = call(
        last_x_kernel, "last_x", (128, 64, 16), g, gx, from_l, from_r, f_up, f_down
    )
    outer, inner = next_chip(outer), other_core(inner)
    pressure, force = call(
        last_z_kernel,
        "last_z",
        (128, 384),
        outer,
        inner,
        f_out,
        total,
        f_up,
        f_down,
        force,
        scratch=(96, 128),
        sems=7,
        hbm_in=(6,),
        hbm_out=(0, 1),
        alias={6: 1},
    )
    return force.reshape(3, 8, 16, 512), pressure.reshape(8, 16, 512)


def solution(mesh):
    placed = (P(None, "wide", "narrow", None), P("wide", "narrow", None))
    return jax.shard_map(
        shards, mesh=mesh, in_specs=placed, out_specs=placed, check_vma=False
    )
```

```python
import functools

import jax
import jax.numpy as jnp
import ml_dtypes
import numpy as np
from jax import lax
from jax.experimental import pallas as pl
from jax.experimental.pallas import tpu as pltpu
from jax.sharding import PartitionSpec as P

F32 = jnp.float32
BF16 = jnp.bfloat16
MIB = 2**20


def legendre_pair(degree, points):
    below, current = np.ones(points.shape), points * 1.0
    for step in range(2, degree + 1):
        below, current = current, ((2 * step - 1) * points * current - (step - 1) * below) / step
    return current, below


def tables_1d():
    points = np.cos(np.pi * np.arange(8) / 7)
    for _ in range(60):
        top, below = legendre_pair(7, points)
        points = points - (points * top - below) / (8 * top)
    points = np.sort(points)
    top, below = legendre_pair(7, points)
    w = 2.0 / (56 * top**2)
    spacing = points[:, None] - points[None, :] + np.eye(8)
    deriv = top[:, None] / (top[None, :] * spacing) * (1.0 - np.eye(8))
    deriv[0, 0], deriv[-1, -1] = -14.0, 14.0
    gauss = np.cos(np.pi * (np.arange(12) + 0.75) / 12.5)
    for _ in range(60):
        top, below = legendre_pair(12, gauss)
        gauss = gauss - top / (12 * (gauss * top - below) / (gauss**2 - 1.0))
    top, below = legendre_pair(12, gauss)
    slope = 12 * (gauss * top - below) / (gauss**2 - 1.0)
    v = 2.0 / ((1.0 - gauss**2) * slope**2)
    interp = np.ones((12, 8))
    for col in range(8):
        for other in range(8):
            if other != col:
                interp[:, col] *= (gauss - points[other]) / (points[col] - points[other])
    stiff = deriv.T @ (w[:, None] * deriv)
    wide_stiff, wide_mass = np.zeros((22, 22)), np.zeros(22)
    for el in range(3):
        r = 7 * el
        wide_stiff[r : r + 8, r : r + 8] += stiff
        wide_mass[r : r + 8] += w
    scale = 1.0 / np.sqrt(wide_mass[6:16])
    lam, vec = np.linalg.eigh(scale[:, None] * wide_stiff[6:16, 6:16] * scale[None, :])
    return interp, interp @ deriv, deriv, stiff, w, scale[:, None] * vec, lam, v


def hi_lo(m):
    hi = m.astype(ml_dtypes.bfloat16)
    return hi, (m - hi.astype(np.float64)).astype(ml_dtypes.bfloat16)


def left_const(m):
    hi, lo = hi_lo(m)
    return np.concatenate([hi, hi, lo], axis=1)


def right_const(m):
    return np.concatenate(hi_lo(m), axis=0)


def block_diag(m, count):
    return np.kron(np.eye(count), m)


def own(z, x):
    return 16 * z + x


def local_rows(terms, xs):
    out = np.zeros((8 * len(xs), 128))
    for k, x in enumerate(xs):
        el, j = divmod(x, 8)
        for z in range(8):
            for zm, xm in terms:
                for z2 in range(8):
                    for j2 in range(8):
                        out[8 * k + z, own(z2, 8 * el + j2)] += zm[z, z2] * xm[j, j2]
    return out


def extended_rows(terms):
    local = local_rows(terms, range(16)).reshape(16, 8, 128)
    out = np.zeros((144, 144))
    for x in range(16):
        for z in range(8):
            out[own(z, x), :128] = local[x, z]
            if x in (7, 8):
                out[own(z, x), :128] += local[15 - x, z]
    for z in range(8):
        for zm, xm in terms:
            for z2 in range(8):
                out[own(z, 0), 128 + z2] += zm[z, z2] * xm[7, 7]
                out[128 + z, 128 + z2] += zm[z, z2] * xm[6, 7]
                out[own(z, 15), 136 + z2] += zm[z, z2] * xm[0, 0]
                out[136 + z, 136 + z2] += zm[z, z2] * xm[1, 0]
    return out


def z_rows(mats):
    blocks = [np.zeros((144, 144)) for _ in mats]
    for out, m in zip(blocks, mats):
        out[:128, :128] = np.kron(m, np.eye(16))
        out[128:136, 128:136] = m
        out[136:, 136:] = m
    return np.concatenate(blocks, axis=1)


def join_rows(zm, w):
    out = np.zeros((192, 384))
    below, above, down, up, far_b, far_a = 144, 200, 256, 296, 336, 360
    for t in range(18):
        side = t - 16
        own_row = lambda z: own(z, t) if t < 16 else 128 + 8 * side + z
        layer = lambda base, k: base + 16 * k + t if t < 16 else base + 48 + 2 * side + k
        msg_face = lambda base: base + 32 + t if t < 16 else base + 52 + side
        face = lambda base, k: base + 16 * k + t if t < 16 else base + 36 + 2 * k + side
        far = lambda base: base + t if t < 16 else base + 20 + side
        b7, b6, a0, a1 = np.zeros((4, 384))
        b7[layer(below, 1)] = b6[layer(below, 0)] = 1.0
        b7[face(down, 0)], b7[face(down, 1)], b7[far(far_b)] = zm[7, 7], w[7], zm[7, 0]
        b6[face(down, 0)], b6[far(far_b)] = zm[6, 7], zm[6, 0]
        a0[layer(above, 0)] = a1[layer(above, 1)] = 1.0
        a0[face(up, 0)], a0[face(up, 1)], a0[far(far_a)] = zm[0, 0], w[0], zm[0, 7]
        a1[face(up, 0)], a1[far(far_a)] = zm[1, 0], zm[1, 7]
        for z in range(8):
            row = out[own_row(z)]
            row[own_row(z)] += 1.0
            row[msg_face(below)] += zm[z, 0]
            row[msg_face(above)] += zm[z, 7]
        out[own_row(0)] += b7
        out[own_row(7)] += a0
        out[144 + t], out[168 + t] = b6, a1
    return out


def box_rows(vec):
    nodes = np.zeros((10, 2, 10, 192))
    for zk in range(10):
        for el in range(2):
            for xk in range(10):
                x = 8 * el + (-2 if xk == 0 else 9 if xk == 9 else xk - 1)
                side = -1 if x < 0 else 1 if x > 15 else 0
                if 0 < zk < 9:
                    row = {0: own(zk - 1, x), -1: 128 + zk - 1, 1: 136 + zk - 1}[side]
                else:
                    row = (144 if zk == 0 else 168) + {0: x, -1: 16, 1: 17}[side]
                nodes[zk, el, xk, row] = 1.0
    into = np.einsum("zi,xj,zexr->iejr", vec, vec, nodes).reshape(200, 192)
    back = np.zeros((8, 16, 10, 2, 10))
    inner = vec[1:9]
    for z in range(8):
        for x in range(16):
            el, j = divmod(x, 8)
            block = inner[z][:, None] * inner[j][None, :]
            if x in (7, 8):
                back[z, x, :, el] += 0.5 * block
                back[z, x, :, 1 - el] += 0.5 * inner[z][:, None] * inner[7 - j][None, :]
            else:
                back[z, x, :, el] += block
    back = back.reshape(128, 200)
    return np.pad(into, ((0, 8), (0, 0))), np.pad(back, ((0, 0), (0, 8)))


def box_lanes(vec, count):
    into = np.zeros((8 * count, 10 * count))
    back = np.zeros((10 * count, 8 * count))
    for e in range(count):
        spots = [8 * e - 2] + list(range(8 * e, 8 * e + 8)) + [8 * e + 9]
        for k, y in enumerate(spots):
            if 0 <= y < 8 * count:
                into[y, 10 * e : 10 * e + 10] += vec[k]
        for j in range(8):
            col = vec[j + 1]
            y = 8 * e + j
            if j == 0 and e > 0:
                back[10 * e : 10 * e + 10, [y - 1, y]] += 0.5 * col[:, None]
            elif j == 7 and e < count - 1:
                back[10 * e : 10 * e + 10, [y, y + 1]] += 0.5 * col[:, None]
            else:
                back[10 * e : 10 * e + 10, y] += col
    return into, back


def face_coefs(zm):
    return np.array([[zm[0, 7], zm[1, 7]], [zm[6, 0], zm[7, 0]]])


def constants():
    interp, slopes, deriv, stiff, w, vec, lam, v = tables_1d()
    c = {}
    c["y_in"] = right_const(
        np.concatenate([block_diag(interp.T, 32), block_diag(slopes.T, 32)], axis=1)
    )
    c["zx_in"] = left_const(
        np.concatenate(
            [np.kron(interp, interp), np.kron(slopes, interp), np.kron(interp, slopes)], axis=0
        )
    )
    test = v[:, None] * interp
    c["zx_out"] = left_const(np.kron(test.T, test.T))
    c["y_out"] = right_const(block_diag(test, 32))
    one, wm, wd = np.eye(8), np.diag(w), w[:, None] * deriv
    sides = (14, 15, 1, 0)
    for name, xm in (("w", wm), ("wd", wd), ("k", stiff)):
        c["xm_" + name] = left_const(local_rows([(one, xm)], sides))
        c["xe_" + name] = left_const(extended_rows([(one, xm)]))
    c["z_div"], c["z_st"] = left_const(z_rows((wd, wm))), left_const(z_rows((stiff, wm)))
    c["pick_div"], c["pick_st"] = face_coefs(wd), face_coefs(stiff)
    c["wd_y"] = right_const(block_diag(wd.T, 32))
    c["k_y"] = right_const(block_diag(stiff.T, 32))
    c["w_y"] = np.tile(w, 64)[None].astype(np.float32)
    into, back = box_rows(vec)
    c["box_div"] = left_const(into @ join_rows(wd, w))
    c["box_st"] = left_const(into @ join_rows(stiff, w))
    c["box_out"] = left_const(back)
    into, back = box_lanes(vec, 64)
    c["ybox_in"], c["ybox_out"] = right_const(into), right_const(back)
    inv = 1.0 / (lam[:, None, None, None] + lam[None, None, :, None] + lam)
    inv = np.broadcast_to(inv[:, :, :, None, :], (10, 1, 10, 64, 10))
    inv = np.broadcast_to(inv, (10, 2, 10, 64, 10)).reshape(200, 640)
    c["inv"] = np.pad(inv, ((0, 8), (0, 0))).astype(np.float32)
    return c


def split(x):
    hi = x.astype(BF16)
    return hi, (x - hi.astype(F32)).astype(BF16)


def rmul(x, const):
    hi, lo = split(x)
    depth = const.shape[0] // 2
    const = jnp.concatenate([const[:depth], const], axis=0)
    return jnp.dot(jnp.concatenate([hi, lo, hi], axis=1), const, preferred_element_type=F32)


def lmul(const, x):
    hi, lo = split(x)
    return jnp.dot(const, jnp.concatenate([hi, lo, hi], axis=0), preferred_element_type=F32)


def rmul_halves(x, const):
    return jnp.concatenate([rmul(x[:, :256], const), rmul(x[:, 256:], const)], axis=1)


def dss_lanes(x):
    lane = lax.broadcasted_iota(jnp.int32, x.shape, 1)
    n = x.shape[1]
    up = jnp.where((lane % 8 == 7) & (lane < n - 1), pltpu.roll(x, n - 1, 1), 0.0)
    down = jnp.where((lane % 8 == 0) & (lane > 0), pltpu.roll(x, 1, 1), 0.0)
    return x + up + down


def flags():
    z, x = lax.axis_index("wide"), lax.axis_index("narrow")
    nz, nx = lax.axis_size("wide"), lax.axis_size("narrow")
    as_flag = lambda t: t.astype(F32)
    return as_flag(z > 0), as_flag(z < nz - 1), as_flag(x > 0), as_flag(x < nx - 1)


def force_kernel(*refs):
    sources, (f_ref, r_ref, l_ref), held, sem = refs[:10], refs[10:13], refs[13:23], refs[23]
    v_ref, b_ref, y_in, zx_in, zx_out, y_out, xm_w, xm_wd, wd_y, w_y = held
    copies = [pltpu.make_async_copy(a, b, sem.at[k]) for k, (a, b) in enumerate(zip(sources, held))]
    for k in (2, 0, 1, 3, 4, 5, 6, 7, 8, 9):
        copies[k].start()
    copies[2].wait()
    copies[0].wait()
    v = jnp.concatenate([v_ref[:, :, k : k + 8].reshape(192, 512) for k in (0, 8)], axis=0)
    parts = [rmul(v[:, cut], y_in[...]) for cut in (slice(0, 256), slice(256, 512))]
    value = jnp.concatenate([p[:, :384] for p in parts], axis=1)
    slope = jnp.concatenate([p[:, 384:] for p in parts], axis=1)
    for copy in (copies[1], *copies[3:]):
        copy.wait()
    b = jnp.concatenate([b_ref[:, k : k + 8].reshape(64, 512) for k in (0, 8)], axis=0)
    parts = [rmul(b[:, cut], y_in[:, :384]) for cut in (slice(0, 256), slice(256, 512))]
    field = jnp.concatenate(parts, axis=1)
    back = []
    for el in range(2):
        u, gz, gx, gy = [], [], [], []
        for c in range(3):
            rows = slice(192 * el + 64 * c, 192 * el + 64 * c + 64)
            most = lmul(zx_in[...], value[rows])
            u.append(most[:144])
            gz.append(most[144:288])
            gx.append(most[288:])
            gy.append(lmul(zx_in[:144], slope[rows]))
        bq = lmul(zx_in[:144], field[64 * el : 64 * el + 64])
        b2 = bq * bq
        for c in range(3):
            conv = u[0] * gz[c] + u[1] * gx[c] + u[2] * gy[c]
            if c != 1:
                conv = conv + b2 * u[c]
            back.append(lmul(zx_out[...], -conv))
    back = jnp.concatenate(back, axis=0)
    halves = [rmul(back[:, cut], y_out[...]) for cut in (slice(0, 384), slice(384, 768))]
    f = dss_lanes(jnp.concatenate(halves, axis=1))
    first, second = f[:192], f[192:]
    node = lax.broadcasted_iota(jnp.int32, (192, 512), 0) % 8
    both = (
        first + jnp.where(node == 7, pltpu.roll(second, 7, 0), 0.0),
        second + jnp.where(node == 0, pltpu.roll(first, 185, 0), 0.0),
    )
    for k in range(24):
        for el in range(2):
            f_ref[16 * k + 8 * el : 16 * k + 8 * el + 8] = both[el][8 * k : 8 * k + 8]
    f = f_ref[...]
    s = lmul(xm_wd[...], f[128:256]) * w_y[...]
    s = s + rmul_halves(lmul(xm_w[...], f[256:]), wd_y[...])
    r_ref[:16] = s[:16]
    l_ref[:16] = s[16:]
    for k, (c, step) in enumerate(((0, 0), (1, 0), (2, 0), (0, 1))):
        r_ref[16 + 8 * k : 24 + 8 * k] = edge(f_ref, 128 * c, 15 - step)
        l_ref[16 + 8 * k : 24 + 8 * k] = edge(f_ref, 128 * c, step)
    to_pairs(r_ref, l_ref)


def to_pairs(r_ref, l_ref):
    right, left = r_ref[...], l_ref[...]
    odd = lax.axis_index("narrow") % 2 == 1
    r_ref[...] = jnp.where(odd, right, left)
    l_ref[...] = jnp.where(odd, left, right)


def from_pairs(far_ref, near_ref):
    far, near = far_ref[...], near_ref[...]
    odd = lax.axis_index("narrow") % 2 == 1
    return jnp.where(odd, near, far), jnp.where(odd, far, near)


def edge(ref, base, x):
    return jnp.concatenate([ref[base + x + 16 * z : base + x + 16 * z + 1] for z in range(8)], axis=0)


def add_edge(ref, base, x, rows):
    for z in range(8):
        ref[base + x + 16 * z : base + x + 16 * z + 1] += rows[z : z + 1]


def extend(s, from_l, from_r, acc_ref):
    acc_ref[...] = s
    add_edge(acc_ref, 0, 0, from_l[8:16])
    add_edge(acc_ref, 0, 15, from_r[8:16])
    acc_ref[128:136] += from_l[:8]
    acc_ref[136:144] += from_r[:8]
    acc_ref[...] = dss_lanes(acc_ref[...])


def with_edges(full, raw_ref, base, has_l, has_r):
    edges = [edge(raw_ref, base, 0) * has_l, edge(raw_ref, base, 15) * has_r]
    return jnp.concatenate([full, *edges], axis=0)


def scaled_edges(ghost, last, w_y, ends):
    return jnp.concatenate([ghost * ends[0], last * ends[1]], axis=0) * w_y[...]


def send_faces(w_end, u, h0_ref, h12_ref, up_ref, down_ref, up_face_ref, down_face_ref, in_ref):
    for ref, own_ref, a, b, z in (
        (up_ref, up_face_ref, 6, 7, 7),
        (down_ref, down_face_ref, 0, 1, 0),
    ):
        ref[:16] = u[16 * a : 16 * a + 16]
        ref[16:32] = u[16 * b : 16 * b + 16]
        ref[32:48] = own_ref[:16] = h0_ref[16 * z : 16 * z + 16]
        own_ref[16:32] = h12_ref[16 * z : 16 * z + 16]
        half = 16 if z == 7 else 0
        ref[half : half + 16] += w_end * own_ref[16:32]
        h12 = [w_end * h12_ref[128 + 8 * s + z : 129 + 8 * s + z] for s in (0, 1)]
        rows = [u[128 + 8 * s + k : 129 + 8 * s + k] for s in (0, 1) for k in (a, b)]
        rows[z // 7] = rows[z // 7] + h12[0]
        rows[2 + z // 7] = rows[2 + z // 7] + h12[1]
        faces = [h[128 + 8 * s + z : 129 + 8 * s + z] for h in (h0_ref, h12_ref) for s in (0, 1)]
        ref[48:56] = jnp.concatenate(rows + faces, axis=0)
        own_ref[32:] = ref[48:56]
    in_ref[...] = jnp.where(is_odd(), down_ref[...], up_ref[...])


def is_odd():
    return lax.axis_index("wide") % 2 == 1


def div_kernel(ends, f_ref, ml_ref, mr_ref, xe_w, xe_wd, z_div, wd_y, w_y, *refs):
    force_ref, f_up_ref, f_down_ref, u_ref, *faces = refs[:9]
    h0_ref, h12_ref, fx_ref, sem = refs[9:]
    _, _, has_l, has_r = flags()
    ml, mr = from_pairs(ml_ref, mr_ref)
    ml, mr = ml * has_l, mr * has_r
    fx_ref[...] = f_ref[...]
    full = []
    for c in range(3):
        base, piece = 128 * c, slice(16 + 8 * c, 24 + 8 * c)
        add_edge(fx_ref, base, 0, ml[piece])
        add_edge(fx_ref, base, 15, mr[piece])
        full.append(with_edges(fx_ref[base : base + 128], f_ref, base, has_l, has_r))
        f_up_ref[16 * c : 16 * c + 16] = fx_ref[base + 112 : base + 128]
        f_down_ref[16 * c : 16 * c + 16] = fx_ref[base : base + 16]
    copy = pltpu.make_async_copy(fx_ref, force_ref, sem.at[0])
    copy.start()
    from_l = scaled_edges(ml[40:48], ml[16:24], w_y, ends)
    from_r = scaled_edges(mr[40:48], mr[16:24], w_y, ends)
    extend(lmul(xe_w[...], full[0]) * w_y[...], from_l, from_r, h0_ref)
    h = lmul(xe_wd[...], full[1]) * w_y[...] + rmul_halves(lmul(xe_w[...], full[2]), wd_y[...])
    extend(h, ml[:16], mr[:16], h12_ref)
    u = lmul(z_div[...], jnp.concatenate([h0_ref[...], h12_ref[...]], axis=0))
    u_ref[...] = u
    send_faces(ends[1], u, h0_ref, h12_ref, *faces)
    copy.wait()


def outer_kernel(coefs, up_ref, down_ref, in_ref, out_ref):
    odd = is_odd()
    ca = jnp.where(odd, coefs[1][0], coefs[0][0])
    cb = jnp.where(odd, coefs[1][1], coefs[0][1])
    out_ref[...] = jnp.where(odd, up_ref[...], down_ref[...])
    face, far_l, far_r = in_ref[32:48], in_ref[52:53], in_ref[53:54]
    out_ref[:16] += ca * face
    out_ref[16:32] += cb * face
    out_ref[48:52] += jnp.concatenate([ca * far_l, cb * far_l, ca * far_r, cb * far_r], axis=0)


def outer_force_kernel(coefs, f_up, f_down, up_ref, down_ref, in_ref, out_ref, f_out_ref):
    outer_kernel(coefs, up_ref, down_ref, in_ref, out_ref)
    f_out_ref[...] = jnp.where(is_odd(), f_up[...], f_down[...])


def far_kernel(out_msg_ref, far_ref):
    has_b, has_a, _, _ = flags()
    flag = jnp.where(is_odd(), has_a, has_b)
    far_ref[:16] = out_msg_ref[32:48] * flag
    far_ref[16:] = out_msg_ref[48:56] * flag


def join(u_ref, up_ref, down_ref, in_ref, out_ref, far_ref, const):
    has_b, has_a, _, _ = flags()
    odd = is_odd()
    inner = in_ref[...]
    outer = out_ref[...] * jnp.where(odd, has_a, has_b)
    far = far_ref[...]
    rows = [
        u_ref[...],
        jnp.where(odd, inner, outer),
        jnp.where(odd, outer, inner),
        down_ref[...] * has_b,
        up_ref[...] * has_a,
        jnp.where(odd, far, 0.0),
        jnp.where(odd, 0.0, far),
    ]
    return lmul(const[...], jnp.concatenate(rows, axis=0))


def box(t, ybox_in, inv, box_out, ybox_out):
    has_b, has_a, has_l, has_r = flags()
    t = rmul(t, ybox_in[...]) * inv[...]
    g = rmul(lmul(box_out[...], t), ybox_out[...])
    row = lax.broadcasted_iota(jnp.int32, (128, 1), 0)
    z, x = row // 16, row % 16
    weight = 1.0 - 0.5 * jnp.where(z == 0, has_b, jnp.where(z == 7, has_a, 0.0))
    weight = weight * (1.0 - 0.5 * jnp.where(x == 0, has_l, jnp.where(x == 15, has_r, 0.0)))
    return g * weight


def first_kernel(*refs):
    t_ref, g_ref = refs[11:]
    t = join(*refs[:7])
    t_ref[...] = t
    g_ref[...] = box(t, *refs[7:11])


def stiff_msg_kernel(g_ref, xm_w, xm_k, k_y, w_y, *refs):
    r_ref, l_ref = refs[-2:]
    g = g_ref[...]
    q = lmul(xm_k[...], g) * w_y[...] + rmul_halves(lmul(xm_w[...], g), k_y[...])
    r_ref[:16] = q[:16]
    l_ref[:16] = q[16:]
    r_ref[16:24] = edge(g_ref, 0, 15)
    l_ref[16:24] = edge(g_ref, 0, 0)
    r_ref[24:] = edge(g_ref, 0, 14)
    l_ref[24:] = edge(g_ref, 0, 1)
    to_pairs(r_ref, l_ref)


def stiff_kernel(ends, g_ref, ml_ref, mr_ref, xe_w, xe_k, z_st, k_y, w_y, *refs):
    gx_ref, u_ref, *faces = refs[:7]
    p_ref, q_ref = refs[7:]
    _, _, has_l, has_r = flags()
    ml, mr = from_pairs(ml_ref, mr_ref)
    ml, mr = ml * has_l, mr * has_r
    gx_ref[...] = g_ref[...]
    add_edge(gx_ref, 0, 0, ml[16:24])
    add_edge(gx_ref, 0, 15, mr[16:24])
    full = with_edges(gx_ref[...], g_ref, 0, has_l, has_r)
    from_l = scaled_edges(ml[24:], ml[16:24], w_y, ends)
    from_r = scaled_edges(mr[24:], mr[16:24], w_y, ends)
    plain = lmul(xe_w[...], full)
    extend(plain * w_y[...], from_l, from_r, p_ref)
    q = lmul(xe_k[...], full) * w_y[...] + rmul_halves(plain, k_y[...])
    extend(q, ml[:16], mr[:16], q_ref)
    u = lmul(z_st[...], jnp.concatenate([p_ref[...], q_ref[...]], axis=0))
    u_ref[...] = u
    send_faces(ends[1], u, p_ref, q_ref, *faces)


def second_kernel(t_ref, *refs):
    join_refs, box_refs, (g_ref, r_ref, l_ref) = refs[:7], refs[7:11], refs[11:]
    g_ref[...] = box(t_ref[...] - join(*join_refs), *box_refs)
    r_ref[...] = edge(g_ref, 0, 15)
    l_ref[...] = edge(g_ref, 0, 0)
    to_pairs(r_ref, l_ref)


def last_x_kernel(g_ref, gx_ref, ml_ref, mr_ref, f_up, f_down, out_ref, in_msg_ref, out_msg_ref):
    _, _, has_l, has_r = flags()
    out_ref[...] = g_ref[...] + gx_ref[...]
    ml, mr = from_pairs(ml_ref, mr_ref)
    add_edge(out_ref, 0, 0, ml * has_l)
    add_edge(out_ref, 0, 15, mr * has_r)
    odd = is_odd()
    up, down = out_ref[112:], out_ref[:16]
    out_msg_ref[...] = jnp.where(odd, up, down)
    in_msg_ref[:16] = jnp.where(odd, down, up)
    in_msg_ref[16:] = jnp.where(odd, f_down[...], f_up[...])


def last_z_kernel(
    out_msg_ref, in_ref, f_out_ref, g_ref, f_up, f_down, _, out_ref, force_ref, face_ref, p_ref, sem
):
    has_b, has_a, _, _ = flags()
    odd = is_odd()
    inner, flag = in_ref[...], jnp.where(odd, has_a, has_b)
    outer = jnp.concatenate([out_msg_ref[...], f_out_ref[...]], axis=0) * flag
    below, above = jnp.where(odd, inner, outer), jnp.where(odd, outer, inner)
    p_ref[...] = g_ref[...]
    p_ref[:16] += below[:16]
    p_ref[112:] += above[:16]
    face_ref[:48] = f_down[...] + below[16:]
    face_ref[48:] = f_up[...] + above[16:]
    copies = [pltpu.make_async_copy(p_ref, out_ref, sem.at[6])]
    for c in range(3):
        for k, row in enumerate((128 * c, 128 * c + 112)):
            src = face_ref.at[pl.ds(48 * k + 16 * c, 16)]
            dst = force_ref.at[pl.ds(row, 16)]
            copies.append(pltpu.make_async_copy(src, dst, sem.at[2 * c + k]))
    for copy in copies:
        copy.start()
    for copy in copies:
        copy.wait()


def call(kernel, name, outs, *args, scratch=(), sems=0, vmem=16, hbm_in=(), hbm_out=(), alias=None):
    shape = lambda rows: jax.ShapeDtypeStruct((rows, 512), F32)
    spec = lambda k, far: pl.BlockSpec(memory_space=pltpu.HBM if k in far else pltpu.VMEM)
    scratch = [pltpu.VMEM((k, 512), F32) if isinstance(k, int) else k for k in scratch]
    return pl.pallas_call(
        kernel,
        out_shape=[shape(o) for o in outs],
        in_specs=[spec(k, hbm_in) for k in range(len(args))],
        out_specs=[spec(k, hbm_out) for k in range(len(outs))],
        scratch_shapes=scratch + ([pltpu.SemaphoreType.DMA((sems,))] if sems else []),
        input_output_aliases=alias or {},
        compiler_params=pltpu.CompilerParams(vmem_limit_bytes=vmem * MIB),
        name=name,
    )(*args)


def exchange_x(far, near):
    nz, nx = lax.axis_size("wide"), lax.axis_size("narrow")
    pairs = []
    for z in range(nz):
        for k in range(nx):
            to = k - 1 + 2 * (k % 2)
            other = (z, to) if 0 <= to < nx else (z + 1 - 2 * (z % 2), k)
            pairs.append((z * nx + k, other[0] * nx + other[1]))
    far = lax.ppermute(far, ("wide", "narrow"), pairs)
    return far, lax.ppermute(near, "narrow", [(k, k + 1 - 2 * (k % 2)) for k in range(nx)])


def other_core(x):
    n = lax.axis_size("wide")
    return lax.ppermute(x, "wide", [(i, i + 1 - 2 * (i % 2)) for i in range(n)])


def next_chip(x):
    nz, nx = lax.axis_size("wide"), lax.axis_size("narrow")
    pairs = []
    for z in range(nz):
        to = z - 1 + 2 * (z % 2)
        for k in range(nx):
            other = (to, k) if 0 <= to < nz else (z, k + 1 - 2 * (k % 2))
            pairs.append((z * nx + k, other[0] * nx + other[1]))
    return lax.ppermute(x, ("wide", "narrow"), pairs)


def meet(up, down, inner_msg, coefs, name, force_faces=()):
    inner = other_core(inner_msg)
    coefs = [[float(t) for t in row] for row in coefs]
    kernel, outs = (outer_force_kernel, (56, 48)) if force_faces else (outer_kernel, (56,))
    msgs = call(functools.partial(kernel, coefs), name, outs, *force_faces, up, down, inner)
    outer = next_chip(msgs[0])
    (far,) = call(far_kernel, name + "_far", (24,), outer)
    return inner, outer, other_core(far), *map(next_chip, msgs[1:])


def shards(velocity, bfield):
    tables = constants()
    picks = tables.pop("pick_div"), tables.pop("pick_st")
    c = {name: jnp.asarray(value) for name, value in tables.items()}
    consts = lambda *names: [c[name] for name in names]
    weights = tables_1d()[4]
    ends = float(weights[1]), float(weights[0])
    force_args = (
        velocity,
        bfield,
        *consts("y_in", "zx_in", "zx_out", "y_out", "xm_w", "xm_wd", "wd_y", "w_y"),
    )
    force_args = [pltpu.with_memory_space_constraint(x, pltpu.HBM) for x in force_args]
    f, right, left = call(
        force_kernel,
        "force",
        (384, 48, 48),
        *force_args,
        scratch=[pltpu.VMEM(a.shape, a.dtype) for a in force_args],
        sems=10,
        vmem=32,
        hbm_in=range(10),
    )
    from_l, from_r = exchange_x(right, left)
    force, f_up, f_down, u, up, down, up_face, down_face, inner = call(
        functools.partial(div_kernel, ends),
        "div",
        (384, 48, 48, 144, 56, 56, 40, 40, 56),
        f,
        from_l,
        from_r,
        *consts("xe_w", "xe_wd", "z_div", "wd_y", "w_y"),
        scratch=(144, 144, 384),
        sems=1,
        hbm_out=(0,),
    )
    inner, outer, far, f_out = meet(up, down, inner, picks[0], "div_out", (f_up, f_down))
    box_consts = consts("ybox_in", "inv", "box_out", "ybox_out")
    spectral, g = call(
        first_kernel,
        "first_pass",
        (208, 128),
        u,
        up_face,
        down_face,
        inner,
        outer,
        far,
        c["box_div"],
        *box_consts,
    )
    msg_consts = consts("xm_w", "xm_k", "k_y", "w_y")
    right, left = call(stiff_msg_kernel, "stiff_msg", (32, 32), g, *msg_consts, f_out)
    from_l, from_r = exchange_x(right, left)
    gx, u, up, down, up_face, down_face, inner = call(
        functools.partial(stiff_kernel, ends),
        "stiff",
        (128, 144, 56, 56, 40, 40, 56),
        g,
        from_l,
        from_r,
        *consts("xe_w", "xe_k", "z_st", "k_y", "w_y"),
        scratch=(144, 144),
    )
    inner, outer, far = meet(up, down, inner, picks[1], "stiff_out")
    g, right, left = call(
        second_kernel,
        "second_pass",
        (128, 8, 8),
        spectral,
        u,
        up_face,
        down_face,
        inner,
        outer,
        far,
        c["box_st"],
        *box_consts,
    )
    from_l, from_r = exchange_x(right, left)
    total, inner, outer = call(
        last_x_kernel, "last_x", (128, 64, 16), g, gx, from_l, from_r, f_up, f_down
    )
    outer, inner = next_chip(outer), other_core(inner)
    pressure, force = call(
        last_z_kernel,
        "last_z",
        (128, 384),
        outer,
        inner,
        f_out,
        total,
        f_up,
        f_down,
        force,
        scratch=(96, 128),
        sems=7,
        hbm_in=(6,),
        hbm_out=(0, 1),
        alias={6: 1},
    )
    return force.reshape(3, 8, 16, 512), pressure.reshape(8, 16, 512)


def solution(mesh):
    placed = (P(None, "wide", "narrow", None), P("wide", "narrow", None))
    return jax.shard_map(
        shards, mesh=mesh, in_specs=placed, out_specs=placed, check_vma=False
    )
```

```python
import functools

import jax
import jax.numpy as jnp
import ml_dtypes
import numpy as np
from jax import lax
from jax.experimental import pallas as pl
from jax.experimental.pallas import tpu as pltpu
from jax.sharding import PartitionSpec as P

F32 = jnp.float32
BF16 = jnp.bfloat16
MIB = 2**20


def legendre_pair(degree, points):
    below, current = np.ones(points.shape), points * 1.0
    for step in range(2, degree + 1):
        below, current = current, ((2 * step - 1) * points * current - (step - 1) * below) / step
    return current, below


def tables_1d():
    points = np.cos(np.pi * np.arange(8) / 7)
    for _ in range(60):
        top, below = legendre_pair(7, points)
        points = points - (points * top - below) / (8 * top)
    points = np.sort(points)
    top, below = legendre_pair(7, points)
    w = 2.0 / (56 * top**2)
    spacing = points[:, None] - points[None, :] + np.eye(8)
    deriv = top[:, None] / (top[None, :] * spacing) * (1.0 - np.eye(8))
    deriv[0, 0], deriv[-1, -1] = -14.0, 14.0
    gauss = np.cos(np.pi * (np.arange(12) + 0.75) / 12.5)
    for _ in range(60):
        top, below = legendre_pair(12, gauss)
        gauss = gauss - top / (12 * (gauss * top - below) / (gauss**2 - 1.0))
    top, below = legendre_pair(12, gauss)
    slope = 12 * (gauss * top - below) / (gauss**2 - 1.0)
    v = 2.0 / ((1.0 - gauss**2) * slope**2)
    interp = np.ones((12, 8))
    for col in range(8):
        for other in range(8):
            if other != col:
                interp[:, col] *= (gauss - points[other]) / (points[col] - points[other])
    stiff = deriv.T @ (w[:, None] * deriv)
    wide_stiff, wide_mass = np.zeros((22, 22)), np.zeros(22)
    for el in range(3):
        r = 7 * el
        wide_stiff[r : r + 8, r : r + 8] += stiff
        wide_mass[r : r + 8] += w
    scale = 1.0 / np.sqrt(wide_mass[6:16])
    lam, vec = np.linalg.eigh(scale[:, None] * wide_stiff[6:16, 6:16] * scale[None, :])
    return interp, interp @ deriv, deriv, stiff, w, scale[:, None] * vec, lam, v


def hi_lo(m):
    hi = m.astype(ml_dtypes.bfloat16)
    return hi, (m - hi.astype(np.float64)).astype(ml_dtypes.bfloat16)


def left_const(m):
    hi, lo = hi_lo(m)
    return np.concatenate([hi, hi, lo], axis=1)


def right_const(m):
    return np.concatenate(hi_lo(m), axis=0)


def block_diag(m, count):
    return np.kron(np.eye(count), m)


def own(z, x):
    return 16 * z + x


def local_rows(terms, xs):
    out = np.zeros((8 * len(xs), 128))
    for k, x in enumerate(xs):
        el, j = divmod(x, 8)
        for z in range(8):
            for zm, xm in terms:
                for z2 in range(8):
                    for j2 in range(8):
                        out[8 * k + z, own(z2, 8 * el + j2)] += zm[z, z2] * xm[j, j2]
    return out


def extended_rows(terms):
    local = local_rows(terms, range(16)).reshape(16, 8, 128)
    out = np.zeros((144, 144))
    for x in range(16):
        for z in range(8):
            out[own(z, x), :128] = local[x, z]
            if x in (7, 8):
                out[own(z, x), :128] += local[15 - x, z]
    for z in range(8):
        for zm, xm in terms:
            for z2 in range(8):
                out[own(z, 0), 128 + z2] += zm[z, z2] * xm[7, 7]
                out[128 + z, 128 + z2] += zm[z, z2] * xm[6, 7]
                out[own(z, 15), 136 + z2] += zm[z, z2] * xm[0, 0]
                out[136 + z, 136 + z2] += zm[z, z2] * xm[1, 0]
    return out


def z_rows(mats):
    blocks = [np.zeros((144, 144)) for _ in mats]
    for out, m in zip(blocks, mats):
        out[:128, :128] = np.kron(m, np.eye(16))
        out[128:136, 128:136] = m
        out[136:, 136:] = m
    return np.concatenate(blocks, axis=1)


def join_rows(zm, w):
    out = np.zeros((192, 384))
    below, above, down, up, far_b, far_a = 144, 200, 256, 296, 336, 360
    for t in range(18):
        side = t - 16
        own_row = lambda z: own(z, t) if t < 16 else 128 + 8 * side + z
        layer = lambda base, k: base + 16 * k + t if t < 16 else base + 48 + 2 * side + k
        msg_face = lambda base: base + 32 + t if t < 16 else base + 52 + side
        face = lambda base, k: base + 16 * k + t if t < 16 else base + 36 + 2 * k + side
        far = lambda base: base + t if t < 16 else base + 20 + side
        b7, b6, a0, a1 = np.zeros((4, 384))
        b7[layer(below, 1)] = b6[layer(below, 0)] = 1.0
        b7[face(down, 0)], b7[face(down, 1)], b7[far(far_b)] = zm[7, 7], w[7], zm[7, 0]
        b6[face(down, 0)], b6[far(far_b)] = zm[6, 7], zm[6, 0]
        a0[layer(above, 0)] = a1[layer(above, 1)] = 1.0
        a0[face(up, 0)], a0[face(up, 1)], a0[far(far_a)] = zm[0, 0], w[0], zm[0, 7]
        a1[face(up, 0)], a1[far(far_a)] = zm[1, 0], zm[1, 7]
        for z in range(8):
            row = out[own_row(z)]
            row[own_row(z)] += 1.0
            row[msg_face(below)] += zm[z, 0]
            row[msg_face(above)] += zm[z, 7]
        out[own_row(0)] += b7
        out[own_row(7)] += a0
        out[144 + t], out[168 + t] = b6, a1
    return out


def box_rows(vec):
    nodes = np.zeros((10, 2, 10, 192))
    for zk in range(10):
        for el in range(2):
            for xk in range(10):
                x = 8 * el + (-2 if xk == 0 else 9 if xk == 9 else xk - 1)
                side = -1 if x < 0 else 1 if x > 15 else 0
                if 0 < zk < 9:
                    row = {0: own(zk - 1, x), -1: 128 + zk - 1, 1: 136 + zk - 1}[side]
                else:
                    row = (144 if zk == 0 else 168) + {0: x, -1: 16, 1: 17}[side]
                nodes[zk, el, xk, row] = 1.0
    into = np.einsum("zi,xj,zexr->iejr", vec, vec, nodes).reshape(200, 192)
    back = np.zeros((8, 16, 10, 2, 10))
    inner = vec[1:9]
    for z in range(8):
        for x in range(16):
            el, j = divmod(x, 8)
            block = inner[z][:, None] * inner[j][None, :]
            if x in (7, 8):
                back[z, x, :, el] += 0.5 * block
                back[z, x, :, 1 - el] += 0.5 * inner[z][:, None] * inner[7 - j][None, :]
            else:
                back[z, x, :, el] += block
    back = back.reshape(128, 200)
    return np.pad(into, ((0, 8), (0, 0))), np.pad(back, ((0, 0), (0, 8)))


def box_lanes(vec, count):
    into = np.zeros((8 * count, 10 * count))
    back = np.zeros((10 * count, 8 * count))
    for e in range(count):
        spots = [8 * e - 2] + list(range(8 * e, 8 * e + 8)) + [8 * e + 9]
        for k, y in enumerate(spots):
            if 0 <= y < 8 * count:
                into[y, 10 * e : 10 * e + 10] += vec[k]
        for j in range(8):
            col = vec[j + 1]
            y = 8 * e + j
            if j == 0 and e > 0:
                back[10 * e : 10 * e + 10, [y - 1, y]] += 0.5 * col[:, None]
            elif j == 7 and e < count - 1:
                back[10 * e : 10 * e + 10, [y, y + 1]] += 0.5 * col[:, None]
            else:
                back[10 * e : 10 * e + 10, y] += col
    return into, back


def face_coefs(zm):
    return np.array([[zm[0, 7], zm[1, 7]], [zm[6, 0], zm[7, 0]]])


def constants():
    interp, slopes, deriv, stiff, w, vec, lam, v = tables_1d()
    c = {}
    c["y_in"] = right_const(
        np.concatenate([block_diag(interp.T, 32), block_diag(slopes.T, 32)], axis=1)
    )
    c["zx_in"] = left_const(
        np.concatenate(
            [np.kron(interp, interp), np.kron(slopes, interp), np.kron(interp, slopes)], axis=0
        )
    )
    test = v[:, None] * interp
    c["zx_out"] = left_const(np.kron(test.T, test.T))
    c["y_out"] = right_const(block_diag(test, 32))
    one, wm, wd = np.eye(8), np.diag(w), w[:, None] * deriv
    sides = (14, 15, 1, 0)
    for name, xm in (("w", wm), ("wd", wd), ("k", stiff)):
        c["xm_" + name] = left_const(local_rows([(one, xm)], sides))
        c["xe_" + name] = left_const(extended_rows([(one, xm)]))
    c["z_div"], c["z_st"] = left_const(z_rows((wd, wm))), left_const(z_rows((stiff, wm)))
    c["pick_div"], c["pick_st"] = face_coefs(wd), face_coefs(stiff)
    c["wd_y"] = right_const(block_diag(wd.T, 32))
    c["k_y"] = right_const(block_diag(stiff.T, 32))
    c["w_y"] = np.tile(w, 64)[None].astype(np.float32)
    into, back = box_rows(vec)
    c["box_div"] = left_const(into @ join_rows(wd, w))
    c["box_st"] = left_const(into @ join_rows(stiff, w))
    c["box_out"] = left_const(back)
    into, back = box_lanes(vec, 64)
    c["ybox_in"], c["ybox_out"] = right_const(into), right_const(back)
    inv = 1.0 / (lam[:, None, None, None] + lam[None, None, :, None] + lam)
    inv = np.broadcast_to(inv[:, :, :, None, :], (10, 1, 10, 64, 10))
    inv = np.broadcast_to(inv, (10, 2, 10, 64, 10)).reshape(200, 640)
    c["inv"] = np.pad(inv, ((0, 8), (0, 0))).astype(np.float32)
    return c


def split(x):
    hi = x.astype(BF16)
    return hi, (x - hi.astype(F32)).astype(BF16)


def rmul(x, const):
    hi, lo = split(x)
    depth = const.shape[0] // 2
    const = jnp.concatenate([const[:depth], const], axis=0)
    return jnp.dot(jnp.concatenate([hi, lo, hi], axis=1), const, preferred_element_type=F32)


def lmul(const, x):
    hi, lo = split(x)
    return jnp.dot(const, jnp.concatenate([hi, lo, hi], axis=0), preferred_element_type=F32)


def rmul_halves(x, const):
    return jnp.concatenate([rmul(x[:, :256], const), rmul(x[:, 256:], const)], axis=1)


def dss_lanes(x):
    lane = lax.broadcasted_iota(jnp.int32, x.shape, 1)
    n = x.shape[1]
    up = jnp.where((lane % 8 == 7) & (lane < n - 1), pltpu.roll(x, n - 1, 1), 0.0)
    down = jnp.where((lane % 8 == 0) & (lane > 0), pltpu.roll(x, 1, 1), 0.0)
    return x + up + down


def flags():
    z, x = lax.axis_index("wide"), lax.axis_index("narrow")
    nz, nx = lax.axis_size("wide"), lax.axis_size("narrow")
    as_flag = lambda t: t.astype(F32)
    return as_flag(z > 0), as_flag(z < nz - 1), as_flag(x > 0), as_flag(x < nx - 1)


def force_kernel(*refs):
    sources, (f_ref, r_ref, l_ref), held, sem = refs[:10], refs[10:13], refs[13:23], refs[23]
    v_ref, b_ref, y_in, zx_in, zx_out, y_out, xm_w, xm_wd, wd_y, w_y = held
    copies = [pltpu.make_async_copy(a, b, sem.at[k]) for k, (a, b) in enumerate(zip(sources, held))]
    for k in (2, 0, 1, 3, 4, 5, 6, 7, 8, 9):
        copies[k].start()
    copies[2].wait()
    copies[0].wait()
    v = jnp.concatenate([v_ref[:, :, k : k + 8].reshape(192, 512) for k in (0, 8)], axis=0)
    parts = [rmul(v[:, cut], y_in[...]) for cut in (slice(0, 256), slice(256, 512))]
    value = jnp.concatenate([p[:, :384] for p in parts], axis=1)
    slope = jnp.concatenate([p[:, 384:] for p in parts], axis=1)
    for copy in (copies[1], *copies[3:]):
        copy.wait()
    b = jnp.concatenate([b_ref[:, k : k + 8].reshape(64, 512) for k in (0, 8)], axis=0)
    parts = [rmul(b[:, cut], y_in[:, :384]) for cut in (slice(0, 256), slice(256, 512))]
    field = jnp.concatenate(parts, axis=1)
    back = []
    for el in range(2):
        u, gz, gx, gy = [], [], [], []
        for c in range(3):
            rows = slice(192 * el + 64 * c, 192 * el + 64 * c + 64)
            most = lmul(zx_in[...], value[rows])
            u.append(most[:144])
            gz.append(most[144:288])
            gx.append(most[288:])
            gy.append(lmul(zx_in[:144], slope[rows]))
        bq = lmul(zx_in[:144], field[64 * el : 64 * el + 64])
        b2 = bq * bq
        for c in range(3):
            conv = u[0] * gz[c] + u[1] * gx[c] + u[2] * gy[c]
            if c != 1:
                conv = conv + b2 * u[c]
            back.append(lmul(zx_out[...], -conv))
    back = jnp.concatenate(back, axis=0)
    halves = [rmul(back[:, cut], y_out[...]) for cut in (slice(0, 384), slice(384, 768))]
    f = dss_lanes(jnp.concatenate(halves, axis=1))
    first, second = f[:192], f[192:]
    node = lax.broadcasted_iota(jnp.int32, (192, 512), 0) % 8
    both = (
        first + jnp.where(node == 7, pltpu.roll(second, 7, 0), 0.0),
        second + jnp.where(node == 0, pltpu.roll(first, 185, 0), 0.0),
    )
    for k in range(24):
        for el in range(2):
            f_ref[16 * k + 8 * el : 16 * k + 8 * el + 8] = both[el][8 * k : 8 * k + 8]
    f = f_ref[...]
    s = lmul(xm_wd[...], f[128:256]) * w_y[...]
    s = s + rmul_halves(lmul(xm_w[...], f[256:]), wd_y[...])
    r_ref[:16] = s[:16]
    l_ref[:16] = s[16:]
    for k, (c, step) in enumerate(((0, 0), (1, 0), (2, 0), (0, 1))):
        r_ref[16 + 8 * k : 24 + 8 * k] = edge(f_ref, 128 * c, 15 - step)
        l_ref[16 + 8 * k : 24 + 8 * k] = edge(f_ref, 128 * c, step)
    to_pairs(r_ref, l_ref)


def to_pairs(r_ref, l_ref):
    right, left = r_ref[...], l_ref[...]
    odd = lax.axis_index("narrow") % 2 == 1
    r_ref[...] = jnp.where(odd, right, left)
    l_ref[...] = jnp.where(odd, left, right)


def from_pairs(far_ref, near_ref):
    far, near = far_ref[...], near_ref[...]
    odd = lax.axis_index("narrow") % 2 == 1
    return jnp.where(odd, near, far), jnp.where(odd, far, near)


def edge(ref, base, x):
    return jnp.concatenate([ref[base + x + 16 * z : base + x + 16 * z + 1] for z in range(8)], axis=0)


def add_edge(ref, base, x, rows):
    for z in range(8):
        ref[base + x + 16 * z : base + x + 16 * z + 1] += rows[z : z + 1]


def extend(s, from_l, from_r, acc_ref):
    acc_ref[...] = s
    add_edge(acc_ref, 0, 0, from_l[8:16])
    add_edge(acc_ref, 0, 15, from_r[8:16])
    acc_ref[128:136] += from_l[:8]
    acc_ref[136:144] += from_r[:8]
    acc_ref[...] = dss_lanes(acc_ref[...])


def with_edges(full, raw_ref, base, has_l, has_r):
    edges = [edge(raw_ref, base, 0) * has_l, edge(raw_ref, base, 15) * has_r]
    return jnp.concatenate([full, *edges], axis=0)


def scaled_edges(ghost, last, w_y, ends):
    return jnp.concatenate([ghost * ends[0], last * ends[1]], axis=0) * w_y[...]


def send_faces(w_end, u, h0_ref, h12_ref, up_ref, down_ref, up_face_ref, down_face_ref, in_ref):
    for ref, own_ref, a, b, z in (
        (up_ref, up_face_ref, 6, 7, 7),
        (down_ref, down_face_ref, 0, 1, 0),
    ):
        ref[:16] = u[16 * a : 16 * a + 16]
        ref[16:32] = u[16 * b : 16 * b + 16]
        ref[32:48] = own_ref[:16] = h0_ref[16 * z : 16 * z + 16]
        own_ref[16:32] = h12_ref[16 * z : 16 * z + 16]
        half = 16 if z == 7 else 0
        ref[half : half + 16] += w_end * own_ref[16:32]
        h12 = [w_end * h12_ref[128 + 8 * s + z : 129 + 8 * s + z] for s in (0, 1)]
        rows = [u[128 + 8 * s + k : 129 + 8 * s + k] for s in (0, 1) for k in (a, b)]
        rows[z // 7] = rows[z // 7] + h12[0]
        rows[2 + z // 7] = rows[2 + z // 7] + h12[1]
        faces = [h[128 + 8 * s + z : 129 + 8 * s + z] for h in (h0_ref, h12_ref) for s in (0, 1)]
        ref[48:56] = jnp.concatenate(rows + faces, axis=0)
        own_ref[32:] = ref[48:56]
    in_ref[...] = jnp.where(is_odd(), down_ref[...], up_ref[...])


def is_odd():
    return lax.axis_index("wide") % 2 == 1


def div_kernel(ends, f_ref, ml_ref, mr_ref, xe_w, xe_wd, z_div, wd_y, w_y, *refs):
    force_ref, f_up_ref, f_down_ref, u_ref, *faces = refs[:9]
    h0_ref, h12_ref, fx_ref, sem = refs[9:]
    _, _, has_l, has_r = flags()
    ml, mr = from_pairs(ml_ref, mr_ref)
    ml, mr = ml * has_l, mr * has_r
    fx_ref[...] = f_ref[...]
    full = []
    for c in range(3):
        base, piece = 128 * c, slice(16 + 8 * c, 24 + 8 * c)
        add_edge(fx_ref, base, 0, ml[piece])
        add_edge(fx_ref, base, 15, mr[piece])
        full.append(with_edges(fx_ref[base : base + 128], f_ref, base, has_l, has_r))
        f_up_ref[16 * c : 16 * c + 16] = fx_ref[base + 112 : base + 128]
        f_down_ref[16 * c : 16 * c + 16] = fx_ref[base : base + 16]
    copy = pltpu.make_async_copy(fx_ref, force_ref, sem.at[0])
    copy.start()
    from_l = scaled_edges(ml[40:48], ml[16:24], w_y, ends)
    from_r = scaled_edges(mr[40:48], mr[16:24], w_y, ends)
    extend(lmul(xe_w[...], full[0]) * w_y[...], from_l, from_r, h0_ref)
    h = lmul(xe_wd[...], full[1]) * w_y[...] + rmul_halves(lmul(xe_w[...], full[2]), wd_y[...])
    extend(h, ml[:16], mr[:16], h12_ref)
    u = lmul(z_div[...], jnp.concatenate([h0_ref[...], h12_ref[...]], axis=0))
    u_ref[...] = u
    send_faces(ends[1], u, h0_ref, h12_ref, *faces)
    copy.wait()


def outer_kernel(coefs, up_ref, down_ref, in_ref, out_ref):
    odd = is_odd()
    ca = jnp.where(odd, coefs[1][0], coefs[0][0])
    cb = jnp.where(odd, coefs[1][1], coefs[0][1])
    out_ref[...] = jnp.where(odd, up_ref[...], down_ref[...])
    face, far_l, far_r = in_ref[32:48], in_ref[52:53], in_ref[53:54]
    out_ref[:16] += ca * face
    out_ref[16:32] += cb * face
    out_ref[48:52] += jnp.concatenate([ca * far_l, cb * far_l, ca * far_r, cb * far_r], axis=0)


def outer_force_kernel(coefs, f_up, f_down, up_ref, down_ref, in_ref, out_ref, f_out_ref, f_in_ref):
    outer_kernel(coefs, up_ref, down_ref, in_ref, out_ref)
    f_out_ref[...] = jnp.where(is_odd(), f_up[...], f_down[...])
    f_in_ref[...] = jnp.where(is_odd(), f_down[...], f_up[...])


def far_kernel(out_msg_ref, far_ref):
    has_b, has_a, _, _ = flags()
    flag = jnp.where(is_odd(), has_a, has_b)
    far_ref[:16] = out_msg_ref[32:48] * flag
    far_ref[16:] = out_msg_ref[48:56] * flag


def join(u_ref, up_ref, down_ref, in_ref, out_ref, far_ref, const):
    has_b, has_a, _, _ = flags()
    odd = is_odd()
    inner = in_ref[...]
    outer = out_ref[...] * jnp.where(odd, has_a, has_b)
    far = far_ref[...]
    rows = [
        u_ref[...],
        jnp.where(odd, inner, outer),
        jnp.where(odd, outer, inner),
        down_ref[...] * has_b,
        up_ref[...] * has_a,
        jnp.where(odd, far, 0.0),
        jnp.where(odd, 0.0, far),
    ]
    return lmul(const[...], jnp.concatenate(rows, axis=0))


def box(t, ybox_in, inv, box_out, ybox_out):
    has_b, has_a, has_l, has_r = flags()
    t = rmul(t, ybox_in[...]) * inv[...]
    g = rmul(lmul(box_out[...], t), ybox_out[...])
    row = lax.broadcasted_iota(jnp.int32, (128, 1), 0)
    z, x = row // 16, row % 16
    weight = 1.0 - 0.5 * jnp.where(z == 0, has_b, jnp.where(z == 7, has_a, 0.0))
    weight = weight * (1.0 - 0.5 * jnp.where(x == 0, has_l, jnp.where(x == 15, has_r, 0.0)))
    return g * weight


def first_kernel(*refs):
    t_ref, g_ref = refs[11:]
    t = join(*refs[:7])
    t_ref[...] = t
    g_ref[...] = box(t, *refs[7:11])


def stiff_msg_kernel(g_ref, xm_w, xm_k, k_y, w_y, *refs):
    r_ref, l_ref = refs[-2:]
    g = g_ref[...]
    q = lmul(xm_k[...], g) * w_y[...] + rmul_halves(lmul(xm_w[...], g), k_y[...])
    r_ref[:16] = q[:16]
    l_ref[:16] = q[16:]
    r_ref[16:24] = edge(g_ref, 0, 15)
    l_ref[16:24] = edge(g_ref, 0, 0)
    r_ref[24:] = edge(g_ref, 0, 14)
    l_ref[24:] = edge(g_ref, 0, 1)
    to_pairs(r_ref, l_ref)


def stiff_kernel(ends, g_ref, ml_ref, mr_ref, xe_w, xe_k, z_st, k_y, w_y, *refs):
    gx_ref, u_ref, *faces = refs[:7]
    p_ref, q_ref = refs[7:]
    _, _, has_l, has_r = flags()
    ml, mr = from_pairs(ml_ref, mr_ref)
    ml, mr = ml * has_l, mr * has_r
    gx_ref[...] = g_ref[...]
    add_edge(gx_ref, 0, 0, ml[16:24])
    add_edge(gx_ref, 0, 15, mr[16:24])
    full = with_edges(gx_ref[...], g_ref, 0, has_l, has_r)
    from_l = scaled_edges(ml[24:], ml[16:24], w_y, ends)
    from_r = scaled_edges(mr[24:], mr[16:24], w_y, ends)
    plain = lmul(xe_w[...], full)
    extend(plain * w_y[...], from_l, from_r, p_ref)
    q = lmul(xe_k[...], full) * w_y[...] + rmul_halves(plain, k_y[...])
    extend(q, ml[:16], mr[:16], q_ref)
    u = lmul(z_st[...], jnp.concatenate([p_ref[...], q_ref[...]], axis=0))
    u_ref[...] = u
    send_faces(ends[1], u, p_ref, q_ref, *faces)


def second_kernel(t_ref, *refs):
    join_refs, box_refs, (g_ref, r_ref, l_ref) = refs[:7], refs[7:11], refs[11:]
    g_ref[...] = box(t_ref[...] - join(*join_refs), *box_refs)
    r_ref[...] = edge(g_ref, 0, 15)
    l_ref[...] = edge(g_ref, 0, 0)
    to_pairs(r_ref, l_ref)


def last_x_kernel(g_ref, gx_ref, ml_ref, mr_ref, out_ref, out_msg_ref, in_msg_ref):
    _, _, has_l, has_r = flags()
    out_ref[...] = g_ref[...] + gx_ref[...]
    ml, mr = from_pairs(ml_ref, mr_ref)
    add_edge(out_ref, 0, 0, ml * has_l)
    add_edge(out_ref, 0, 15, mr * has_r)
    odd = is_odd()
    up, down = out_ref[112:], out_ref[:16]
    out_msg_ref[...] = jnp.where(odd, up, down)
    in_msg_ref[...] = jnp.where(odd, down, up)


def last_z_kernel(
    out_msg_ref, in_ref, f_out_ref, f_in_ref, g_ref, f_up, f_down, _, out_ref, force_ref, face_ref, p_ref, sem
):
    has_b, has_a, _, _ = flags()
    odd = is_odd()
    flag = jnp.where(odd, has_a, has_b)
    inner = jnp.concatenate([in_ref[...], f_in_ref[...]], axis=0)
    outer = jnp.concatenate([out_msg_ref[...], f_out_ref[...]], axis=0) * flag
    below, above = jnp.where(odd, inner, outer), jnp.where(odd, outer, inner)
    p_ref[...] = g_ref[...]
    p_ref[:16] += below[:16]
    p_ref[112:] += above[:16]
    face_ref[:48] = f_down[...] + below[16:]
    face_ref[48:] = f_up[...] + above[16:]
    copies = [pltpu.make_async_copy(p_ref, out_ref, sem.at[6])]
    for c in range(3):
        for k, row in enumerate((128 * c, 128 * c + 112)):
            src = face_ref.at[pl.ds(48 * k + 16 * c, 16)]
            dst = force_ref.at[pl.ds(row, 16)]
            copies.append(pltpu.make_async_copy(src, dst, sem.at[2 * c + k]))
    for copy in copies:
        copy.start()
    for copy in copies:
        copy.wait()


def call(kernel, name, outs, *args, scratch=(), sems=0, vmem=16, hbm_in=(), hbm_out=(), alias=None):
    shape = lambda rows: jax.ShapeDtypeStruct((rows, 512), F32)
    spec = lambda k, far: pl.BlockSpec(memory_space=pltpu.HBM if k in far else pltpu.VMEM)
    scratch = [pltpu.VMEM((k, 512), F32) if isinstance(k, int) else k for k in scratch]
    return pl.pallas_call(
        kernel,
        out_shape=[shape(o) for o in outs],
        in_specs=[spec(k, hbm_in) for k in range(len(args))],
        out_specs=[spec(k, hbm_out) for k in range(len(outs))],
        scratch_shapes=scratch + ([pltpu.SemaphoreType.DMA((sems,))] if sems else []),
        input_output_aliases=alias or {},
        compiler_params=pltpu.CompilerParams(vmem_limit_bytes=vmem * MIB),
        name=name,
    )(*args)


def exchange_x(far, near):
    nz, nx = lax.axis_size("wide"), lax.axis_size("narrow")
    pairs = []
    for z in range(nz):
        for k in range(nx):
            to = k - 1 + 2 * (k % 2)
            other = (z, to) if 0 <= to < nx else (z + 1 - 2 * (z % 2), k)
            pairs.append((z * nx + k, other[0] * nx + other[1]))
    far = lax.ppermute(far, ("wide", "narrow"), pairs)
    return far, lax.ppermute(near, "narrow", [(k, k + 1 - 2 * (k % 2)) for k in range(nx)])


def other_core(x):
    n = lax.axis_size("wide")
    return lax.ppermute(x, "wide", [(i, i + 1 - 2 * (i % 2)) for i in range(n)])


def next_chip(x):
    nz, nx = lax.axis_size("wide"), lax.axis_size("narrow")
    pairs = []
    for z in range(nz):
        to = z - 1 + 2 * (z % 2)
        for k in range(nx):
            other = (to, k) if 0 <= to < nz else (z, k + 1 - 2 * (k % 2))
            pairs.append((z * nx + k, other[0] * nx + other[1]))
    return lax.ppermute(x, ("wide", "narrow"), pairs)


def meet(up, down, inner_msg, coefs, name, force_faces=()):
    inner = other_core(inner_msg)
    coefs = [[float(t) for t in row] for row in coefs]
    kernel, outs = (outer_force_kernel, (56, 48, 48)) if force_faces else (outer_kernel, (56,))
    msgs = call(functools.partial(kernel, coefs), name, outs, *force_faces, up, down, inner)
    outer = next_chip(msgs[0])
    (far,) = call(far_kernel, name + "_far", (24,), outer)
    faces = [next_chip(msgs[1]), other_core(msgs[2])] if force_faces else []
    return inner, outer, other_core(far), *faces


def shards(velocity, bfield):
    tables = constants()
    picks = tables.pop("pick_div"), tables.pop("pick_st")
    c = {name: jnp.asarray(value) for name, value in tables.items()}
    consts = lambda *names: [c[name] for name in names]
    weights = tables_1d()[4]
    ends = float(weights[1]), float(weights[0])
    force_args = (
        velocity,
        bfield,
        *consts("y_in", "zx_in", "zx_out", "y_out", "xm_w", "xm_wd", "wd_y", "w_y"),
    )
    force_args = [pltpu.with_memory_space_constraint(x, pltpu.HBM) for x in force_args]
    f, right, left = call(
        force_kernel,
        "force",
        (384, 48, 48),
        *force_args,
        scratch=[pltpu.VMEM(a.shape, a.dtype) for a in force_args],
        sems=10,
        vmem=32,
        hbm_in=range(10),
    )
    from_l, from_r = exchange_x(right, left)
    force, f_up, f_down, u, up, down, up_face, down_face, inner = call(
        functools.partial(div_kernel, ends),
        "div",
        (384, 48, 48, 144, 56, 56, 40, 40, 56),
        f,
        from_l,
        from_r,
        *consts("xe_w", "xe_wd", "z_div", "wd_y", "w_y"),
        scratch=(144, 144, 384),
        sems=1,
        hbm_out=(0,),
    )
    inner, outer, far, f_out, f_in = meet(up, down, inner, picks[0], "div_out", (f_up, f_down))
    box_consts = consts("ybox_in", "inv", "box_out", "ybox_out")
    spectral, g = call(
        first_kernel,
        "first_pass",
        (208, 128),
        u,
        up_face,
        down_face,
        inner,
        outer,
        far,
        c["box_div"],
        *box_consts,
    )
    msg_consts = consts("xm_w", "xm_k", "k_y", "w_y")
    right, left = call(stiff_msg_kernel, "stiff_msg", (32, 32), g, *msg_consts, f_out, f_in)
    from_l, from_r = exchange_x(right, left)
    gx, u, up, down, up_face, down_face, inner = call(
        functools.partial(stiff_kernel, ends),
        "stiff",
        (128, 144, 56, 56, 40, 40, 56),
        g,
        from_l,
        from_r,
        *consts("xe_w", "xe_k", "z_st", "k_y", "w_y"),
        scratch=(144, 144),
    )
    inner, outer, far = meet(up, down, inner, picks[1], "stiff_out")
    g, right, left = call(
        second_kernel,
        "second_pass",
        (128, 8, 8),
        spectral,
        u,
        up_face,
        down_face,
        inner,
        outer,
        far,
        c["box_st"],
        *box_consts,
    )
    from_l, from_r = exchange_x(right, left)
    total, outer, inner = call(
        last_x_kernel, "last_x", (128, 16, 16), g, gx, from_l, from_r
    )
    outer, inner = next_chip(outer), other_core(inner)
    pressure, force = call(
        last_z_kernel,
        "last_z",
        (128, 384),
        outer,
        inner,
        f_out,
        f_in,
        total,
        f_up,
        f_down,
        force,
        scratch=(96, 128),
        sems=7,
        hbm_in=(7,),
        hbm_out=(0, 1),
        alias={7: 1},
    )
    return force.reshape(3, 8, 16, 512), pressure.reshape(8, 16, 512)


def solution(mesh):
    placed = (P(None, "wide", "narrow", None), P("wide", "narrow", None))
    return jax.shard_map(
        shards, mesh=mesh, in_specs=placed, out_specs=placed, check_vma=False
    )
```
